32 devices in a mesh: dp: 16 (over z, y, core), mp: 2 (over x).
Axes of the slice: x: 2, y: 2, z: 4, core: 2. Of those that a mesh axis runs over, the one named last changes fastest.
Arguments:
- tokens: bfloat16 [20480, 1280], P(('dp', 'mp')), may hold values from -6 to 6
- segment_ids: int32 [128, 160], P('dp'), may hold values from 0 to 3, never falling along the last dimension, each value on 1 to 80 neighbouring positions
- game_ids: int32 [128], P('dp'), may hold values from 0 to 40
- return_bins: int32 [20480], P(('dp', 'mp')), may hold values from 0 to 119
- action_bins: int32 [20480], P(('dp', 'mp')), may hold values from 0 to 17
- reward_bins: int32 [20480], P(('dp', 'mp')), may hold values from 0 to 3
- valid_flags: int32 [20480, 3], P(('dp', 'mp')), may hold values 0 or 1
- step_count: int32 [1], replicated, may hold values from 1 to 20
- entry_weight: float32 [3, 1280, 1280], P(None, 'dp', 'mp'), may hold values from -0.15625 to 0.15625
- entry_state: float32 [2, 3, 1280, 1280], P(None, None, 'dp', 'mp')
- exit_weight: float32 [1280, 1280], P(('mp', 'dp')), may hold values from -0.5 to 0.5
- exit_state: float32 [2, 1280, 1280], P(None, ('mp', 'dp'))
- up_weight: float32 [1280, 5120], P('dp', 'mp'), may hold values from -0.15625 to 0.15625
- up_state: float32 [2, 1280, 5120], P(None, 'dp', 'mp')
- down_weight: float32 [5120, 1280], P(('mp', 'dp')), may hold values from -0.078125 to 0.078125
- down_state: float32 [2, 5120, 1280], P(None, ('mp', 'dp'))
- head_weight: float32 [142, 1280], replicated, may hold values from -0.15625 to 0.15625
- head_state: float32 [2, 142, 1280], replicated
- norm_params: float32 [6, 1280], replicated
- norm_state: float32 [2, 6, 1280], replicated
Outputs:
- entry_new: float32 [3, 1280, 1280], P(None, 'dp', 'mp')
- entry_moments: float32 [2, 3, 1280, 1280], P(None, None, 'dp', 'mp')
- entry_half: bfloat16 [3, 1280, 1280], P(None, 'dp', 'mp')
- exit_new: float32 [1280, 1280], P(('mp', 'dp'))
- exit_moments: float32 [2, 1280, 1280], P(None, ('mp', 'dp'))
- exit_half: bfloat16 [1280, 1280], P(('mp', 'dp'))
- up_new: float32 [1280, 5120], P('dp', 'mp')
- up_moments: float32 [2, 1280, 5120], P(None, 'dp', 'mp')
- up_half: bfloat16 [1280, 5120], P('dp', 'mp')
- down_new: float32 [5120, 1280], P(('mp', 'dp'))
- down_moments: float32 [2, 5120, 1280], P(None, ('mp', 'dp'))
- down_half: bfloat16 [5120, 1280], P(('mp', 'dp'))
- head_new: float32 [142, 1280], replicated
- head_moments: float32 [2, 142, 1280], replicated
- norm_new: float32 [6, 1280], replicated
- norm_moments: float32 [2, 6, 1280], replicated
- total_loss: float32 [], replicated
- grad_norm: float32 [], replicated
- matrix_norms: float32 [2, 5], replicated
The draws below stay inside these ranges and needn't reach their ends.
Inputs may be any that keep to these rules, and one draw needn't show every extreme that they name: `segment_ids`: within each sequence of 160 tokens the segment numbers never fall.
All inputs are finite; a program needn't handle non-finite values. No bound on the sum of `valid_flags` on one device may be relied on, other than what follows from the above.
Results may differ from the reference program's by a relative error of at most 0.007.
Values may be sent and summed in bfloat16 or wider, within the bound.
No kernel may reach another device: no remote copies, remote signals or barrier semaphores. Data moves between devices by JAX's collectives and lax.ppermute only.
A program may use at most 384 MiB of HBM per device.

```python
import math
import jax
import jax.numpy as jnp
import numpy as np
from jax import lax

D = 1280
H = 20
HD = 64
FF = 5120
RB = 120
AB = 18
WB = 4
GAMES = 41
LEN = 160
SEQ_DEV = 8
R = 142
SEQS = 128
TOKENS = 20480
N_DP = 16


def clipped_size():
    return 0.05 / math.sqrt(4 * D * D + 2 * D * FF + D * R + 6 * D)


def moment_pair(key, label, shape, size):
    own_key = jax.random.fold_in(key, label)
    first_key = jax.random.fold_in(own_key, 11)
    second_key = jax.random.fold_in(own_key, 23)
    first = jax.random.normal(first_key, shape, jnp.float32) * size
    factor = jnp.exp(jax.random.uniform(second_key, shape, jnp.float32, 0.0, math.log(4.0)))
    return jnp.stack([first, jnp.sqrt(factor) * size])


def draw_entry_state(key, part):
    return moment_pair(key, 101, (3, D, D), clipped_size())


def draw_exit_state(key, part):
    return moment_pair(key, 202, (D, D), clipped_size())


def draw_up_state(key, part):
    return moment_pair(key, 303, (D, FF), clipped_size())


def draw_down_state(key, part):
    return moment_pair(key, 404, (FF, D), clipped_size())


def draw_head_state(key, part):
    return moment_pair(key, 505, (R, D), clipped_size())


def draw_norm_state(key, part):
    return moment_pair(key, 606, (6, D), 5.0 * clipped_size())


def draw_norm_params(key, part):
    gain_key = jax.random.fold_in(key, 31)
    shift_key = jax.random.fold_in(key, 37)
    place = jnp.arange(D, dtype=jnp.float32) / D
    ramp = 0.5 * jnp.exp(math.log(4.0) * place)
    rough = jax.random.uniform(gain_key, (3, D), jnp.float32, 0.7, 1.3)
    gains = rough * ramp[None, :]
    shifts = jax.random.normal(shift_key, (3, D), jnp.float32) * 0.2
    return jnp.concatenate([gains, shifts], 0)


def place_ends(array, key, low, largest):
    longest = array.shape.index(max(array.shape))
    spots = []
    for shift in (0, 1):
        where = [jax.random.randint(jax.random.fold_in(key, axis), (), 0, length) for axis, length in enumerate(array.shape)]
        where[longest] = (where[longest] + shift) % array.shape[longest]
        spots.append(tuple(where))
    return array.at[spots[0]].set(low).at[spots[1]].set(largest)


def shard_levels(rng, extent, shards, low, high):
    loudness = 1.0
    for position, shards_of in shards:
        heights = jax.random.uniform(jax.random.fold_in(jax.random.fold_in(rng, 6), position), (shards_of,), jnp.float32, low / len(shards), high / len(shards))
        loudness = loudness * jnp.repeat(jnp.exp(heights), extent[position] // shards_of).reshape((-1,) + (1,) * (len(extent) - 1 - position))
    return loudness


def length_profile(number_of, total, reach, slope):
    portions = [(1 << 20) // math.isqrt(grade ** slope) + 1 for grade in range(2, number_of + 1)]
    surplus, holding = total - reach - (number_of - 1), [1] * (number_of - 1)
    while surplus > 0:
        movable = [i for i in range(number_of - 1) if holding[i] < reach]
        whole, left = sum([portions[i] for i in movable]), surplus
        for i in movable:
            extra = min(reach - holding[i], max(1, left * portions[i] // whole), surplus)
            holding[i] = holding[i] + extra
            surplus = surplus - extra
    return np.array([reach] + holding)


def ragged(key, amount, total, limit, lean):
    if amount == 2:
        one = jax.random.randint(key, (), max(1, total - limit), min(limit, total - 1) + 1)
        return jnp.stack([one, total - one])
    sizes = jnp.asarray(length_profile(amount, total, limit, lean), jnp.int32)
    twos = (amount - 1) // 2
    source_of, sink = sizes[1:1 + 2 * twos:2], sizes[2:2 + 2 * twos:2]
    slack = jnp.minimum(source_of - 1, limit - sink)
    passed = jax.random.randint(jax.random.fold_in(key, 1), (twos,), 0, 1 << 20) % (slack + 1)
    sizes = sizes.at[1:1 + 2 * twos:2].set(source_of - passed).at[2:2 + 2 * twos:2].set(sink + passed)
    return sizes[jax.random.permutation(jax.random.fold_in(key, 2), amount)]


def bell_draw(key, shape, deviation, most, shards=(), held_as=jnp.bfloat16):
    level = shard_levels(key, shape, shards, -0.22, 0.18) if shards else 1.0
    values = jax.random.normal(key, shape, jnp.float32) * deviation * level
    return jnp.minimum(jnp.maximum(values, -most), most).astype(held_as)


def setup_inputs(seed: int = 0) -> dict:
    splits = jax.random.split(jax.random.key(seed), 21)
    tokens = bell_draw(splits[0], (TOKENS, D), 1.0, 6.0, ((0, 32),))
    segment_ids = jax.vmap(lambda own: jnp.searchsorted(jnp.cumsum(ragged(own, 4, LEN, LEN // 2, 0)), jnp.arange(LEN), side="right"))(jax.random.split(splits[1], SEQS)).reshape((SEQS, LEN)).astype(jnp.int32)
    game_ids = place_ends(jax.random.randint(splits[2], (SEQS,), 0, GAMES), jax.random.fold_in(splits[2], 1), 0, GAMES - 1).astype(jnp.int32)
    return_bins = place_ends(jax.random.randint(splits[3], (TOKENS,), 0, RB), jax.random.fold_in(splits[3], 1), 0, RB - 1).astype(jnp.int32)
    action_bins = place_ends(jax.random.randint(splits[4], (TOKENS,), 0, AB), jax.random.fold_in(splits[4], 1), 0, AB - 1).astype(jnp.int32)
    reward_bins = place_ends(jax.random.randint(splits[5], (TOKENS,), 0, WB), jax.random.fold_in(splits[5], 1), 0, WB - 1).astype(jnp.int32)
    valid_flags = place_ends((jax.random.randint(splits[6], (TOKENS, 3), 0, 4) < 3).astype(jnp.int32), jax.random.fold_in(splits[6], 1), 0, 1)
    step_count = jax.random.randint(splits[7], (1,), 1, 21).astype(jnp.int32)
    entry_weight = bell_draw(splits[8], (3, D, D), D ** -0.5, 0.15625, ((1, 16), (2, 2)), jnp.float32)
    entry_state = draw_entry_state(jax.random.fold_in(splits[20], 71), 0)
    exit_weight = bell_draw(splits[10], (D, D), (D // 8) ** -0.5, 0.5, ((0, 32),), jnp.float32)
    exit_state = draw_exit_state(jax.random.fold_in(splits[20], 71), 0)
    up_weight = bell_draw(splits[12], (D, FF), D ** -0.5, 0.15625, ((0, 16), (1, 2)), jnp.float32)
    up_state = draw_up_state(jax.random.fold_in(splits[20], 71), 0)
    down_weight = bell_draw(splits[14], (FF, D), FF ** -0.5, 0.078125, ((0, 32),), jnp.float32)
    down_state = draw_down_state(jax.random.fold_in(splits[20], 71), 0)
    head_weight = bell_draw(splits[16], (R, D), D ** -0.5, 0.15625, (), jnp.float32)
    head_state = draw_head_state(jax.random.fold_in(splits[20], 71), 0)
    norm_params = draw_norm_params(jax.random.fold_in(splits[20], 71), 0)
    norm_state = draw_norm_state(jax.random.fold_in(splits[20], 71), 0)
    return dict(tokens=tokens, segment_ids=segment_ids, game_ids=game_ids, return_bins=return_bins, action_bins=action_bins, reward_bins=reward_bins, valid_flags=valid_flags, step_count=step_count, entry_weight=entry_weight, entry_state=entry_state, exit_weight=exit_weight, exit_state=exit_state, up_weight=up_weight, up_state=up_state, down_weight=down_weight, down_state=down_state, head_weight=head_weight, head_state=head_state, norm_params=norm_params, norm_state=norm_state)


@jax.custom_vjp
def low(v):
    return lax.optimization_barrier(v.astype(jnp.bfloat16)).astype(jnp.float32)

@jax.custom_vjp
def low_back(v):
    return v

def low_keep(v):
    return (low(v), None)

def low_pass(kept, grad):
    return (grad,)

def back_keep(v):
    return (v, None)

def back_low(kept, grad):
    return (low(grad),)
low.defvjp(low_keep, low_pass)
low_back.defvjp(back_keep, back_low)
precise = lax.Precision.HIGHEST
clip_limit = 0.05
learn_rate = 0.5
beta_first = 0.5
beta_second = 0.5
weight_decay = 0.01
adam_eps = 1e-08
norm_eps = 1e-05
masked_score = -1e+30

def layer_norm(rows, gain, shift):
    centred = rows - lax.optimization_barrier(jnp.mean(rows, -1, keepdims=True))
    spread = lax.optimization_barrier(jnp.mean(centred * centred, -1, keepdims=True))
    return centred * lax.rsqrt(spread + norm_eps) * gain + shift

def matmul(left, right):
    return jnp.dot(left, right, precision=precise, preferred_element_type=jnp.float32)

def both_ways(value):
    return low(low_back(value))

def part_loss(logits, targets, flags, token_scale):
    summed = jnp.zeros((), jnp.float32)
    offset = 0
    for column, span_cols in enumerate((RB, AB, WB)):
        section = logits[:, offset:offset + span_cols]
        log_probs = jax.nn.log_softmax(section, axis=-1)
        picked = (targets[column][:, None] == jnp.arange(span_cols)[None, :]).astype(jnp.float32)
        cross = -lax.optimization_barrier(jnp.sum(log_probs * picked, -1))
        summed = summed + jnp.sum(flags[:, column].astype(jnp.float32) * token_scale * cross)
        offset = offset + span_cols
    return summed

def attend_block(inputs):
    queries, key_rows, values, combined = inputs
    count_rows = combined.shape[0]
    order_ids = jnp.arange(count_rows)
    allowed = (combined[:, None] == combined[None, :]) & (order_ids[None, :] <= order_ids[:, None])
    shape_heads = (count_rows, H, HD)
    scores = jnp.einsum('ihd,jhd->hij', queries.reshape(shape_heads), key_rows.reshape(shape_heads), precision=precise) * HD ** (-0.5)
    scores = jnp.where(allowed[None], low_back(scores), masked_score)
    log_total = jax.nn.logsumexp(scores, axis=-1, keepdims=True)
    probs = low(jnp.exp(scores - log_total))
    context = jnp.einsum('hij,jhd->ihd', probs, values.reshape(shape_heads), precision=precise)
    return context.reshape(count_rows, D)

def forward(weights, tokens_f, combined, targets, flags, token_scale):
    entry_mat, exit_mat, up_mat, down_mat, head_mat, norm_rows = weights
    normed_one = low(layer_norm(tokens_f, norm_rows[0], norm_rows[3]))
    queries = both_ways(matmul(normed_one, entry_mat[0]))
    key_rows = both_ways(matmul(normed_one, entry_mat[1]))
    values = both_ways(matmul(normed_one, entry_mat[2]))
    block_shape = (N_DP, SEQ_DEV * LEN, D)
    context = lax.map(jax.checkpoint(attend_block), (queries.reshape(block_shape), key_rows.reshape(block_shape), values.reshape(block_shape), combined))
    context = both_ways(context.reshape(TOKENS, D))
    after_attn = tokens_f + low_back(matmul(context, exit_mat))
    normed_two = low(layer_norm(after_attn, norm_rows[1], norm_rows[4]))
    up_pre = low_back(matmul(normed_two, up_mat))
    activated = low(jax.nn.gelu(up_pre))
    after_mlp = after_attn + low_back(matmul(activated, down_mat))
    final_norm = low(layer_norm(after_mlp, norm_rows[2], norm_rows[5]))
    logits = low_back(matmul(final_norm, head_mat.T))
    return part_loss(logits, targets, flags, token_scale)

def adam_moments(state, grad, clip_factor, corr_first, corr_second):
    clipped = clip_factor * grad
    first = beta_first * state[0] + (1.0 - beta_first) * clipped
    second = beta_second * state[1] * state[1] + (1.0 - beta_second) * clipped * clipped
    direction = first / corr_first / (jnp.sqrt(second / corr_second) + adam_eps)
    return (jnp.stack([first, jnp.sqrt(second)]), direction)

def reference(tokens, segment_ids, game_ids, return_bins, action_bins, reward_bins, valid_flags, step_count, entry_weight, entry_state, exit_weight, exit_state, up_weight, up_state, down_weight, down_state, head_weight, head_state, norm_params, norm_state):
    flag_float = valid_flags.astype(jnp.float32)
    token_games = jnp.repeat(game_ids, LEN)
    game_match = (token_games[:, None] == jnp.arange(GAMES)[None, :]).astype(jnp.float32)
    counts = lax.optimization_barrier(jnp.sum(game_match * lax.optimization_barrier(jnp.sum(flag_float, -1, keepdims=True)), 0))
    inverse = 1.0 / (GAMES * jnp.maximum(counts, 1.0))
    token_scale = lax.optimization_barrier(jnp.sum(game_match * inverse[None, :], -1))
    combined = (jnp.arange(SEQS)[:, None] * LEN + segment_ids).reshape(N_DP, SEQ_DEV * LEN)
    targets = (return_bins, action_bins, reward_bins)
    tokens_f = tokens.astype(jnp.float32)
    masters = (entry_weight, exit_weight, up_weight, down_weight, head_weight, norm_params)
    states = (entry_state, exit_state, up_state, down_state, head_state, norm_state)
    rounded = (low(entry_weight), low(exit_weight), low(up_weight), low(down_weight), low(head_weight), norm_params)
    total_loss, pullback = jax.vjp(lambda params: forward(params, tokens_f, combined, targets, valid_flags, token_scale), rounded)
    grads = pullback(jnp.ones_like(total_loss))[0]
    grad_norm = jnp.sqrt(sum((jnp.sum(grad_part * grad_part) for grad_part in grads)))
    clip_factor = jnp.minimum(1.0, clip_limit / grad_norm)
    step_float = step_count[0].astype(jnp.float32)
    corr_first = 1.0 - jnp.power(beta_first, step_float)
    corr_second = 1.0 - jnp.power(beta_second, step_float)
    new_weights = []
    new_states = []
    weight_norms = []
    update_norms = []
    for matrix_id in range(5):
        state_new, direction = adam_moments(states[matrix_id], grads[matrix_id], clip_factor, corr_first, corr_second)
        direction = direction + weight_decay * masters[matrix_id]
        weight_norm = jnp.sqrt(jnp.sum(masters[matrix_id] * masters[matrix_id]))
        update_norm = jnp.sqrt(jnp.sum(direction * direction))
        new_weights.append(masters[matrix_id] - learn_rate * (weight_norm / update_norm) * direction)
        new_states.append(state_new)
        weight_norms.append(weight_norm)
        update_norms.append(update_norm)
    norm_moments, norm_direction = adam_moments(norm_state, grads[5], clip_factor, corr_first, corr_second)
    norm_new = norm_params - learn_rate * norm_direction
    matrix_norms = jnp.stack([jnp.stack(weight_norms), jnp.stack(update_norms)])
    return (new_weights[0], new_states[0], new_weights[0].astype(jnp.bfloat16), new_weights[1], new_states[1], new_weights[1].astype(jnp.bfloat16), new_weights[2], new_states[2], new_weights[2].astype(jnp.bfloat16), new_weights[3], new_states[3], new_weights[3].astype(jnp.bfloat16), new_weights[4], new_states[4], norm_new, norm_moments, total_loss, grad_norm, matrix_norms)
```

```python
import functools

import jax
import jax.numpy as jnp
import numpy as np
from jax import lax
from jax.experimental import pallas as pl
from jax.experimental.pallas import tpu as pltpu
from jax.sharding import PartitionSpec as P

HD = 64
RB = 120
AB = 18
WB = 4
GAMES = 41
LEN = 160


clip_limit = 0.05
learn_rate = 0.5
beta_first = 0.5
beta_second = 0.5
weight_decay = 0.01
adam_eps = 1e-08
norm_eps = 1e-05
masked_score = -1e30


def layer_norm(rows, gain, shift):
    centred = rows - jnp.mean(rows, -1, keepdims=True)
    spread = jnp.mean(centred * centred, -1, keepdims=True)
    return centred * lax.rsqrt(spread + norm_eps) * gain + shift


def norm_back(rows, gain, shift, upstream):
    _, pullback = jax.vjp(layer_norm, rows, gain, shift)
    return pullback(upstream)


def matmul(left, right):
    return jnp.dot(left, right, preferred_element_type=jnp.float32)


def matmul_t(left, right):
    return jnp.einsum("ti,ji->tj", left, right, preferred_element_type=jnp.float32)


def contract(left, right):
    return jnp.einsum("ti,tj->ij", left, right, preferred_element_type=jnp.float32)


def part_loss(logits, targets, flags, token_scale):
    summed = jnp.zeros((), jnp.float32)
    offset = 0
    for column, span_cols in enumerate((RB, AB, WB)):
        section = logits[:, offset : offset + span_cols]
        log_probs = jax.nn.log_softmax(section, axis=-1)
        picked = (targets[column][:, None] == jnp.arange(span_cols)[None, :]).astype(jnp.float32)
        cross = -jnp.sum(log_probs * picked, -1)
        summed = summed + jnp.sum(flags[:, column].astype(jnp.float32) * token_scale * cross)
        offset = offset + span_cols
    return summed


AXES = ("dp", "mp")
VMEM_LIMIT = 60 * 2**20
ANY = pl.BlockSpec(memory_space=pl.ANY)


class Plan:
    def __init__(self, dp, mp):
        self.dp, self.mp = dp, mp
        self.core = 2 if dp % 2 == 0 else 1
        self.y = 2 if dp % (2 * self.core) == 0 else 1
        self.z = dp // (self.core * self.y)
        self.n = dp * mp
        self.grid = np.arange(self.n).reshape(self.z, self.y, self.core, mp)
        self.place = [tuple(int(v) for v in np.argwhere(self.grid == i)[0]) for i in range(self.n)]

    def pairs(self, move):
        found = []
        for i, spot in enumerate(self.place):
            target = move(*spot)
            if target is not None and 0 <= target[0] < self.z:
                found.append((i, int(self.grid[target])))
        return found

    def flip_core(self):
        return self.pairs(lambda z, y, c, x: (z, y, 1 - c, x))

    def flip_first(self):
        return self.pairs(lambda z, y, c, x: (z, 1 - y, c, x) if c == 0 else (z, y, c, 1 - x))

    def flip_second(self):
        return self.pairs(lambda z, y, c, x: (z, y, c, 1 - x) if c == 0 else (z, 1 - y, c, x))

    def flip_z(self, bits):
        return self.pairs(lambda z, y, c, x: (z ^ bits, y, c, x))

    def z_moves(self):
        return [self.flip_z(bits) for bits in range(1, self.z)]


def moved(table, pairs):
    got = np.full_like(table, -1)
    for source, target in pairs:
        got[target] = table[source]
    return got


def send(value, pairs):
    return lax.ppermute(value, AXES, pairs)


def add_all(parts, dtype=jnp.bfloat16):
    total = parts[0].astype(jnp.float32)
    for part in parts[1:]:
        total = total + part.astype(jnp.float32)
    return total.astype(dtype)


class Travel:
    def __init__(self, name, steps, quiet=False):
        self.name, self.steps, self.quiet = name, steps, quiet
        self.result, self.going = None, None
        self.wanted = next(steps)


class Clock:
    def __init__(self):
        self.gates = []

    def hold(self, values):
        flat, tree = jax.tree.flatten(values)
        passed = lax.optimization_barrier(tuple(flat) + tuple(self.gates))
        return jax.tree.unflatten(tree, passed[: len(flat)])

    def start(self, travels, more=()):
        values, more = self.hold(([[v for v, _ in travel.wanted] for travel in travels], more))
        self.gates = []
        for travel, ready in zip(travels, values):
            with jax.named_scope(travel.name):
                travel.going = [send(v, pairs) for v, (_, pairs) in zip(ready, travel.wanted)]
        return more

    def wait(self, travels):
        for travel in travels:
            if not travel.quiet:
                self.gates = self.gates + travel.going
            try:
                travel.wanted = travel.steps.send(travel.going)
            except StopIteration as end:
                travel.wanted, travel.result = None, end.value
            travel.going = None

    def also(self, *values):
        self.gates = self.gates + list(values)


def path_table(plan):
    first, second, core = plan.flip_first(), plan.flip_second(), plan.flip_core()
    own = np.arange(plan.n)[:, None]
    line = np.concatenate([own] + [moved(own, pairs) for pairs in plan.z_moves()], 1)
    near, side = moved(line, first), moved(line, second)
    table = np.concatenate([line, near, side, moved(near, second)], 1)
    return np.concatenate([table, moved(table, core)], 1)


def gather_shards(plan, shard):
    first, second, core = plan.flip_first(), plan.flip_second(), plan.flip_core()
    got = yield [(shard[None], pairs) for pairs in plan.z_moves()]
    line = jnp.concatenate([shard[None]] + got)
    near, side = yield [(line, first), (line, second)]
    far, line_twin, near_twin = yield [(near, second), (line, core), (near, core)]
    side_twin, far_twin = yield [(side, core), (far, core)]
    return [line, near, side, far, line_twin, near_twin, side_twin, far_twin]


def scatter_counts(plan):
    return [4 * plan.z, 3 * plan.z, plan.z]


def scatter_shards(plan, pieces):
    first, second, core = plan.flip_first(), plan.flip_second(), plan.flip_core()
    own, rest_twin, far_twin = pieces
    size = plan.z

    def quarter(value, k):
        return value[k * size : (k + 1) * size]

    far_got, rest_got = yield [(far_twin, core), (rest_twin, core)]
    (far_got,) = yield [(add_all([quarter(own, 3), far_got]), second)]
    near = add_all([quarter(own, 1), quarter(rest_got, 1), far_got])
    side = add_all([quarter(own, 2), quarter(rest_got, 2)])
    near_got, side_got = yield [(near, first), (side, second)]
    terms = [quarter(own, 0), quarter(rest_got, 0), near_got, side_got]
    got = yield [
        (add_all([term[k + 1 : k + 2] for term in terms]), pairs)
        for k, pairs in enumerate(plan.z_moves())
    ]
    return add_all([term[:1] for term in terms] + got, jnp.float32)[0]


def total_steps(plan, value, halves=False):
    if halves:
        half = value.shape[0] // 2
        upper = lax.axis_index("dp") % 2 == 1
        keep = jnp.where(upper, value[half:], value[:half])
        (got,) = yield [(jnp.where(upper, value[:half], value[half:]), plan.flip_core())]
        value = keep + got
    else:
        (got,) = yield [(value, plan.flip_core())]
        value = value + got
    moves = [
        plan.pairs(lambda z, y, c, x: (z, y, c, 1 - x)),
        plan.pairs(lambda z, y, c, x: (z, 1 - y, c, x)),
    ]
    bit = 1
    while bit < plan.z:
        moves.append(plan.flip_z(bit))
        bit *= 2
    for pairs in moves:
        (got,) = yield [(value, pairs)]
        value = value + got
    if halves:
        (got,) = yield [(value, plan.flip_core())]
        return jnp.where(upper, jnp.concatenate([got, value]), jnp.concatenate([value, got]))
    return value


def total_over_devices(plan, value):
    travel, clock = Travel("small_sum", total_steps(plan, value)), Clock()
    while travel.wanted:
        clock.start([travel])
        clock.wait([travel])
    return travel.result


def slot_counts(pieces):
    counts = [piece.shape[0] for piece in pieces]
    return counts, [sum(counts[:i]) for i in range(len(counts))]


def spot_of(device, plan, split_columns):
    if split_columns:
        return device // plan.mp, device % plan.mp
    return (device % plan.mp) * plan.dp + device // plan.mp, 0


def assemble(plan, pieces, slots, split_columns):
    counts, offsets = slot_counts(pieces)
    total = sum(counts)
    rows, width = pieces[0].shape[1:]
    groups = plan.mp if split_columns else 1
    blocks = total // groups
    if rows % 16 and groups > 1 or width % 128:
        stacked = jnp.concatenate(pieces)
        stacked = lax.fori_loop(
            0,
            total,
            lambda i, held: lax.dynamic_update_index_in_dim(held, stacked[i], slots[i], 0),
            stacked,
        ).reshape(plan.dp, plan.mp, rows, width)
        if split_columns:
            return stacked.transpose(0, 2, 1, 3).reshape(plan.dp * rows, plan.mp * width)
        return stacked.transpose(1, 0, 2, 3).reshape(total * rows, width)
    depth = 8

    def kernel(slots_ref, *refs):
        sources, out = refs[: len(pieces)], refs[len(pieces)]
        held, in_sems, out_sems = refs[len(pieces) + 1 :]
        steps = [(a, s) for a in range(len(pieces)) for s in range(counts[a])]
        reads, writes = [], []
        for i, (a, s) in enumerate(steps):
            block, group = spot_of(slots_ref[i], plan, split_columns)
            columns = pl.ds(pl.multiple_of(group * width, 128), width)
            reads.append(pltpu.make_async_copy(sources[a].at[s], held.at[i], in_sems.at[i]))
            writes.append(
                pltpu.make_async_copy(held.at[i], out.at[block, :, columns], out_sems.at[i])
            )
        for i in range(total):
            reads[i].start()
        for i in range(total):
            reads[i].wait()
            writes[i].start()
        for i in range(total):
            writes[i].wait()

    whole = pl.pallas_call(
        kernel,
        out_shape=jax.ShapeDtypeStruct((blocks, rows, groups * width), pieces[0].dtype),
        grid_spec=pltpu.PrefetchScalarGridSpec(
            num_scalar_prefetch=1,
            grid=(1,),
            in_specs=[ANY] * len(pieces),
            out_specs=ANY,
            scratch_shapes=[
                pltpu.VMEM((total, rows, width), pieces[0].dtype),
                pltpu.SemaphoreType.DMA((total,)),
                pltpu.SemaphoreType.DMA((total,)),
            ],
        ),
        compiler_params=pltpu.CompilerParams(vmem_limit_bytes=VMEM_LIMIT),
        cost_estimate=pl.CostEstimate(
            flops=0, bytes_accessed=4 * total * rows * width, transcendentals=0
        ),
    )(slots, *pieces)
    return whole.reshape(blocks * rows, groups * width)


def disassemble(plan, whole, shard_shape, counts, slots, split_columns):
    total = sum(counts)
    rows, width = shard_shape
    groups = plan.mp if split_columns else 1
    offsets = [sum(counts[:i]) for i in range(len(counts))]
    if rows % 16 and groups > 1 or width % 128:
        if split_columns:
            shards = whole.reshape(plan.dp, rows, plan.mp, width).transpose(0, 2, 1, 3)
        else:
            shards = whole.reshape(plan.mp, plan.dp, rows, width).transpose(1, 0, 2, 3)
        source = shards.reshape(total, rows, width)
        shards = lax.fori_loop(
            0,
            total,
            lambda i, held: lax.dynamic_update_index_in_dim(held, source[slots[i]], i, 0),
            source,
        )
        return [shards[o : o + c] for o, c in zip(offsets, counts)]
    blocks = total // groups

    def kernel(slots_ref, source, *refs):
        outs = refs[: len(counts)]
        held, in_sems, out_sems = refs[len(counts) :]
        steps = [(a, s) for a in range(len(counts)) for s in range(counts[a])]
        reads, writes = [], []
        for i, (a, s) in enumerate(steps):
            block, group = spot_of(slots_ref[i], plan, split_columns)
            columns = pl.ds(pl.multiple_of(group * width, 128), width)
            reads.append(
                pltpu.make_async_copy(source.at[block, :, columns], held.at[i], in_sems.at[i])
            )
            writes.append(pltpu.make_async_copy(held.at[i], outs[a].at[s], out_sems.at[i]))
        for i in range(total):
            reads[i].start()
        for i in range(total):
            reads[i].wait()
            writes[i].start()
        for i in range(total):
            writes[i].wait()

    return pl.pallas_call(
        kernel,
        out_shape=[jax.ShapeDtypeStruct((c, rows, width), whole.dtype) for c in counts],
        grid_spec=pltpu.PrefetchScalarGridSpec(
            num_scalar_prefetch=1,
            grid=(1,),
            in_specs=[ANY],
            out_specs=[ANY] * len(counts),
            scratch_shapes=[
                pltpu.VMEM((total, rows, width), whole.dtype),
                pltpu.SemaphoreType.DMA((total,)),
                pltpu.SemaphoreType.DMA((total,)),
            ],
        ),
        compiler_params=pltpu.CompilerParams(vmem_limit_bytes=VMEM_LIMIT),
        cost_estimate=pl.CostEstimate(
            flops=0, bytes_accessed=4 * total * rows * width, transcendentals=0
        ),
    )(slots, whole.reshape(blocks, rows, groups * width))


PAIR = 2 * HD


def pair_blocks(ref, offset, group, pair, pairs):
    start = group * 3 * pairs * PAIR + pair * PAIR
    span = pairs * PAIR
    return [ref[:, start + part * span : start + part * span + PAIR] for part in range(3)]


def both_heads(block):
    low_lane = lax.broadcasted_iota(jnp.int32, block.shape, 1) < HD
    zero = jnp.zeros_like(block)
    return jnp.concatenate([jnp.where(low_lane, block, zero), jnp.where(low_lane, zero, block)])


def own_columns(stacked):
    rows = stacked.shape[0] // 2
    low_lane = lax.broadcasted_iota(jnp.int32, (rows, PAIR), 1) < HD
    return jnp.where(low_lane, stacked[:rows], stacked[rows:])


def rows_by_rows(left, right):
    return lax.dot_general(left, right, (((1,), (1,)), ((), ())), preferred_element_type=jnp.float32)


def rows_of_both(left, right):
    return lax.dot_general(left, right, (((0,), (0,)), ((), ())), preferred_element_type=jnp.float32)


def pair_probs(stacked_queries, keys, allowed):
    scores = rows_by_rows(stacked_queries, keys) * HD ** (-0.5)
    scores = jnp.where(allowed, scores, masked_score)
    raised = jnp.exp(scores - jnp.max(scores, -1, keepdims=True))
    return raised * (1.0 / jnp.sum(raised, -1, keepdims=True))


def allowed_pairs(column_ref, row_ref):
    same = column_ref[0] == row_ref[0]
    shape = same.shape
    causal = lax.broadcasted_iota(jnp.int32, shape, 1) <= lax.broadcasted_iota(jnp.int32, shape, 0)
    one = (same & causal).astype(jnp.float32)
    return jnp.concatenate([one, one]) > 0.5


def attend_kernel(groups, pairs, column_ref, row_ref, qkv_ref, context_ref):
    allowed = allowed_pairs(column_ref, row_ref)
    for group in range(groups):
        for pair in range(pairs):
            queries, keys, values = pair_blocks(qkv_ref, 0, group, pair, pairs)
            probs = pair_probs(both_heads(queries), keys, allowed).astype(jnp.bfloat16)
            context = own_columns(matmul(probs, values))
            start = (group * pairs + pair) * PAIR
            context_ref[:, start : start + PAIR] = context.astype(jnp.bfloat16)


def attend_back_kernel(groups, pairs, column_ref, row_ref, qkv_ref, d_context_ref, d_qkv_ref):
    allowed = allowed_pairs(column_ref, row_ref)
    span = pairs * PAIR
    for group in range(groups):
        for pair in range(pairs):
            queries, keys, values = pair_blocks(qkv_ref, 0, group, pair, pairs)
            start = (group * pairs + pair) * PAIR
            d_context = both_heads(d_context_ref[:, start : start + PAIR])
            queries = both_heads(queries)
            probs = pair_probs(queries, keys, allowed)
            d_probs = rows_by_rows(d_context, values)
            d_values = rows_of_both(probs.astype(jnp.bfloat16), d_context)
            mean = jnp.sum(probs * d_probs, -1, keepdims=True)
            d_scores = (probs * (d_probs - mean)).astype(jnp.bfloat16)
            d_queries = own_columns(matmul(d_scores, keys)) * HD ** (-0.5)
            d_keys = rows_of_both(d_scores, queries) * HD ** (-0.5)
            start = group * 3 * span + pair * PAIR
            for part, value in enumerate((d_queries, d_keys, d_values)):
                at = start + part * span
                d_qkv_ref[:, at : at + PAIR] = value.astype(jnp.bfloat16)


def attend_call(kernel, segments, qkv, others, out_columns, groups, scale):
    count = segments.shape[0]
    columns = qkv.shape[1]
    pairs = columns // (3 * groups * PAIR)
    rows = lambda wide: pl.BlockSpec((LEN, wide), lambda i: (i, 0))
    return pl.pallas_call(
        functools.partial(kernel, groups, pairs),
        out_shape=jax.ShapeDtypeStruct((qkv.shape[0], out_columns), jnp.bfloat16),
        grid=(count,),
        in_specs=[
            pl.BlockSpec((1, LEN, 1), lambda i: (i, 0, 0)),
            pl.BlockSpec((1, 1, LEN), lambda i: (i, 0, 0)),
            rows(columns),
        ]
        + [rows(other.shape[1]) for other in others],
        out_specs=rows(out_columns),
        compiler_params=pltpu.CompilerParams(vmem_limit_bytes=VMEM_LIMIT),
        cost_estimate=pl.CostEstimate(
            flops=scale * count * 2 * LEN * LEN * columns // 3,
            bytes_accessed=scale * qkv.size * 2,
            transcendentals=count * LEN * LEN * columns // (3 * HD),
        ),
    )(segments[:, :, None], segments[:, None, :], qkv, *others)


class Spread:
    def __init__(self, plan, parts, split_columns):
        self.plan, self.parts, self.split_columns = plan, parts, split_columns
        self.pieces = [piece for pieces, _ in parts for piece in pieces]
        self.slots = jnp.concatenate([slots for _, slots in parts])
        self.rows = self.pieces[0].shape[1]
        widths = [pieces[0].shape[2] for pieces, _ in parts]
        self.offsets = [sum(widths[:k]) for k in range(len(widths))]
        self.stride = sum(widths)
        groups = plan.mp if split_columns else 1
        self.shape = (plan.n // groups * self.rows, groups * self.stride)
        self.aligned = self.rows % 16 == 0 and all(width % 128 == 0 for width in widths)

    def matrix(self):
        groups = self.plan.mp if self.split_columns else 1
        wholes = [
            assemble(self.plan, pieces, slots, self.split_columns).reshape(
                self.shape[0], groups, -1
            )
            for pieces, slots in self.parts
        ]
        return jnp.concatenate(wholes, 2).reshape(self.shape)

    def places(self):
        found, first = [], 0
        for (pieces, _), offset in zip(self.parts, self.offsets):
            for k, piece in enumerate(pieces):
                found = found + [(first + k, slot, offset) for slot in range(piece.shape[0])]
            first = first + len(pieces)
        return found


def spot_slice(matrix_ref, plan, device, rows, width, split_columns, offset, stride):
    block, group = spot_of(device, plan, split_columns)
    at_rows = pl.ds(pl.multiple_of(block * rows, rows), rows)
    start = offset if isinstance(group, int) else pl.multiple_of(group * stride + offset, 128)
    return matrix_ref.at[at_rows, pl.ds(start, width)]


def with_matrices(plan, body, spreads, operands, outs, steps, flops):
    sizes = [len(spread.pieces) for spread in spreads]
    total = sum(spread.slots.shape[0] for spread in spreads)

    def kernel(slots_ref, *refs):
        inputs, refs = refs[: len(operands)], refs[len(operands) :]
        sources, refs = refs[: sum(sizes)], refs[sum(sizes) :]
        results, refs = refs[: len(outs)], refs[len(outs) :]
        matrices, sems = refs[: len(spreads)], refs[len(spreads)]

        @pl.when(pl.program_id(0) == 0)
        def _():
            copies, first = [], 0
            for spread, matrix in zip(spreads, matrices):
                for which, slot, offset in spread.places():
                    i = len(copies)
                    spot = spot_slice(
                        matrix,
                        plan,
                        slots_ref[i],
                        spread.rows,
                        spread.pieces[which].shape[2],
                        spread.split_columns,
                        offset,
                        spread.stride,
                    )
                    source = sources[first + which].at[slot]
                    copies.append(pltpu.make_async_copy(source, spot, sems.at[i]))
                    copies[-1].start()
                first = first + len(spread.pieces)
            for copy in copies:
                copy.wait()

        body(inputs, matrices, results)

    moved_bytes = sum(2 * spread.shape[0] * spread.shape[1] for spread in spreads)
    moved_bytes += sum(array.size * array.dtype.itemsize for array, _, _ in operands)
    moved_bytes += sum(np.prod(shape) * np.dtype(dtype).itemsize for shape, dtype, _, _ in outs)
    return pl.pallas_call(
        kernel,
        out_shape=[jax.ShapeDtypeStruct(shape, dtype) for shape, dtype, _, _ in outs],
        grid_spec=pltpu.PrefetchScalarGridSpec(
            num_scalar_prefetch=1,
            grid=(steps,),
            in_specs=[pl.BlockSpec(block, index) for _, block, index in operands]
            + [ANY] * sum(sizes),
            out_specs=[pl.BlockSpec(block, index) for _, _, block, index in outs],
            scratch_shapes=[pltpu.VMEM(spread.shape, jnp.bfloat16) for spread in spreads]
            + [pltpu.SemaphoreType.DMA((total,))],
        ),
        compiler_params=pltpu.CompilerParams(vmem_limit_bytes=VMEM_LIMIT),
        cost_estimate=pl.CostEstimate(
            flops=flops, bytes_accessed=int(moved_bytes), transcendentals=0
        ),
    )(
        jnp.concatenate([spread.slots for spread in spreads]),
        *[array for array, _, _ in operands],
        *[piece for spread in spreads for piece in spread.pieces],
    )


def fixed(step, slots):
    return (0, 0)


def by_columns(step, slots):
    return (0, step)


def by_rows(step, slots):
    return (step, 0)


def step_slice(size):
    return pl.ds(pl.multiple_of(pl.program_id(0) * size, size), size)


def project(rows, spread, block):
    count, deep = rows.shape
    wide = spread.shape[1]
    if not spread.aligned or wide % block:
        return matmul(rows, spread.matrix()).astype(jnp.bfloat16)

    def body(inputs, matrices, results):
        product = matmul(inputs[0][...], matrices[0][:, step_slice(block)])
        results[0][...] = product.astype(jnp.bfloat16)

    return with_matrices(
        spread.plan,
        body,
        [spread],
        [(rows, (count, deep), fixed)],
        [((count, wide), jnp.bfloat16, (count, block), by_columns)],
        wide // block,
        2 * count * deep * wide,
    )[0]


def project_back(rows, spread, block):
    count, deep = rows.shape
    wide = spread.shape[0]
    if not spread.aligned or wide % block:
        return matmul_t(rows, spread.matrix())

    def body(inputs, matrices, results):
        results[0][...] = rows_by_rows(inputs[0][...], matrices[0][step_slice(block), :])

    return with_matrices(
        spread.plan,
        body,
        [spread],
        [(rows, (count, deep), fixed)],
        [((count, wide), jnp.float32, (count, block), by_columns)],
        wide // block,
        2 * count * deep * wide,
    )[0]


def hidden_forward(rows, spread, block):
    count, deep = rows.shape
    wide = spread.shape[1]
    if not spread.aligned or wide % block:
        up_pre = matmul(rows, spread.matrix())
        return up_pre, jax.nn.gelu(up_pre).astype(jnp.bfloat16)

    def body(inputs, matrices, results):
        up_pre = matmul(inputs[0][...], matrices[0][:, step_slice(block)])
        results[0][...] = up_pre
        results[1][...] = jax.nn.gelu(up_pre).astype(jnp.bfloat16)

    return with_matrices(
        spread.plan,
        body,
        [spread],
        [(rows, (count, deep), fixed)],
        [
            ((count, wide), jnp.float32, (count, block), by_columns),
            ((count, wide), jnp.bfloat16, (count, block), by_columns),
        ],
        wide // block,
        2 * count * deep * wide,
    )


def hidden_back(d_out, up_pre, spread, block):
    count, wide = up_pre.shape
    if not spread.aligned or wide % block:
        d_activated = matmul_t(d_out, spread.matrix())
        return jax.vjp(jax.nn.gelu, up_pre)[1](d_activated)[0].astype(jnp.bfloat16)

    def body(inputs, matrices, results):
        d_activated = rows_by_rows(inputs[0][...], matrices[0][step_slice(block), :])
        slope = jax.vjp(jax.nn.gelu, inputs[1][...])[1](d_activated)[0]
        results[0][...] = slope.astype(jnp.bfloat16)

    return with_matrices(
        spread.plan,
        body,
        [spread],
        [(d_out, d_out.shape, fixed), (up_pre, (count, block), by_columns)],
        [((count, wide), jnp.bfloat16, (count, block), by_columns)],
        wide // block,
        2 * count * d_out.shape[1] * wide,
    )[0]


def hidden_out(activated, base, spread, block):
    count, deep = activated.shape
    wide = base.shape[1]
    if not spread.aligned or count % block:
        return base + matmul(activated, spread.matrix())

    def body(inputs, matrices, results):
        results[0][...] = inputs[1][...] + matmul(inputs[0][...], matrices[0][...])

    return with_matrices(
        spread.plan,
        body,
        [spread],
        [(activated, (block, deep), by_rows), (base, (block, wide), by_rows)],
        [((count, wide), jnp.float32, (block, wide), by_rows)],
        count // block,
        2 * count * deep * wide,
    )[0]


def weight_grad(plan, left, right, rows, parts, split_columns, block):
    tokens, high = left.shape
    wide = right.shape[1]
    groups = plan.mp if split_columns else 1
    stride = wide // groups
    along = wide if split_columns else high
    unit = stride if split_columns else rows
    widths = [width for width, _, _ in parts]
    offsets = [sum(widths[:k]) for k in range(len(parts))]
    fits = along % block == 0 and (block % unit == 0 or unit % block == 0)
    if rows % 16 or any(width % 128 for width in widths) or not fits:
        whole = contract(left, right).astype(jnp.bfloat16).reshape(high, groups, stride)
        found = []
        for (width, counts, slots), offset in zip(parts, offsets):
            part = whole[:, :, offset : offset + width].reshape(high, groups * width)
            found.append(disassemble(plan, part, (rows, width), counts, slots, split_columns))
        return found
    tile = 256 if split_columns else block
    outs_of = [(width, count) for width, counts, _ in parts for count in counts]
    places = [
        (width, offset, slot)
        for (width, counts, _), offset in zip(parts, offsets)
        for count in counts
        for slot in range(count)
    ]

    def kernel(slots_ref, left_ref, right_ref, *refs):
        outs, gradient, sems = refs[: len(outs_of)], refs[len(outs_of)], refs[len(outs_of) + 1]
        step = pl.program_id(0)
        for start in range(0, high if split_columns else block, tile):
            lefts = left_ref[:, start : start + tile]
            product = rows_of_both(lefts, right_ref[...]).astype(jnp.bfloat16)
            if split_columns:
                gradient[start : start + tile, step_slice(block)] = product
            else:
                gradient[step_slice(block), :] = product
        targets = [out.at[slot] for out, (_, count) in zip(outs, outs_of) for slot in range(count)]
        copies = []
        for i, (width, offset, _) in enumerate(places):
            spot = spot_slice(
                gradient, plan, slots_ref[i], rows, width, split_columns, offset, stride
            )
            copies.append(pltpu.make_async_copy(spot, targets[i], sems.at[i]))
        for i, (width, offset, _) in enumerate(places):
            row_block, group = spot_of(slots_ref[i], plan, split_columns)
            if split_columns:
                done_in = (group * stride + offset + width - 1) // block
            else:
                done_in = (row_block * rows) // block

            @pl.when(done_in == step)
            def _(copy=copies[i]):
                copy.start()

        @pl.when(step == pl.num_programs(0) - 1)
        def _():
            for copy in copies:
                copy.wait()

    if split_columns:
        left_spec = pl.BlockSpec((tokens, high), fixed)
        right_spec = pl.BlockSpec((tokens, block), by_columns)
    else:
        left_spec = pl.BlockSpec((tokens, block), by_columns)
        right_spec = pl.BlockSpec((tokens, wide), fixed)
    flat = pl.pallas_call(
        kernel,
        out_shape=[
            jax.ShapeDtypeStruct((count, rows, width), jnp.bfloat16) for width, count in outs_of
        ],
        grid_spec=pltpu.PrefetchScalarGridSpec(
            num_scalar_prefetch=1,
            grid=(along // block,),
            in_specs=[left_spec, right_spec],
            out_specs=[ANY] * len(outs_of),
            scratch_shapes=[
                pltpu.VMEM((high, wide), jnp.bfloat16),
                pltpu.SemaphoreType.DMA((len(places),)),
            ],
        ),
        compiler_params=pltpu.CompilerParams(vmem_limit_bytes=VMEM_LIMIT),
        cost_estimate=pl.CostEstimate(
            flops=2 * tokens * high * wide,
            bytes_accessed=2 * (tokens * (high + wide) + high * wide),
            transcendentals=0,
        ),
    )(jnp.concatenate([slots for _, _, slots in parts]), left, right)
    found = []
    for _, counts, _ in parts:
        found.append(flat[: len(counts)])
        flat = flat[len(counts) :]
    return found


def adam_step(first, root, clipped, corr_first, corr_second):
    first = beta_first * first + (1.0 - beta_first) * clipped
    second = beta_second * root * root + (1.0 - beta_second) * clipped * clipped
    direction = first / corr_first / (jnp.sqrt(second / corr_second) + adam_eps)
    return first, jnp.sqrt(second), direction


def views(matrix, columns):
    width = matrix.shape[-1]
    if len(matrix.shape) == 3:
        return [((k,), 0, width) for k in range(matrix.shape[0])]
    starts = [sum(columns[:k]) for k in range(len(columns))]
    return [((), start, size) for start, size in zip(starts, columns)]


def moments_and_directions(scalars, gradients, states, masters, norms):
    count = len(masters)
    flat = [part for parts in gradients for part in parts]
    smem = pl.BlockSpec(memory_space=pltpu.SMEM)
    vmem = pl.BlockSpec(memory_space=pltpu.VMEM)

    def kernel(scalars_ref, *refs):
        parts, refs = list(refs[: len(flat)]), refs[len(flat) :]
        old, weights, refs = refs[:count], refs[count : 2 * count], refs[2 * count :]
        (norm_grad, norm_old, norm_weight), refs = refs[:3], refs[3:]
        fresh, ways, refs = refs[:count], refs[count : 2 * count], refs[2 * count :]
        norm_fresh, norm_out, squares = refs
        clip, corr_first, corr_second = scalars_ref[0], scalars_ref[1], scalars_ref[2]
        for k in range(count):
            mine = [parts.pop(0) for _ in gradients[k]]
            total = jnp.float32(0.0)
            for which, (lead, start, width) in enumerate(
                views(masters[k], [part.shape[1] for part in gradients[k]])
            ):
                columns = slice(start, start + width)
                if lead:
                    gradient = mine[0][:, which * width : (which + 1) * width]
                else:
                    gradient = mine[which][...]
                spot = lead + (slice(None), columns)
                first, root, direction = adam_step(
                    old[k][(0,) + spot],
                    old[k][(1,) + spot],
                    clip * gradient,
                    corr_first,
                    corr_second,
                )
                fresh[k][(0,) + spot] = first
                fresh[k][(1,) + spot] = root
                direction = direction + weight_decay * weights[k][spot]
                ways[k][spot] = direction
                total = total + jnp.sum(direction * direction)
            squares[k] = total
        first, root, direction = adam_step(
            norm_old[0], norm_old[1], clip * norm_grad[...], corr_first, corr_second
        )
        norm_fresh[0] = first
        norm_fresh[1] = root
        norm_out[...] = norm_weight[...] - learn_rate * direction

    like = lambda value: jax.ShapeDtypeStruct(value.shape, jnp.float32)
    found = pl.pallas_call(
        kernel,
        out_shape=[like(state) for state in states]
        + [like(master) for master in masters]
        + [like(norms[1]), like(norms[2]), jax.ShapeDtypeStruct((count,), jnp.float32)],
        in_specs=[smem] + [vmem] * (len(flat) + 2 * count + 3),
        out_specs=[vmem] * (2 * count + 2) + [smem],
        compiler_params=pltpu.CompilerParams(vmem_limit_bytes=VMEM_LIMIT),
    )(scalars, *flat, *states, *masters, *norms)
    return found[:count], found[count : 2 * count], *found[2 * count :]


def new_weights(steps, masters, directions):
    count = len(masters)
    smem = pl.BlockSpec(memory_space=pltpu.SMEM)
    vmem = pl.BlockSpec(memory_space=pltpu.VMEM)

    def kernel(steps_ref, *refs):
        weights, ways, refs = refs[:count], refs[count : 2 * count], refs[2 * count :]
        for k in range(count):
            value = weights[k][...] - steps_ref[k] * ways[k][...]
            refs[k][...] = value
            if k < count - 1:
                refs[count + k][...] = value.astype(jnp.bfloat16)

    found = pl.pallas_call(
        kernel,
        out_shape=[jax.ShapeDtypeStruct(master.shape, jnp.float32) for master in masters]
        + [jax.ShapeDtypeStruct(master.shape, jnp.bfloat16) for master in masters[:-1]],
        in_specs=[smem] + [vmem] * (2 * count),
        out_specs=[vmem] * (2 * count - 1),
        compiler_params=pltpu.CompilerParams(vmem_limit_bytes=VMEM_LIMIT),
    )(steps, *masters, *directions)
    return found[:count], found[count:]


BY_COLUMNS = ("entry", "up")


def per_device(
    plan,
    tokens,
    segment_ids,
    game_ids,
    return_bins,
    action_bins,
    reward_bins,
    valid_flags,
    step_count,
    entry_weight,
    entry_state,
    exit_weight,
    exit_state,
    up_weight,
    up_state,
    down_weight,
    down_state,
    head_weight,
    head_state,
    norm_params,
    norm_state,
):
    own_rows = tokens.shape[0]
    here = lax.axis_index("dp") * plan.mp + lax.axis_index("mp")
    row_start = lax.axis_index("mp") * own_rows
    own_seqs = own_rows // LEN
    segments = lax.dynamic_slice_in_dim(segment_ids, lax.axis_index("mp") * own_seqs, own_seqs)
    row_games = lax.dynamic_slice_in_dim(jnp.repeat(game_ids, LEN), row_start, own_rows)

    clock = Clock()
    masters = {"entry": entry_weight, "exit": exit_weight, "up": up_weight, "down": down_weight}
    rows_here, half_wide = entry_weight.shape[1:]
    halves = {name: value.astype(jnp.bfloat16) for name, value in masters.items()}
    down_half = down_weight.shape[1] // 2
    shards = {
        "entry": halves["entry"].transpose(1, 0, 2).reshape(rows_here, 3 * half_wide),
        "exit": halves["exit"],
        "up": halves["up"],
        "down_a": halves["down"][:, :down_half],
        "down_b": halves["down"][:, down_half:],
    }
    paths = {
        name: Travel("gather_" + name, gather_shards(plan, shard))
        for name, shard in shards.items()
        if name != "up"
    }
    up_gathered = lax.all_gather(shards["up"], AXES, axis=0)
    slots = jnp.asarray(path_table(plan), jnp.int32)[here]

    def chosen(names):
        return [paths[name] for name in names.split() if paths[name].wanted]

    def start(names, more=()):
        return clock.start(chosen(names), more)

    def wait(names):
        clock.wait([path for path in chosen(names) if path.going])

    def finish(name):
        while paths[name].wanted:
            start(name)
            wait(name)
        return paths[name].result

    def whole(*names):
        parts = [(finish(name), slots) for name in names]
        return Spread(plan, parts, names[0] in BY_COLUMNS)

    game_match = (row_games[:, None] == jnp.arange(GAMES)[None, :]).astype(jnp.float32)
    flag_float = valid_flags.astype(jnp.float32)
    local_counts = jnp.sum(game_match * jnp.sum(flag_float, -1, keepdims=True), 0)
    paths["games"] = Travel("game_counts", total_steps(plan, local_counts), True)

    start("games entry")
    resid, gains = clock.hold((tokens.astype(jnp.float32), norm_params))
    normed_one = layer_norm(resid, gains[0], gains[3]).astype(jnp.bfloat16)
    clock.also(normed_one)
    wait("entry games")
    start("entry exit")
    wait("entry exit")
    start("entry exit")
    wait("entry exit")
    (normed_one,) = start("entry down_a", (normed_one,))
    wait("entry")
    (normed_one,) = start("exit games", (normed_one,))
    entry_all = whole("entry")
    projected = project(normed_one, entry_all, 768)
    clock.also(projected)
    wait("down_a exit games")
    (projected,) = start("down_a down_b exit", (projected,))
    context = attend_call(
        attend_kernel, segments, projected, [], tokens.shape[1], plan.mp, 2
    )
    clock.also(context)
    wait("exit down_a down_b")
    (context,) = start("down_a down_b games", (context,))
    exit_all = whole("exit").matrix()
    after_attn = resid + matmul(context, exit_all)
    normed_two = layer_norm(after_attn, norm_params[1], norm_params[4]).astype(jnp.bfloat16)
    clock.also(normed_two)
    wait("down_a down_b games")
    start("down_a down_b games")
    up_all = Spread(plan, [([up_gathered], jnp.arange(plan.n, dtype=jnp.int32))], True)
    up_pre, activated = hidden_forward(normed_two, up_all, 512)
    wait("down_a down_b games")
    start("down_b games")
    wait("down_b games")
    counts_all = finish("games")
    inverse = 1.0 / (GAMES * jnp.maximum(counts_all, 1.0))
    token_scale = jnp.sum(game_match * inverse[None, :], -1)
    down_all = whole("down_a", "down_b")
    after_mlp = hidden_out(activated, after_attn, down_all, 320)
    final_norm = layer_norm(after_mlp, norm_params[2], norm_params[5]).astype(jnp.bfloat16)
    head_half = head_weight.astype(jnp.bfloat16)
    logits = matmul_t(final_norm, head_half)
    targets = (return_bins, action_bins, reward_bins)
    loss_local, loss_pull = jax.vjp(
        lambda values: part_loss(values, targets, valid_flags, token_scale), logits
    )
    d_logits = loss_pull(jnp.ones_like(loss_local))[0].astype(jnp.bfloat16)
    d_final = matmul(d_logits, head_half)
    d_mlp_in, d_gain_three, d_shift_three = norm_back(
        after_mlp, norm_params[2], norm_params[5], d_final
    )
    d_mlp_out = d_mlp_in.astype(jnp.bfloat16)

    def leave(name, left, right, block):
        rows, width = shards[name].shape
        (pieces,) = weight_grad(
            plan,
            left,
            right,
            rows,
            [(width, scatter_counts(plan), slots)],
            name in BY_COLUMNS,
            block,
        )
        paths[name] = Travel("scatter_" + name, scatter_shards(plan, pieces))

    def waiting(name):
        return [value for value, _ in paths[name].wanted]

    head_rows = head_weight.shape[0]
    leave("down_a", activated, d_mlp_out[:, :down_half], 1280)
    d_mlp_out, d_logits = start("down_a", (d_mlp_out, d_logits))
    wait("down_a")
    d_mlp_out, d_logits = start("down_a", (d_mlp_out, d_logits))
    leave("down_b", activated, d_mlp_out[:, down_half:], 1280)
    d_head = jnp.pad(contract(d_logits, final_norm), ((0, head_rows % 2), (0, 0)))
    paths["head"] = Travel("sum_head", total_steps(plan, d_head, halves=True), True)
    clock.also(*waiting("down_b"))
    wait("down_a")
    (d_mlp_out,) = start("down_a down_b head", (d_mlp_out,))
    d_up_pre = hidden_back(d_mlp_out, up_pre, down_all, 512)
    clock.also(d_up_pre)
    wait("down_a down_b head")
    (d_up_pre,) = start("down_a down_b head", (d_up_pre,))
    leave("up", normed_two, d_up_pre, 2560)
    clock.also(*waiting("up"))
    wait("down_a down_b head")
    (d_up_pre,) = start("down_b up head", (d_up_pre,))
    d_normed_two = project_back(d_up_pre, up_all, 256)
    clock.also(d_normed_two)
    wait("down_b up head")
    (d_normed_two,) = start("down_b up head", (d_normed_two,))
    d_ln_two, d_gain_two, d_shift_two = norm_back(
        after_attn, norm_params[1], norm_params[4], d_normed_two
    )
    d_attn_out = (d_mlp_in + d_ln_two).astype(jnp.bfloat16)
    leave("exit", context, d_attn_out, 1280)
    d_context = matmul_t(d_attn_out, exit_all).astype(jnp.bfloat16)
    clock.also(d_context, *waiting("exit"))
    wait("down_b up head")
    (d_context,) = start("up exit head", (d_context,))
    d_projected = attend_call(
        attend_back_kernel, segments, projected, [d_context], projected.shape[1], plan.mp, 5
    )
    clock.also(d_projected)
    wait("up exit head")
    (d_projected,) = start("up exit head", (d_projected,))
    leave("entry", normed_one, d_projected, 1920)
    clock.also(*waiting("entry"))
    wait("exit head")
    (d_projected,) = start("entry", (d_projected,))
    wait("entry")
    (d_projected,) = start("entry exit", (d_projected,))
    d_normed_one = project_back(d_projected, entry_all, 256)
    _, d_gain_one, d_shift_one = norm_back(resid, norm_params[0], norm_params[3], d_normed_one)
    clock.also(d_gain_one, d_shift_one)
    wait("entry exit up")
    start("entry exit")
    wait("entry exit")
    start("entry")
    wait("entry")
    reds = {name: finish(name) for name in shards}
    red_head = finish("head")[:head_rows]

    masters = [entry_weight, exit_weight, up_weight, down_weight, head_weight]
    states = [entry_state, exit_state, up_state, down_state, head_state]
    local_square = sum(jnp.sum(reds[name] * reds[name]) for name in shards)
    weight_local = jnp.stack([jnp.sum(master * master) for master in masters[:4]])
    wide = norm_params.shape[1]
    scalars = jnp.concatenate([jnp.stack([loss_local, local_square]), weight_local])
    small = total_over_devices(
        plan,
        jnp.stack(
            [
                d_gain_one,
                d_gain_two,
                d_gain_three,
                d_shift_one,
                d_shift_two,
                d_shift_three,
                jnp.pad(scalars, (0, wide - scalars.shape[0])),
            ]
        ),
    )
    red_norms = small[:6]
    loss_sum, grad_total, weight_sums = small[6, 0], small[6, 1], small[6, 2:6]
    small_square = jnp.sum(red_head * red_head) + jnp.sum(red_norms * red_norms)
    grad_norm = jnp.sqrt(grad_total + small_square)
    clip_factor = jnp.minimum(1.0, clip_limit / grad_norm)
    step_float = step_count[0].astype(jnp.float32)
    corr_first = 1.0 - jnp.power(beta_first, step_float)
    corr_second = 1.0 - jnp.power(beta_second, step_float)
    gradients = [
        [reds["entry"]],
        [reds["exit"]],
        [reds["up"]],
        [reds["down_a"], reds["down_b"]],
        [red_head],
    ]
    moments, directions, norm_moments, norm_new, squares = moments_and_directions(
        jnp.stack([clip_factor, corr_first, corr_second]),
        gradients,
        states,
        masters,
        (red_norms, norm_state, norm_params),
    )
    update_sums = total_over_devices(plan, squares[:4])
    weight_norms = jnp.sqrt(weight_sums)
    update_norms = jnp.sqrt(update_sums)
    head_wnorm = jnp.sqrt(jnp.sum(head_weight * head_weight))
    head_unorm = jnp.sqrt(squares[4])
    matrix_norms = jnp.stack(
        [
            jnp.concatenate([weight_norms, head_wnorm[None]]),
            jnp.concatenate([update_norms, head_unorm[None]]),
        ]
    )
    new, rounded = new_weights(
        learn_rate * (matrix_norms[0] / matrix_norms[1]), masters, directions
    )
    return (
        new[0],
        moments[0],
        rounded[0],
        new[1],
        moments[1],
        rounded[1],
        new[2],
        moments[2],
        rounded[2],
        new[3],
        moments[3],
        rounded[3],
        new[4],
        moments[4],
        norm_new,
        norm_moments,
        loss_sum,
        grad_norm,
        matrix_norms,
    )


def solution(mesh):
    in_specs = (
        P(("dp", "mp"), None),
        P("dp", None),
        P("dp"),
        P(("dp", "mp")),
        P(("dp", "mp")),
        P(("dp", "mp")),
        P(("dp", "mp"), None),
        P(),
        P(None, "dp", "mp"),
        P(None, None, "dp", "mp"),
        P(("mp", "dp"), None),
        P(None, ("mp", "dp"), None),
        P("dp", "mp"),
        P(None, "dp", "mp"),
        P(("mp", "dp"), None),
        P(None, ("mp", "dp"), None),
        P(),
        P(),
        P(),
        P(),
    )
    out_specs = (
        P(None, "dp", "mp"),
        P(None, None, "dp", "mp"),
        P(None, "dp", "mp"),
        P(("mp", "dp"), None),
        P(None, ("mp", "dp"), None),
        P(("mp", "dp"), None),
        P("dp", "mp"),
        P(None, "dp", "mp"),
        P("dp", "mp"),
        P(("mp", "dp"), None),
        P(None, ("mp", "dp"), None),
        P(("mp", "dp"), None),
        P(),
        P(),
        P(),
        P(),
        P(),
        P(),
        P(),
    )
    plan = Plan(mesh.shape["dp"], mesh.shape["mp"])
    return jax.shard_map(
        functools.partial(per_device, plan), mesh=mesh, in_specs=in_specs, out_specs=out_specs, check_vma=False
    )
```

```python
import functools

import jax
import jax.numpy as jnp
import numpy as np
from jax import lax
from jax.experimental import pallas as pl
from jax.experimental.pallas import tpu as pltpu
from jax.sharding import PartitionSpec as P

HD = 64
RB = 120
AB = 18
WB = 4
GAMES = 41
LEN = 160


clip_limit = 0.05
learn_rate = 0.5
beta_first = 0.5
beta_second = 0.5
weight_decay = 0.01
adam_eps = 1e-08
norm_eps = 1e-05
masked_score = -1e30


def layer_norm(rows, gain, shift):
    centred = rows - jnp.mean(rows, -1, keepdims=True)
    spread = jnp.mean(centred * centred, -1, keepdims=True)
    return centred * lax.rsqrt(spread + norm_eps) * gain + shift


def norm_back(rows, gain, shift, upstream):
    _, pullback = jax.vjp(layer_norm, rows, gain, shift)
    return pullback(upstream)


def matmul(left, right):
    return jnp.dot(left, right, preferred_element_type=jnp.float32)


def matmul_t(left, right):
    return jnp.einsum("ti,ji->tj", left, right, preferred_element_type=jnp.float32)


def contract(left, right):
    return jnp.einsum("ti,tj->ij", left, right, preferred_element_type=jnp.float32)


def part_loss(logits, targets, flags, token_scale):
    summed = jnp.zeros((), jnp.float32)
    offset = 0
    for column, span_cols in enumerate((RB, AB, WB)):
        section = logits[:, offset : offset + span_cols]
        log_probs = jax.nn.log_softmax(section, axis=-1)
        picked = (targets[column][:, None] == jnp.arange(span_cols)[None, :]).astype(jnp.float32)
        cross = -jnp.sum(log_probs * picked, -1)
        summed = summed + jnp.sum(flags[:, column].astype(jnp.float32) * token_scale * cross)
        offset = offset + span_cols
    return summed


AXES = ("dp", "mp")
VMEM_LIMIT = 60 * 2**20
ANY = pl.BlockSpec(memory_space=pl.ANY)


class Plan:
    def __init__(self, dp, mp):
        self.dp, self.mp = dp, mp
        self.core = 2 if dp % 2 == 0 else 1
        self.y = 2 if dp % (2 * self.core) == 0 else 1
        self.z = dp // (self.core * self.y)
        self.n = dp * mp
        self.grid = np.arange(self.n).reshape(self.z, self.y, self.core, mp)
        self.place = [tuple(int(v) for v in np.argwhere(self.grid == i)[0]) for i in range(self.n)]

    def pairs(self, move):
        found = []
        for i, spot in enumerate(self.place):
            target = move(*spot)
            if target is not None and 0 <= target[0] < self.z:
                found.append((i, int(self.grid[target])))
        return found

    def flip_core(self):
        return self.pairs(lambda z, y, c, x: (z, y, 1 - c, x))

    def flip_first(self):
        return self.pairs(lambda z, y, c, x: (z, 1 - y, c, x) if c == 0 else (z, y, c, 1 - x))

    def flip_second(self):
        return self.pairs(lambda z, y, c, x: (z, y, c, 1 - x) if c == 0 else (z, 1 - y, c, x))

    def flip_z(self, bits):
        return self.pairs(lambda z, y, c, x: (z ^ bits, y, c, x))

    def z_moves(self):
        return [self.flip_z(bits) for bits in range(1, self.z)]

    def z_groups(self, split):
        return split if split and self.z == 4 else (tuple(range(self.z - 1)),)


def moved(table, pairs):
    got = np.full_like(table, -1)
    for source, target in pairs:
        got[target] = table[source]
    return got


def send(value, pairs):
    return lax.ppermute(value, AXES, pairs)


def add_all(parts, dtype=jnp.bfloat16):
    total = parts[0].astype(jnp.float32)
    for part in parts[1:]:
        total = total + part.astype(jnp.float32)
    return total.astype(dtype)


class Travel:
    def __init__(self, name, steps, quiet=False):
        self.name, self.steps, self.quiet = name, steps, quiet
        self.result, self.going = None, None
        self.wanted = next(steps)


class Clock:
    def __init__(self, token):
        self.token = token

    def through(self, values):
        flat, tree = jax.tree.flatten(values)
        passed = lax.optimization_barrier(tuple(flat) + (self.token,))
        self.token = passed[-1]
        return jax.tree.unflatten(tree, passed[:-1])

    def start(self, travels, more=()):
        values, more = self.through(([[v for v, _ in travel.wanted] for travel in travels], more))
        for travel, ready in zip(travels, values):
            with jax.named_scope(travel.name):
                travel.going = [send(v, pairs) for v, (_, pairs) in zip(ready, travel.wanted)]
        return more

    def wait(self, travels, more=()):
        loud = [travel for travel in travels if not travel.quiet]
        arrived, more = self.through(([travel.going for travel in loud], more))
        for travel, got in zip(loud, arrived):
            travel.going = got
        for travel in travels:
            got, travel.going = travel.going, None
            try:
                travel.wanted = travel.steps.send(got)
            except StopIteration as end:
                travel.wanted, travel.result = None, end.value
        return more


def path_table(plan):
    first, second, core = plan.flip_first(), plan.flip_second(), plan.flip_core()
    own = np.arange(plan.n)[:, None]
    line = np.concatenate([own] + [moved(own, pairs) for pairs in plan.z_moves()], 1)
    near, side = moved(line, first), moved(line, second)
    table = np.concatenate([line, near, side, moved(near, second)], 1)
    return np.concatenate([table, moved(table, core)], 1)


def gather_shards(plan, shard, split=()):
    first, second, core = plan.flip_first(), plan.flip_second(), plan.flip_core()
    moves, got = plan.z_moves(), {}
    for group in plan.z_groups(split):
        arrived = yield [(shard[None], moves[k]) for k in group]
        got.update(zip(group, arrived))
    line = jnp.concatenate([shard[None]] + [got[k] for k in range(len(moves))])
    near, side = yield [(line, first), (line, second)]
    far, line_twin, near_twin = yield [(near, second), (line, core), (near, core)]
    side_twin, far_twin = yield [(side, core), (far, core)]
    return [line, near, side, far, line_twin, near_twin, side_twin, far_twin]


def scatter_counts(plan):
    return [4 * plan.z, 3 * plan.z, plan.z]


def scatter_shards(plan, pieces, split=()):
    first, second, core = plan.flip_first(), plan.flip_second(), plan.flip_core()
    own, rest_twin, far_twin = pieces
    size = plan.z

    def quarter(value, k):
        return value[k * size : (k + 1) * size]

    far_got, rest_got = yield [(far_twin, core), (rest_twin, core)]
    (far_got,) = yield [(add_all([quarter(own, 3), far_got]), second)]
    near = add_all([quarter(own, 1), quarter(rest_got, 1), far_got])
    side = add_all([quarter(own, 2), quarter(rest_got, 2)])
    near_got, side_got = yield [(near, first), (side, second)]
    terms = [quarter(own, 0), quarter(rest_got, 0), near_got, side_got]
    moves, arrived = plan.z_moves(), []
    for group in plan.z_groups(split):
        arrived += yield [
            (add_all([term[k + 1 : k + 2] for term in terms]), moves[k]) for k in group
        ]
    return add_all([term[:1] for term in terms] + arrived, jnp.float32)[0]


def total_steps(plan, value, halves=False):
    if halves:
        half = value.shape[0] // 2
        upper = lax.axis_index("dp") % 2 == 1
        keep = jnp.where(upper, value[half:], value[:half])
        (got,) = yield [(jnp.where(upper, value[:half], value[half:]), plan.flip_core())]
        value = keep + got
    else:
        (got,) = yield [(value, plan.flip_core())]
        value = value + got
    moves = [plan.pairs(lambda z, y, c, x: (z, y, c, 1 - x))]
    bit = 1
    while bit < plan.z:
        moves.append(plan.flip_z(bit))
        bit *= 2
    moves.append(plan.pairs(lambda z, y, c, x: (z, 1 - y, c, x)))
    for pairs in moves:
        (got,) = yield [(value, pairs)]
        value = value + got
    if halves:
        (got,) = yield [(value, plan.flip_core())]
        return jnp.where(upper, jnp.concatenate([got, value]), jnp.concatenate([value, got]))
    return value


def total_over_devices(plan, value):
    travel = Travel("small_sum", total_steps(plan, value))
    while travel.wanted:
        with jax.named_scope(travel.name):
            got = [send(v, pairs) for v, pairs in travel.wanted]
        try:
            travel.wanted = travel.steps.send(got)
        except StopIteration as end:
            travel.wanted, travel.result = None, end.value
    return travel.result


def slot_counts(pieces):
    counts = [piece.shape[0] for piece in pieces]
    return counts, [sum(counts[:i]) for i in range(len(counts))]


def spot_of(device, plan, split_columns):
    if split_columns:
        return device // plan.mp, device % plan.mp
    return (device % plan.mp) * plan.dp + device // plan.mp, 0


def assemble(plan, pieces, slots, split_columns):
    counts, offsets = slot_counts(pieces)
    total = sum(counts)
    rows, width = pieces[0].shape[1:]
    groups = plan.mp if split_columns else 1
    blocks = total // groups
    if rows % 16 and groups > 1 or width % 128:
        stacked = jnp.concatenate(pieces)
        stacked = lax.fori_loop(
            0,
            total,
            lambda i, held: lax.dynamic_update_index_in_dim(held, stacked[i], slots[i], 0),
            stacked,
        ).reshape(plan.dp, plan.mp, rows, width)
        if split_columns:
            return stacked.transpose(0, 2, 1, 3).reshape(plan.dp * rows, plan.mp * width)
        return stacked.transpose(1, 0, 2, 3).reshape(total * rows, width)
    depth = 8

    def kernel(slots_ref, *refs):
        sources, out = refs[: len(pieces)], refs[len(pieces)]
        held, in_sems, out_sems = refs[len(pieces) + 1 :]
        steps = [(a, s) for a in range(len(pieces)) for s in range(counts[a])]
        reads, writes = [], []
        for i, (a, s) in enumerate(steps):
            block, group = spot_of(slots_ref[i], plan, split_columns)
            columns = pl.ds(pl.multiple_of(group * width, 128), width)
            reads.append(pltpu.make_async_copy(sources[a].at[s], held.at[i], in_sems.at[i]))
            writes.append(
                pltpu.make_async_copy(held.at[i], out.at[block, :, columns], out_sems.at[i])
            )
        for i in range(total):
            reads[i].start()
        for i in range(total):
            reads[i].wait()
            writes[i].start()
        for i in range(total):
            writes[i].wait()

    whole = pl.pallas_call(
        kernel,
        out_shape=jax.ShapeDtypeStruct((blocks, rows, groups * width), pieces[0].dtype),
        grid_spec=pltpu.PrefetchScalarGridSpec(
            num_scalar_prefetch=1,
            grid=(1,),
            in_specs=[ANY] * len(pieces),
            out_specs=ANY,
            scratch_shapes=[
                pltpu.VMEM((total, rows, width), pieces[0].dtype),
                pltpu.SemaphoreType.DMA((total,)),
                pltpu.SemaphoreType.DMA((total,)),
            ],
        ),
        compiler_params=pltpu.CompilerParams(vmem_limit_bytes=VMEM_LIMIT),
        cost_estimate=pl.CostEstimate(
            flops=0, bytes_accessed=4 * total * rows * width, transcendentals=0
        ),
    )(slots, *pieces)
    return whole.reshape(blocks * rows, groups * width)


def disassemble(plan, whole, shard_shape, counts, slots, split_columns):
    total = sum(counts)
    rows, width = shard_shape
    groups = plan.mp if split_columns else 1
    offsets = [sum(counts[:i]) for i in range(len(counts))]
    if rows % 16 and groups > 1 or width % 128:
        if split_columns:
            shards = whole.reshape(plan.dp, rows, plan.mp, width).transpose(0, 2, 1, 3)
        else:
            shards = whole.reshape(plan.mp, plan.dp, rows, width).transpose(1, 0, 2, 3)
        source = shards.reshape(total, rows, width)
        shards = lax.fori_loop(
            0,
            total,
            lambda i, held: lax.dynamic_update_index_in_dim(held, source[slots[i]], i, 0),
            source,
        )
        return [shards[o : o + c] for o, c in zip(offsets, counts)]
    blocks = total // groups

    def kernel(slots_ref, source, *refs):
        outs = refs[: len(counts)]
        held, in_sems, out_sems = refs[len(counts) :]
        steps = [(a, s) for a in range(len(counts)) for s in range(counts[a])]
        reads, writes = [], []
        for i, (a, s) in enumerate(steps):
            block, group = spot_of(slots_ref[i], plan, split_columns)
            columns = pl.ds(pl.multiple_of(group * width, 128), width)
            reads.append(
                pltpu.make_async_copy(source.at[block, :, columns], held.at[i], in_sems.at[i])
            )
            writes.append(pltpu.make_async_copy(held.at[i], outs[a].at[s], out_sems.at[i]))
        for i in range(total):
            reads[i].start()
        for i in range(total):
            reads[i].wait()
            writes[i].start()
        for i in range(total):
            writes[i].wait()

    return pl.pallas_call(
        kernel,
        out_shape=[jax.ShapeDtypeStruct((c, rows, width), whole.dtype) for c in counts],
        grid_spec=pltpu.PrefetchScalarGridSpec(
            num_scalar_prefetch=1,
            grid=(1,),
            in_specs=[ANY],
            out_specs=[ANY] * len(counts),
            scratch_shapes=[
                pltpu.VMEM((total, rows, width), whole.dtype),
                pltpu.SemaphoreType.DMA((total,)),
                pltpu.SemaphoreType.DMA((total,)),
            ],
        ),
        compiler_params=pltpu.CompilerParams(vmem_limit_bytes=VMEM_LIMIT),
        cost_estimate=pl.CostEstimate(
            flops=0, bytes_accessed=4 * total * rows * width, transcendentals=0
        ),
    )(slots, whole.reshape(blocks, rows, groups * width))


PAIR = 2 * HD


def pair_blocks(ref, offset, group, pair, pairs):
    start = group * 3 * pairs * PAIR + pair * PAIR
    span = pairs * PAIR
    return [ref[:, start + part * span : start + part * span + PAIR] for part in range(3)]


def both_heads(block):
    low_lane = lax.broadcasted_iota(jnp.int32, block.shape, 1) < HD
    zero = jnp.zeros_like(block)
    return jnp.concatenate([jnp.where(low_lane, block, zero), jnp.where(low_lane, zero, block)])


def own_columns(stacked):
    rows = stacked.shape[0] // 2
    low_lane = lax.broadcasted_iota(jnp.int32, (rows, PAIR), 1) < HD
    return jnp.where(low_lane, stacked[:rows], stacked[rows:])


def rows_by_rows(left, right):
    return lax.dot_general(left, right, (((1,), (1,)), ((), ())), preferred_element_type=jnp.float32)


def rows_of_both(left, right):
    return lax.dot_general(left, right, (((0,), (0,)), ((), ())), preferred_element_type=jnp.float32)


def pair_probs(stacked_queries, keys, allowed):
    scores = rows_by_rows(keys, stacked_queries) * HD ** (-0.5)
    scores = jnp.where(allowed, scores, masked_score)
    raised = jnp.exp(scores - jnp.max(scores, 0, keepdims=True))
    return raised * (1.0 / jnp.sum(raised, 0, keepdims=True))


def allowed_pairs(column_ref, row_ref):
    same = column_ref[0] == row_ref[0]
    shape = same.shape
    causal = lax.broadcasted_iota(jnp.int32, shape, 0) <= (
        lax.broadcasted_iota(jnp.int32, shape, 1) % LEN
    )
    return same & causal


def attend_kernel(groups, pairs, column_ref, row_ref, qkv_ref, context_ref):
    allowed = allowed_pairs(column_ref, row_ref)
    for group in range(groups):
        for pair in range(pairs):
            queries, keys, values = pair_blocks(qkv_ref, 0, group, pair, pairs)
            probs = pair_probs(both_heads(queries), keys, allowed).astype(jnp.bfloat16)
            context = own_columns(rows_of_both(probs, values))
            start = (group * pairs + pair) * PAIR
            context_ref[:, start : start + PAIR] = context.astype(jnp.bfloat16)


def attend_back_kernel(groups, pairs, column_ref, row_ref, qkv_ref, d_context_ref, d_qkv_ref):
    allowed = allowed_pairs(column_ref, row_ref)
    span = pairs * PAIR
    for group in range(groups):
        for pair in range(pairs):
            queries, keys, values = pair_blocks(qkv_ref, 0, group, pair, pairs)
            start = (group * pairs + pair) * PAIR
            d_context = both_heads(d_context_ref[:, start : start + PAIR])
            queries = both_heads(queries)
            probs = pair_probs(queries, keys, allowed)
            d_probs = rows_by_rows(values, d_context)
            d_values = matmul(probs.astype(jnp.bfloat16), d_context)
            weighted = probs * d_probs
            mean = jnp.sum(weighted, 0, keepdims=True)
            d_scores = (weighted - probs * mean).astype(jnp.bfloat16)
            d_queries = own_columns(rows_of_both(d_scores, keys)) * HD ** (-0.5)
            d_keys = matmul(d_scores, queries) * HD ** (-0.5)
            start = group * 3 * span + pair * PAIR
            for part, value in enumerate((d_queries, d_keys, d_values)):
                at = start + part * span
                d_qkv_ref[:, at : at + PAIR] = value.astype(jnp.bfloat16)


def attend_call(kernel, segments, qkv, others, out_columns, groups, scale):
    count = segments.shape[0]
    columns = qkv.shape[1]
    pairs = columns // (3 * groups * PAIR)
    rows = lambda wide: pl.BlockSpec((LEN, wide), lambda i: (i, 0))
    return pl.pallas_call(
        functools.partial(kernel, groups, pairs),
        out_shape=jax.ShapeDtypeStruct((qkv.shape[0], out_columns), jnp.bfloat16),
        grid=(count,),
        in_specs=[
            pl.BlockSpec((1, LEN, 1), lambda i: (i, 0, 0)),
            pl.BlockSpec((1, 1, 2 * LEN), lambda i: (i, 0, 0)),
            rows(columns),
        ]
        + [rows(other.shape[1]) for other in others],
        out_specs=rows(out_columns),
        compiler_params=pltpu.CompilerParams(vmem_limit_bytes=VMEM_LIMIT),
        cost_estimate=pl.CostEstimate(
            flops=scale * count * 2 * LEN * LEN * columns // 3,
            bytes_accessed=scale * qkv.size * 2,
            transcendentals=count * LEN * LEN * columns // (3 * HD),
        ),
    )(segments[:, :, None], jnp.tile(segments, (1, 2))[:, None, :], qkv, *others)


class Spread:
    def __init__(self, plan, parts, split_columns):
        self.plan, self.parts, self.split_columns = plan, parts, split_columns
        self.pieces = [piece for pieces, _ in parts for piece in pieces]
        self.slots = jnp.concatenate([slots for _, slots in parts])
        self.rows = self.pieces[0].shape[1]
        widths = [pieces[0].shape[2] for pieces, _ in parts]
        self.offsets = [sum(widths[:k]) for k in range(len(widths))]
        self.stride = sum(widths)
        groups = plan.mp if split_columns else 1
        self.shape = (plan.n // groups * self.rows, groups * self.stride)
        self.aligned = self.rows % 16 == 0 and all(width % 128 == 0 for width in widths)

    def matrix(self):
        groups = self.plan.mp if self.split_columns else 1
        wholes = [
            assemble(self.plan, pieces, slots, self.split_columns).reshape(
                self.shape[0], groups, -1
            )
            for pieces, slots in self.parts
        ]
        return jnp.concatenate(wholes, 2).reshape(self.shape)

    def places(self):
        found, first = [], 0
        for (pieces, _), offset in zip(self.parts, self.offsets):
            for k, piece in enumerate(pieces):
                found = found + [(first + k, slot, offset) for slot in range(piece.shape[0])]
            first = first + len(pieces)
        return found


def spot_slice(matrix_ref, plan, device, rows, width, split_columns, offset, stride):
    block, group = spot_of(device, plan, split_columns)
    at_rows = pl.ds(pl.multiple_of(block * rows, rows), rows)
    start = offset if isinstance(group, int) else pl.multiple_of(group * stride + offset, 128)
    return matrix_ref.at[at_rows, pl.ds(start, width)]


def with_matrices(plan, body, spreads, operands, outs, steps, flops):
    sizes = [len(spread.pieces) for spread in spreads]
    total = sum(spread.slots.shape[0] for spread in spreads)

    def kernel(slots_ref, *refs):
        inputs, refs = refs[: len(operands)], refs[len(operands) :]
        sources, refs = refs[: sum(sizes)], refs[sum(sizes) :]
        results, refs = refs[: len(outs)], refs[len(outs) :]
        matrices, sems = refs[: len(spreads)], refs[len(spreads)]

        @pl.when(pl.program_id(0) == 0)
        def _():
            copies, first = [], 0
            for spread, matrix in zip(spreads, matrices):
                for which, slot, offset in spread.places():
                    i = len(copies)
                    spot = spot_slice(
                        matrix,
                        plan,
                        slots_ref[i],
                        spread.rows,
                        spread.pieces[which].shape[2],
                        spread.split_columns,
                        offset,
                        spread.stride,
                    )
                    source = sources[first + which].at[slot]
                    copies.append(pltpu.make_async_copy(source, spot, sems.at[i]))
                    copies[-1].start()
                first = first + len(spread.pieces)
            for copy in copies:
                copy.wait()

        body(inputs, matrices, results)

    moved_bytes = sum(2 * spread.shape[0] * spread.shape[1] for spread in spreads)
    moved_bytes += sum(array.size * array.dtype.itemsize for array, _, _ in operands)
    moved_bytes += sum(np.prod(shape) * np.dtype(dtype).itemsize for shape, dtype, _, _ in outs)
    return pl.pallas_call(
        kernel,
        out_shape=[jax.ShapeDtypeStruct(shape, dtype) for shape, dtype, _, _ in outs],
        grid_spec=pltpu.PrefetchScalarGridSpec(
            num_scalar_prefetch=1,
            grid=(steps,),
            in_specs=[pl.BlockSpec(block, index) for _, block, index in operands]
            + [ANY] * sum(sizes),
            out_specs=[pl.BlockSpec(block, index) for _, _, block, index in outs],
            scratch_shapes=[pltpu.VMEM(spread.shape, jnp.bfloat16) for spread in spreads]
            + [pltpu.SemaphoreType.DMA((total,))],
        ),
        compiler_params=pltpu.CompilerParams(vmem_limit_bytes=VMEM_LIMIT),
        cost_estimate=pl.CostEstimate(
            flops=flops, bytes_accessed=int(moved_bytes), transcendentals=0
        ),
    )(
        jnp.concatenate([spread.slots for spread in spreads]),
        *[array for array, _, _ in operands],
        *[piece for spread in spreads for piece in spread.pieces],
    )


def fixed(step, slots):
    return (0, 0)


def by_columns(step, slots):
    return (0, step)


def by_rows(step, slots):
    return (step, 0)


def step_slice(size):
    return pl.ds(pl.multiple_of(pl.program_id(0) * size, size), size)


def project(rows, spread, block):
    count, deep = rows.shape
    wide = spread.shape[1]
    if not spread.aligned or wide % block:
        return matmul(rows, spread.matrix()).astype(jnp.bfloat16)

    def body(inputs, matrices, results):
        product = matmul(inputs[0][...], matrices[0][:, step_slice(block)])
        results[0][...] = product.astype(jnp.bfloat16)

    return with_matrices(
        spread.plan,
        body,
        [spread],
        [(rows, (count, deep), fixed)],
        [((count, wide), jnp.bfloat16, (count, block), by_columns)],
        wide // block,
        2 * count * deep * wide,
    )[0]


def project_back(rows, spread, block):
    count, deep = rows.shape
    wide = spread.shape[0]
    if not spread.aligned or wide % block:
        return matmul_t(rows, spread.matrix())

    def body(inputs, matrices, results):
        results[0][...] = rows_by_rows(inputs[0][...], matrices[0][step_slice(block), :])

    return with_matrices(
        spread.plan,
        body,
        [spread],
        [(rows, (count, deep), fixed)],
        [((count, wide), jnp.float32, (count, block), by_columns)],
        wide // block,
        2 * count * deep * wide,
    )[0]


def gelu_and_slope(value):
    scale, cubic = (2.0 / np.pi) ** 0.5, 0.044715
    square = value * value
    bent = jnp.tanh(value * (scale + scale * cubic * square))
    half = 0.5 * bent + 0.5
    inner = value * (scale + 3.0 * scale * cubic * square)
    return value * half, half + (0.5 - 0.5 * bent * bent) * inner


def hidden_forward(rows, spread, block):
    count, deep = rows.shape
    wide = spread.shape[1]
    if not spread.aligned or wide % block:
        gelu, slope = gelu_and_slope(matmul(rows, spread.matrix()))
        return gelu.astype(jnp.bfloat16), slope.astype(jnp.bfloat16)

    def body(inputs, matrices, results):
        up_pre = matmul(inputs[0][...], matrices[0][:, step_slice(block)])
        gelu, slope = gelu_and_slope(up_pre)
        results[0][...] = gelu.astype(jnp.bfloat16)
        results[1][...] = slope.astype(jnp.bfloat16)

    return with_matrices(
        spread.plan,
        body,
        [spread],
        [(rows, (count, deep), fixed)],
        [((count, wide), jnp.bfloat16, (count, block), by_columns)] * 2,
        wide // block,
        2 * count * deep * wide,
    )


def hidden_back(d_out, slope, spread, block):
    count, wide = slope.shape
    if not spread.aligned or wide % block:
        d_activated = matmul_t(d_out, spread.matrix())
        return (d_activated * slope.astype(jnp.float32)).astype(jnp.bfloat16)

    def body(inputs, matrices, results):
        d_activated = rows_by_rows(inputs[0][...], matrices[0][step_slice(block), :])
        d_up = d_activated * inputs[1][...].astype(jnp.float32)
        results[0][...] = d_up.astype(jnp.bfloat16)

    return with_matrices(
        spread.plan,
        body,
        [spread],
        [(d_out, d_out.shape, fixed), (slope, (count, block), by_columns)],
        [((count, wide), jnp.bfloat16, (count, block), by_columns)],
        wide // block,
        2 * count * d_out.shape[1] * wide,
    )[0]


def hidden_out(activated, base, spread, block):
    count, deep = activated.shape
    wide = base.shape[1]
    if not spread.aligned or count % block:
        return base + matmul(activated, spread.matrix())

    def body(inputs, matrices, results):
        results[0][...] = inputs[1][...] + matmul(inputs[0][...], matrices[0][...])

    return with_matrices(
        spread.plan,
        body,
        [spread],
        [(activated, (block, deep), by_rows), (base, (block, wide), by_rows)],
        [((count, wide), jnp.float32, (block, wide), by_rows)],
        count // block,
        2 * count * deep * wide,
    )[0]


def weight_grad(plan, left, right, rows, parts, split_columns, block):
    tokens, high = left.shape
    wide = right.shape[1]
    groups = plan.mp if split_columns else 1
    stride = wide // groups
    along = wide if split_columns else high
    unit = stride if split_columns else rows
    widths = [width for width, _, _ in parts]
    offsets = [sum(widths[:k]) for k in range(len(parts))]
    fits = along % block == 0 and (block % unit == 0 or unit % block == 0)
    if rows % 16 or any(width % 128 for width in widths) or not fits:
        whole = contract(left, right).astype(jnp.bfloat16).reshape(high, groups, stride)
        found = []
        for (width, counts, slots), offset in zip(parts, offsets):
            part = whole[:, :, offset : offset + width].reshape(high, groups * width)
            found.append(disassemble(plan, part, (rows, width), counts, slots, split_columns))
        return found
    tile = 256 if split_columns else block
    outs_of = [(width, count) for width, counts, _ in parts for count in counts]
    places = [
        (width, offset, slot)
        for (width, counts, _), offset in zip(parts, offsets)
        for count in counts
        for slot in range(count)
    ]

    def kernel(slots_ref, left_ref, right_ref, *refs):
        outs, gradient, sems = refs[: len(outs_of)], refs[len(outs_of)], refs[len(outs_of) + 1]
        step = pl.program_id(0)
        for start in range(0, high if split_columns else block, tile):
            lefts = left_ref[:, start : start + tile]
            product = rows_of_both(lefts, right_ref[...]).astype(jnp.bfloat16)
            if split_columns:
                gradient[start : start + tile, step_slice(block)] = product
            else:
                gradient[step_slice(block), :] = product
        targets = [out.at[slot] for out, (_, count) in zip(outs, outs_of) for slot in range(count)]
        copies = []
        for i, (width, offset, _) in enumerate(places):
            spot = spot_slice(
                gradient, plan, slots_ref[i], rows, width, split_columns, offset, stride
            )
            copies.append(pltpu.make_async_copy(spot, targets[i], sems.at[i]))
        for i, (width, offset, _) in enumerate(places):
            row_block, group = spot_of(slots_ref[i], plan, split_columns)
            if split_columns:
                done_in = (group * stride + offset + width - 1) // block
            else:
                done_in = (row_block * rows) // block

            @pl.when(done_in == step)
            def _(copy=copies[i]):
                copy.start()

        @pl.when(step == pl.num_programs(0) - 1)
        def _():
            for copy in copies:
                copy.wait()

    if split_columns:
        left_spec = pl.BlockSpec((tokens, high), fixed)
        right_spec = pl.BlockSpec((tokens, block), by_columns)
    else:
        left_spec = pl.BlockSpec((tokens, block), by_columns)
        right_spec = pl.BlockSpec((tokens, wide), fixed)
    flat = pl.pallas_call(
        kernel,
        out_shape=[
            jax.ShapeDtypeStruct((count, rows, width), jnp.bfloat16) for width, count in outs_of
        ],
        grid_spec=pltpu.PrefetchScalarGridSpec(
            num_scalar_prefetch=1,
            grid=(along // block,),
            in_specs=[left_spec, right_spec],
            out_specs=[ANY] * len(outs_of),
            scratch_shapes=[
                pltpu.VMEM((high, wide), jnp.bfloat16),
                pltpu.SemaphoreType.DMA((len(places),)),
            ],
        ),
        compiler_params=pltpu.CompilerParams(vmem_limit_bytes=VMEM_LIMIT),
        cost_estimate=pl.CostEstimate(
            flops=2 * tokens * high * wide,
            bytes_accessed=2 * (tokens * (high + wide) + high * wide),
            transcendentals=0,
        ),
    )(jnp.concatenate([slots for _, _, slots in parts]), left, right)
    found = []
    for _, counts, _ in parts:
        found.append(flat[: len(counts)])
        flat = flat[len(counts) :]
    return found


def adam_step(first, root, clipped, corr_first, corr_second):
    first = beta_first * first + (1.0 - beta_first) * clipped
    second = beta_second * root * root + (1.0 - beta_second) * clipped * clipped
    direction = first / corr_first / (jnp.sqrt(second / corr_second) + adam_eps)
    return first, jnp.sqrt(second), direction


def views(matrix, columns):
    width = matrix.shape[-1]
    if len(matrix.shape) == 3:
        return [((k,), 0, width) for k in range(matrix.shape[0])]
    starts = [sum(columns[:k]) for k in range(len(columns))]
    return [((), start, size) for start, size in zip(starts, columns)]


def moments_and_directions(scalars, gradients, states, masters, norms):
    count = len(masters)
    flat = [part for parts in gradients for part in parts]
    smem = pl.BlockSpec(memory_space=pltpu.SMEM)
    vmem = pl.BlockSpec(memory_space=pltpu.VMEM)

    def kernel(scalars_ref, *refs):
        parts, refs = list(refs[: len(flat)]), refs[len(flat) :]
        old, weights, refs = refs[:count], refs[count : 2 * count], refs[2 * count :]
        (norm_grad, norm_old, norm_weight), refs = refs[:3], refs[3:]
        fresh, ways, refs = refs[:count], refs[count : 2 * count], refs[2 * count :]
        norm_fresh, norm_out, squares = refs
        clip, corr_first, corr_second = scalars_ref[0], scalars_ref[1], scalars_ref[2]
        for k in range(count):
            mine = [parts.pop(0) for _ in gradients[k]]
            total = jnp.float32(0.0)
            for which, (lead, start, width) in enumerate(
                views(masters[k], [part.shape[1] for part in gradients[k]])
            ):
                columns = slice(start, start + width)
                if lead:
                    gradient = mine[0][:, which * width : (which + 1) * width]
                else:
                    gradient = mine[which][...]
                spot = lead + (slice(None), columns)
                first, root, direction = adam_step(
                    old[k][(0,) + spot],
                    old[k][(1,) + spot],
                    clip * gradient,
                    corr_first,
                    corr_second,
                )
                fresh[k][(0,) + spot] = first
                fresh[k][(1,) + spot] = root
                direction = direction + weight_decay * weights[k][spot]
                ways[k][spot] = direction
                total = total + jnp.sum(direction * direction)
            squares[k] = total
        first, root, direction = adam_step(
            norm_old[0], norm_old[1], clip * norm_grad[...], corr_first, corr_second
        )
        norm_fresh[0] = first
        norm_fresh[1] = root
        norm_out[...] = norm_weight[...] - learn_rate * direction

    like = lambda value: jax.ShapeDtypeStruct(value.shape, jnp.float32)
    found = pl.pallas_call(
        kernel,
        out_shape=[like(state) for state in states]
        + [like(master) for master in masters]
        + [like(norms[1]), like(norms[2]), jax.ShapeDtypeStruct((count,), jnp.float32)],
        in_specs=[smem] + [vmem] * (len(flat) + 2 * count + 3),
        out_specs=[vmem] * (2 * count + 2) + [smem],
        compiler_params=pltpu.CompilerParams(vmem_limit_bytes=VMEM_LIMIT),
    )(scalars, *flat, *states, *masters, *norms)
    return found[:count], found[count : 2 * count], *found[2 * count :]


def new_weights(steps, masters, directions):
    count = len(masters)
    smem = pl.BlockSpec(memory_space=pltpu.SMEM)
    vmem = pl.BlockSpec(memory_space=pltpu.VMEM)

    def kernel(steps_ref, *refs):
        weights, ways, refs = refs[:count], refs[count : 2 * count], refs[2 * count :]
        for k in range(count):
            value = weights[k][...] - steps_ref[k] * ways[k][...]
            refs[k][...] = value
            if k < count - 1:
                refs[count + k][...] = value.astype(jnp.bfloat16)

    found = pl.pallas_call(
        kernel,
        out_shape=[jax.ShapeDtypeStruct(master.shape, jnp.float32) for master in masters]
        + [jax.ShapeDtypeStruct(master.shape, jnp.bfloat16) for master in masters[:-1]],
        in_specs=[smem] + [vmem] * (2 * count),
        out_specs=[vmem] * (2 * count - 1),
        compiler_params=pltpu.CompilerParams(vmem_limit_bytes=VMEM_LIMIT),
    )(steps, *masters, *directions)
    return found[:count], found[count:]


BY_COLUMNS = ("entry", "up")
SPLITS = {"up": ((0, 1), (2,)), "exit": ((0,), (1, 2))}


def per_device(
    plan,
    tokens,
    segment_ids,
    game_ids,
    return_bins,
    action_bins,
    reward_bins,
    valid_flags,
    step_count,
    entry_weight,
    entry_state,
    exit_weight,
    exit_state,
    up_weight,
    up_state,
    down_weight,
    down_state,
    head_weight,
    head_state,
    norm_params,
    norm_state,
):
    own_rows = tokens.shape[0]
    here = lax.axis_index("dp") * plan.mp + lax.axis_index("mp")
    row_start = lax.axis_index("mp") * own_rows
    own_seqs = own_rows // LEN
    segments = lax.dynamic_slice_in_dim(segment_ids, lax.axis_index("mp") * own_seqs, own_seqs)
    row_games = lax.dynamic_slice_in_dim(jnp.repeat(game_ids, LEN), row_start, own_rows)

    clock = Clock(step_count.astype(jnp.float32))
    masters = {"entry": entry_weight, "exit": exit_weight, "up": up_weight, "down": down_weight}
    rows_here, half_wide = entry_weight.shape[1:]
    halves = {name: value.astype(jnp.bfloat16) for name, value in masters.items()}
    down_half = down_weight.shape[1] // 2
    entry_shard = halves["entry"].transpose(1, 0, 2).reshape(rows_here, 3 * half_wide)
    paths = {
        name: Travel("gather_" + name, gather_shards(plan, shard, split))
        for name, shard, split in (
            ("entry", entry_shard, ()),
            ("up", halves["up"], ((0, 1), (2,))),
            ("down", halves["down"], ()),
        )
    }
    game_match = (row_games[:, None] == jnp.arange(GAMES)[None, :]).astype(jnp.float32)
    flag_float = valid_flags.astype(jnp.float32)
    local_counts = jnp.sum(game_match * jnp.sum(flag_float, -1, keepdims=True), 0)
    exit_rows, wide = exit_weight.shape
    tens = jnp.floor(local_counts / 64.0)
    pair = jnp.concatenate([tens, local_counts - 64.0 * tens]).astype(jnp.bfloat16)
    below = jnp.zeros((16 - exit_rows % 16, wide), jnp.bfloat16).at[0, : 2 * GAMES].set(pair)
    gathered = lax.all_gather(jnp.concatenate([halves["exit"], below]), ("mp", "dp"), axis=0)
    exit_all = gathered[:, :exit_rows].reshape(-1, wide)
    pairs_all = jnp.sum(gathered[:, exit_rows, : 2 * GAMES].astype(jnp.float32), 0)
    counts_all = 64.0 * pairs_all[:GAMES] + pairs_all[GAMES:]
    inverse = 1.0 / (GAMES * jnp.maximum(counts_all, 1.0))
    token_scale = jnp.sum(game_match * inverse[None, :], -1)

    slots = jnp.asarray(path_table(plan), jnp.int32)[here]

    def chosen(names):
        return [paths[name] for name in names.split() if paths[name].wanted]

    def start(names, *more):
        return clock.start(chosen(names), more)

    def wait(names, *more):
        return clock.wait([path for path in chosen(names) if path.going], more)

    def finish(name):
        while paths[name].wanted:
            start(name)
            wait(name)
        return paths[name].result

    def whole(name):
        return Spread(plan, [(finish(name), slots)], name in BY_COLUMNS)


    resid, gains = start("entry", tokens.astype(jnp.float32), norm_params)
    normed_one = layer_norm(resid, gains[0], gains[3]).astype(jnp.bfloat16)
    (normed_one,) = wait("entry", normed_one)
    start("entry up")
    wait("entry up")
    start("entry up")
    wait("entry up")
    start("entry up")
    wait("entry")
    (normed_one,) = start("down", normed_one)
    entry_all = whole("entry")
    projected = project(normed_one, entry_all, 768)
    (projected,) = wait("up down", projected)
    (projected,) = start("up", projected)
    context = attend_call(
        attend_kernel, segments, projected, [], tokens.shape[1], plan.mp, 2
    )
    after_attn = resid + matmul(context, exit_all)
    normed_two = layer_norm(after_attn, norm_params[1], norm_params[4]).astype(jnp.bfloat16)
    after_attn, normed_two = wait("up", after_attn, normed_two)
    (normed_two,) = start("up down", normed_two)
    wait("up")
    (normed_two,) = start("", normed_two)
    up_all = whole("up")
    activated, slope = hidden_forward(normed_two, up_all, 512)
    activated, slope = wait("down", activated, slope)
    start("down")
    wait("down")
    start("down")
    wait("down")
    down_all = whole("down")
    after_mlp = hidden_out(activated, after_attn, down_all, 320)
    final_norm = layer_norm(after_mlp, norm_params[2], norm_params[5]).astype(jnp.bfloat16)
    head_half = head_weight.astype(jnp.bfloat16)
    logits = matmul_t(final_norm, head_half)
    targets = (return_bins, action_bins, reward_bins)
    loss_local, loss_pull = jax.vjp(
        lambda values: part_loss(values, targets, valid_flags, token_scale), logits
    )
    d_logits = loss_pull(jnp.ones_like(loss_local))[0].astype(jnp.bfloat16)
    d_final = matmul(d_logits, head_half)
    d_mlp_in, d_gain_three, d_shift_three = norm_back(
        after_mlp, norm_params[2], norm_params[5], d_final
    )
    d_mlp_out = d_mlp_in.astype(jnp.bfloat16)

    def leave(name, left, right, block):
        rows = {"entry": rows_here, "exit": exit_weight.shape[0], "up": rows_here}
        by_columns = name in BY_COLUMNS
        width = right.shape[1] // (plan.mp if by_columns else 1)
        part = (width, scatter_counts(plan), slots)
        (pieces,) = weight_grad(
            plan,
            left,
            right,
            rows.get(name, down_weight.shape[0]),
            [part],
            by_columns,
            block,
        )
        paths[name] = Travel(
            "scatter_" + name,
            scatter_shards(plan, pieces, SPLITS.get(name, ())),
        )

    leave("down_a", activated, d_mlp_out[:, :down_half], 1280)
    d_mlp_out, d_logits = start("down_a", d_mlp_out, d_logits)
    d_mlp_out, d_logits = wait("down_a", d_mlp_out, d_logits)
    d_mlp_out, d_logits = start("down_a", d_mlp_out, d_logits)
    leave("down_b", activated, d_mlp_out[:, down_half:], 1280)
    head_rows = head_weight.shape[0]
    d_head = jnp.pad(contract(d_logits, final_norm), ((0, head_rows % 2), (0, 0)))
    d_mlp_out, d_head = wait("down_a", d_mlp_out, d_head)
    paths["head"] = Travel("sum_head", total_steps(plan, d_head, halves=True))
    d_mlp_out, *late = start("down_a down_b head", d_mlp_out, *masters.values())
    d_up_pre = hidden_back(d_mlp_out, slope, down_all, 512)
    weight_local = jnp.stack([jnp.sum(master * master) for master in late])
    d_up_pre, weight_local = wait("down_a down_b head", d_up_pre, weight_local)
    (d_up_pre,) = start("down_a down_b head", d_up_pre)
    leave("up", normed_two, d_up_pre, 2560)
    (d_up_pre,) = wait("down_a down_b head", d_up_pre)
    (d_up_pre,) = start("down_b up head", d_up_pre)
    d_normed_two = project_back(d_up_pre, up_all, 256)
    (d_normed_two,) = wait("down_b up head", d_normed_two)
    (d_normed_two,) = start("down_b up", d_normed_two)
    d_ln_two, d_gain_two, d_shift_two = norm_back(
        after_attn, norm_params[1], norm_params[4], d_normed_two
    )
    d_attn_out = (d_mlp_in + d_ln_two).astype(jnp.bfloat16)
    leave("exit", context, d_attn_out, 1280)
    d_context = matmul_t(d_attn_out, exit_all).astype(jnp.bfloat16)
    (d_context,) = wait("down_b up", d_context)
    (d_context,) = start("up exit", d_context)
    (d_context,) = wait("exit", d_context)
    (d_context,) = start("exit head", d_context)
    d_projected = attend_call(
        attend_back_kernel, segments, projected, [d_context], projected.shape[1], plan.mp, 5
    )
    (d_projected,) = wait("up exit head", d_projected)
    (d_projected,) = start("exit head", d_projected)
    leave("entry", normed_one, d_projected, 1920)
    (d_projected,) = wait("exit head", d_projected)
    (d_projected,) = start("entry", d_projected)
    (d_projected,) = wait("entry", d_projected)
    (d_projected,) = start("entry up exit", d_projected)
    d_normed_one = project_back(d_projected, entry_all, 256)
    (d_normed_one,) = wait("entry up exit", d_normed_one)
    (d_normed_one,) = start("entry up exit", d_normed_one)
    _, d_gain_one, d_shift_one = norm_back(resid, norm_params[0], norm_params[3], d_normed_one)
    d_gain_one, d_shift_one = wait("entry up exit", d_gain_one, d_shift_one)
    start("entry head")
    wait("entry head")
    red_head = finish("head")[:head_rows]
    names = ("entry", "exit", "up", "down_a", "down_b")
    reds = {name: finish(name) for name in names}

    masters = [entry_weight, exit_weight, up_weight, down_weight, head_weight]
    states = [entry_state, exit_state, up_state, down_state, head_state]
    local_square = sum(jnp.sum(reds[name] * reds[name]) for name in names)
    wide = norm_params.shape[1]
    scalars = jnp.concatenate(
        [jnp.stack([loss_local, local_square]), weight_local, clock.token]
    )
    small = total_over_devices(
        plan,
        jnp.stack(
            [
                d_gain_one,
                d_gain_two,
                d_gain_three,
                d_shift_one,
                d_shift_two,
                d_shift_three,
                jnp.pad(scalars, (0, wide - scalars.shape[0])),
            ]
        ),
    )
    red_norms = small[:6]
    loss_sum, grad_total, weight_sums = small[6, 0], small[6, 1], small[6, 2:6]
    small_square = jnp.sum(red_head * red_head) + jnp.sum(red_norms * red_norms)
    grad_norm = jnp.sqrt(grad_total + small_square)
    clip_factor = jnp.minimum(1.0, clip_limit / grad_norm)
    step_float = step_count[0].astype(jnp.float32)
    corr_first = 1.0 - jnp.power(beta_first, step_float)
    corr_second = 1.0 - jnp.power(beta_second, step_float)
    gradients = [
        [reds["entry"]],
        [reds["exit"]],
        [reds["up"]],
        [reds["down_a"], reds["down_b"]],
        [red_head],
    ]
    moments, directions, norm_moments, norm_new, squares = moments_and_directions(
        jnp.stack([clip_factor, corr_first, corr_second]),
        gradients,
        states,
        masters,
        (red_norms, norm_state, norm_params),
    )
    update_sums = total_over_devices(plan, squares[:4])
    weight_norms = jnp.sqrt(weight_sums)
    update_norms = jnp.sqrt(update_sums)
    head_wnorm = jnp.sqrt(jnp.sum(head_weight * head_weight))
    head_unorm = jnp.sqrt(squares[4])
    matrix_norms = jnp.stack(
        [
            jnp.concatenate([weight_norms, head_wnorm[None]]),
            jnp.concatenate([update_norms, head_unorm[None]]),
        ]
    )
    new, rounded = new_weights(
        learn_rate * (matrix_norms[0] / matrix_norms[1]), masters, directions
    )
    return (
        new[0],
        moments[0],
        rounded[0],
        new[1],
        moments[1],
        rounded[1],
        new[2],
        moments[2],
        rounded[2],
        new[3],
        moments[3],
        rounded[3],
        new[4],
        moments[4],
        norm_new,
        norm_moments,
        loss_sum,
        grad_norm,
        matrix_norms,
    )


def solution(mesh):
    in_specs = (
        P(("dp", "mp"), None),
        P("dp", None),
        P("dp"),
        P(("dp", "mp")),
        P(("dp", "mp")),
        P(("dp", "mp")),
        P(("dp", "mp"), None),
        P(),
        P(None, "dp", "mp"),
        P(None, None, "dp", "mp"),
        P(("mp", "dp"), None),
        P(None, ("mp", "dp"), None),
        P("dp", "mp"),
        P(None, "dp", "mp"),
        P(("mp", "dp"), None),
        P(None, ("mp", "dp"), None),
        P(),
        P(),
        P(),
        P(),
    )
    out_specs = (
        P(None, "dp", "mp"),
        P(None, None, "dp", "mp"),
        P(None, "dp", "mp"),
        P(("mp", "dp"), None),
        P(None, ("mp", "dp"), None),
        P(("mp", "dp"), None),
        P("dp", "mp"),
        P(None, "dp", "mp"),
        P("dp", "mp"),
        P(("mp", "dp"), None),
        P(None, ("mp", "dp"), None),
        P(("mp", "dp"), None),
        P(),
        P(),
        P(),
        P(),
        P(),
        P(),
        P(),
    )
    plan = Plan(mesh.shape["dp"], mesh.shape["mp"])
    return jax.shard_map(
        functools.partial(per_device, plan), mesh=mesh, in_specs=in_specs, out_specs=out_specs, check_vma=False
    )
```

```python
import functools

import jax
import jax.numpy as jnp
import numpy as np
from jax import lax
from jax.experimental import pallas as pl
from jax.experimental.pallas import tpu as pltpu
from jax.sharding import PartitionSpec as P

HD = 64
RB = 120
AB = 18
WB = 4
GAMES = 41
LEN = 160


clip_limit = 0.05
learn_rate = 0.5
beta_first = 0.5
beta_second = 0.5
weight_decay = 0.01
adam_eps = 1e-08
norm_eps = 1e-05
masked_score = -1e30


def layer_norm(rows, gain, shift):
    centred = rows - jnp.mean(rows, -1, keepdims=True)
    spread = jnp.mean(centred * centred, -1, keepdims=True)
    return centred * lax.rsqrt(spread + norm_eps) * gain + shift


def norm_back(rows, gain, shift, upstream):
    _, pullback = jax.vjp(layer_norm, rows, gain, shift)
    return pullback(upstream)


def matmul(left, right):
    return jnp.dot(left, right, preferred_element_type=jnp.float32)


def matmul_t(left, right):
    return jnp.einsum("ti,ji->tj", left, right, preferred_element_type=jnp.float32)


def contract(left, right):
    return jnp.einsum("ti,tj->ij", left, right, preferred_element_type=jnp.float32)


def part_loss(logits, targets, flags, token_scale):
    summed = jnp.zeros((), jnp.float32)
    offset = 0
    for column, span_cols in enumerate((RB, AB, WB)):
        section = logits[:, offset : offset + span_cols]
        log_probs = jax.nn.log_softmax(section, axis=-1)
        picked = (targets[column][:, None] == jnp.arange(span_cols)[None, :]).astype(jnp.float32)
        cross = -jnp.sum(log_probs * picked, -1)
        summed = summed + jnp.sum(flags[:, column].astype(jnp.float32) * token_scale * cross)
        offset = offset + span_cols
    return summed


AXES = ("dp", "mp")
VMEM_LIMIT = 60 * 2**20
ANY = pl.BlockSpec(memory_space=pl.ANY)


def room_for(*buffers):
    need = sum(int(np.prod(shape)) * size * copies for shape, size, copies in buffers)
    room = min(60 * 2**20, need + need // 8 + 8 * 2**20)
    return pltpu.CompilerParams(vmem_limit_bytes=int(room))


class Plan:
    def __init__(self, dp, mp):
        self.dp, self.mp = dp, mp
        self.core = 2 if dp % 2 == 0 else 1
        self.y = 2 if dp % (2 * self.core) == 0 else 1
        self.z = dp // (self.core * self.y)
        self.n = dp * mp
        self.grid = np.arange(self.n).reshape(self.z, self.y, self.core, mp)
        self.place = [tuple(int(v) for v in np.argwhere(self.grid == i)[0]) for i in range(self.n)]

    def pairs(self, move):
        found = []
        for i, spot in enumerate(self.place):
            target = move(*spot)
            if target is not None and 0 <= target[0] < self.z:
                found.append((i, int(self.grid[target])))
        return found

    def flip_core(self):
        return self.pairs(lambda z, y, c, x: (z, y, 1 - c, x))

    def flip_first(self):
        return self.pairs(lambda z, y, c, x: (z, 1 - y, c, x) if c == 0 else (z, y, c, 1 - x))

    def flip_second(self):
        return self.pairs(lambda z, y, c, x: (z, y, c, 1 - x) if c == 0 else (z, 1 - y, c, x))

    def flip_z(self, bits):
        return self.pairs(lambda z, y, c, x: (z ^ bits, y, c, x))

    def z_moves(self):
        return [self.flip_z(bits) for bits in range(1, self.z)]

    def z_groups(self, split):
        return split if split and self.z == 4 else (tuple(range(self.z - 1)),)


def moved(table, pairs):
    got = np.full_like(table, -1)
    for source, target in pairs:
        got[target] = table[source]
    return got


def send(value, pairs):
    return lax.ppermute(value, AXES, pairs)


def add_all(parts, dtype=jnp.bfloat16):
    total = parts[0].astype(jnp.float32)
    for part in parts[1:]:
        total = total + part.astype(jnp.float32)
    return total.astype(dtype)


class Sum:
    def __init__(self, terms, count):
        self.terms, self.count = terms, count
        self.shape = terms[0][0].shape[1:]


def make_sums(sums):
    if not sums:
        return []
    arrays = [array for job in sums for array, _ in job.terms]
    parts = [job.count // 2 if job.count % 2 == 0 else job.count for job in sums]
    in_specs, out_specs = [], []
    for job, part in zip(sums, parts):
        moves = int(part < job.count)

        def spec(offset, part=part, moves=moves, shape=job.shape):
            return pl.BlockSpec(
                (part,) + shape, lambda i, at=offset // part: (at + moves * i, 0, 0)
            )

        in_specs = in_specs + [spec(offset) for _, offset in job.terms]
        out_specs.append(spec(0))

    def kernel(*refs):
        outs, first = refs[len(arrays) :], 0
        for job, part, out in zip(sums, parts, outs):
            mine = refs[first : first + len(job.terms)]
            first = first + len(job.terms)

            def add(mine=mine, out=out):
                out[...] = add_all([ref[...] for ref in mine])

            if part < job.count:
                add()
            else:
                pl.when(pl.program_id(0) == 0)(add)

    size = sum(job.count * np.prod(job.shape) * (len(job.terms) + 1) for job in sums)
    return pl.pallas_call(
        kernel,
        out_shape=[jax.ShapeDtypeStruct((job.count,) + job.shape, jnp.bfloat16) for job in sums],
        grid=(2,),
        in_specs=in_specs,
        out_specs=out_specs,
        compiler_params=pltpu.CompilerParams(vmem_limit_bytes=VMEM_LIMIT),
        cost_estimate=pl.CostEstimate(
            flops=int(size), bytes_accessed=int(2 * size), transcendentals=0
        ),
    )(*arrays)


class Travel:
    def __init__(self, name, steps, quiet=False):
        self.name, self.steps, self.quiet = name, steps, quiet
        self.result, self.going = None, None
        self.wanted = next(steps)


class Clock:
    def __init__(self, token):
        self.token = token

    def through(self, values):
        flat, tree = jax.tree.flatten(values)
        passed = lax.optimization_barrier(tuple(flat) + (self.token,))
        self.token = passed[-1]
        return jax.tree.unflatten(tree, passed[:-1])

    def start(self, travels, more=()):
        wanted = [[v for v, _ in travel.wanted] for travel in travels]
        made = list(make_sums([v for want in wanted for v in want if isinstance(v, Sum)]))
        wanted = [[made.pop(0) if isinstance(v, Sum) else v for v in want] for want in wanted]
        values, more = self.through((wanted, more))
        for travel, ready in zip(travels, values):
            with jax.named_scope(travel.name):
                travel.going = [send(v, pairs) for v, (_, pairs) in zip(ready, travel.wanted)]
        return more

    def wait(self, travels, more=()):
        loud = [travel for travel in travels if not travel.quiet]
        arrived, more = self.through(([travel.going for travel in loud], more))
        for travel, got in zip(loud, arrived):
            travel.going = got
        for travel in travels:
            got, travel.going = travel.going, None
            try:
                travel.wanted = travel.steps.send(got)
            except StopIteration as end:
                travel.wanted, travel.result = None, end.value
        return more


def path_table(plan):
    first, second, core = plan.flip_first(), plan.flip_second(), plan.flip_core()
    own = np.arange(plan.n)[:, None]
    line = np.concatenate([own] + [moved(own, pairs) for pairs in plan.z_moves()], 1)
    near, side = moved(line, first), moved(line, second)
    table = np.concatenate([line, near, side, moved(near, second)], 1)
    return np.concatenate([table, moved(table, core)], 1)


def gather_shards(plan, shard, split=()):
    first, second, core = plan.flip_first(), plan.flip_second(), plan.flip_core()
    moves, got = plan.z_moves(), {}
    for group in plan.z_groups(split):
        arrived = yield [(shard[None], moves[k]) for k in group]
        got.update(zip(group, arrived))
    line = jnp.concatenate([shard[None]] + [got[k] for k in range(len(moves))])
    near, side = yield [(line, first), (line, second)]
    far, line_twin, near_twin = yield [(near, second), (line, core), (near, core)]
    side_twin, far_twin = yield [(side, core), (far, core)]
    return [line, near, side, far, line_twin, near_twin, side_twin, far_twin]


def scatter_counts(plan):
    return [4 * plan.z, 3 * plan.z, plan.z]


def scatter_shards(plan, pieces, split=(), apart=False):
    first, second, core = plan.flip_first(), plan.flip_second(), plan.flip_core()
    own, rest_twin, far_twin = pieces
    size = plan.z
    far_got, rest_got = yield [(far_twin, core), (rest_twin, core)]
    (far_got,) = yield [(Sum([(own, 3 * size), (far_got, 0)], size), second)]
    near_sum = Sum([(own, size), (rest_got, size), (far_got, 0)], size)
    side_sum = Sum([(own, 2 * size), (rest_got, 2 * size)], size)
    if apart:
        (near_got,) = yield [(near_sum, first)]
        (side_got,) = yield [(side_sum, second)]
    else:
        near_got, side_got = yield [(near_sum, first), (side_sum, second)]
    terms = [own, rest_got, near_got, side_got]
    moves, arrived = plan.z_moves(), []
    for group in plan.z_groups(split):
        arrived += yield [(Sum([(term, k + 1) for term in terms], 1), moves[k]) for k in group]
    return add_all([term[:1] for term in terms] + arrived, jnp.float32)[0]


def total_steps(plan, value, halves=False):
    if halves:
        half = value.shape[0] // 2
        upper = lax.axis_index("dp") % 2 == 1
        keep = jnp.where(upper, value[half:], value[:half])
        (got,) = yield [(jnp.where(upper, value[:half], value[half:]), plan.flip_core())]
        value = keep + got
    else:
        (got,) = yield [(value, plan.flip_core())]
        value = value + got
    moves, bit = [], 1
    while bit < plan.z:
        moves.append(plan.flip_z(bit))
        bit *= 2
    moves.append(plan.pairs(lambda z, y, c, x: (z, y, c, 1 - x)))
    moves.append(plan.pairs(lambda z, y, c, x: (z, 1 - y, c, x)))
    for pairs in moves:
        (got,) = yield [(value, pairs)]
        value = value + got
    if halves:
        (got,) = yield [(value, plan.flip_core())]
        return jnp.where(upper, jnp.concatenate([got, value]), jnp.concatenate([value, got]))
    return value


def total_over_devices(plan, value, more=()):
    travel, clock = Travel("small_sum", total_steps(plan, value)), None
    while travel.wanted:
        with jax.named_scope(travel.name):
            got = [send(v, pairs) for v, pairs in travel.wanted]
        if clock is None:
            clock = Clock(got[0])
            more = clock.through(more)
            got = [clock.token]
        try:
            travel.wanted = travel.steps.send(got)
        except StopIteration as end:
            travel.wanted, travel.result = None, end.value
    return travel.result, more


def slot_counts(pieces):
    counts = [piece.shape[0] for piece in pieces]
    return counts, [sum(counts[:i]) for i in range(len(counts))]


def spot_of(device, plan, split_columns):
    if split_columns:
        return device // plan.mp, device % plan.mp
    return (device % plan.mp) * plan.dp + device // plan.mp, 0


def assemble(plan, pieces, slots, split_columns):
    counts, offsets = slot_counts(pieces)
    total = sum(counts)
    rows, width = pieces[0].shape[1:]
    groups = plan.mp if split_columns else 1
    blocks = total // groups
    if rows % 16 and groups > 1 or width % 128:
        stacked = jnp.concatenate(pieces)
        stacked = lax.fori_loop(
            0,
            total,
            lambda i, held: lax.dynamic_update_index_in_dim(held, stacked[i], slots[i], 0),
            stacked,
        ).reshape(plan.dp, plan.mp, rows, width)
        if split_columns:
            return stacked.transpose(0, 2, 1, 3).reshape(plan.dp * rows, plan.mp * width)
        return stacked.transpose(1, 0, 2, 3).reshape(total * rows, width)
    depth = 8

    def kernel(slots_ref, *refs):
        sources, out = refs[: len(pieces)], refs[len(pieces)]
        held, in_sems, out_sems = refs[len(pieces) + 1 :]
        steps = [(a, s) for a in range(len(pieces)) for s in range(counts[a])]
        reads, writes = [], []
        for i, (a, s) in enumerate(steps):
            block, group = spot_of(slots_ref[i], plan, split_columns)
            columns = pl.ds(pl.multiple_of(group * width, 128), width)
            reads.append(pltpu.make_async_copy(sources[a].at[s], held.at[i], in_sems.at[i]))
            writes.append(
                pltpu.make_async_copy(held.at[i], out.at[block, :, columns], out_sems.at[i])
            )
        for i in range(total):
            reads[i].start()
        for i in range(total):
            reads[i].wait()
            writes[i].start()
        for i in range(total):
            writes[i].wait()

    whole = pl.pallas_call(
        kernel,
        out_shape=jax.ShapeDtypeStruct((blocks, rows, groups * width), pieces[0].dtype),
        grid_spec=pltpu.PrefetchScalarGridSpec(
            num_scalar_prefetch=1,
            grid=(1,),
            in_specs=[ANY] * len(pieces),
            out_specs=ANY,
            scratch_shapes=[
                pltpu.VMEM((total, rows, width), pieces[0].dtype),
                pltpu.SemaphoreType.DMA((total,)),
                pltpu.SemaphoreType.DMA((total,)),
            ],
        ),
        compiler_params=pltpu.CompilerParams(vmem_limit_bytes=VMEM_LIMIT),
        cost_estimate=pl.CostEstimate(
            flops=0, bytes_accessed=4 * total * rows * width, transcendentals=0
        ),
    )(slots, *pieces)
    return whole.reshape(blocks * rows, groups * width)


def disassemble(plan, whole, shard_shape, counts, slots, split_columns):
    total = sum(counts)
    rows, width = shard_shape
    groups = plan.mp if split_columns else 1
    offsets = [sum(counts[:i]) for i in range(len(counts))]
    if rows % 16 and groups > 1 or width % 128:
        if split_columns:
            shards = whole.reshape(plan.dp, rows, plan.mp, width).transpose(0, 2, 1, 3)
        else:
            shards = whole.reshape(plan.mp, plan.dp, rows, width).transpose(1, 0, 2, 3)
        source = shards.reshape(total, rows, width)
        shards = lax.fori_loop(
            0,
            total,
            lambda i, held: lax.dynamic_update_index_in_dim(held, source[slots[i]], i, 0),
            source,
        )
        return [shards[o : o + c] for o, c in zip(offsets, counts)]
    blocks = total // groups

    def kernel(slots_ref, source, *refs):
        outs = refs[: len(counts)]
        held, in_sems, out_sems = refs[len(counts) :]
        steps = [(a, s) for a in range(len(counts)) for s in range(counts[a])]
        reads, writes = [], []
        for i, (a, s) in enumerate(steps):
            block, group = spot_of(slots_ref[i], plan, split_columns)
            columns = pl.ds(pl.multiple_of(group * width, 128), width)
            reads.append(
                pltpu.make_async_copy(source.at[block, :, columns], held.at[i], in_sems.at[i])
            )
            writes.append(pltpu.make_async_copy(held.at[i], outs[a].at[s], out_sems.at[i]))
        for i in range(total):
            reads[i].start()
        for i in range(total):
            reads[i].wait()
            writes[i].start()
        for i in range(total):
            writes[i].wait()

    return pl.pallas_call(
        kernel,
        out_shape=[jax.ShapeDtypeStruct((c, rows, width), whole.dtype) for c in counts],
        grid_spec=pltpu.PrefetchScalarGridSpec(
            num_scalar_prefetch=1,
            grid=(1,),
            in_specs=[ANY],
            out_specs=[ANY] * len(counts),
            scratch_shapes=[
                pltpu.VMEM((total, rows, width), whole.dtype),
                pltpu.SemaphoreType.DMA((total,)),
                pltpu.SemaphoreType.DMA((total,)),
            ],
        ),
        compiler_params=pltpu.CompilerParams(vmem_limit_bytes=VMEM_LIMIT),
        cost_estimate=pl.CostEstimate(
            flops=0, bytes_accessed=4 * total * rows * width, transcendentals=0
        ),
    )(slots, whole.reshape(blocks, rows, groups * width))


PAIR = 2 * HD


def pair_blocks(ref, offset, group, pair, pairs):
    start = group * 3 * pairs * PAIR + pair * PAIR
    span = pairs * PAIR
    return [ref[:, start + part * span : start + part * span + PAIR] for part in range(3)]


def both_heads(block):
    low_lane = lax.broadcasted_iota(jnp.int32, block.shape, 1) < HD
    zero = jnp.zeros_like(block)
    return jnp.concatenate([jnp.where(low_lane, block, zero), jnp.where(low_lane, zero, block)])


def own_columns(stacked):
    rows = stacked.shape[0] // 2
    low_lane = lax.broadcasted_iota(jnp.int32, (rows, PAIR), 1) < HD
    return jnp.where(low_lane, stacked[:rows], stacked[rows:])


def rows_by_rows(left, right):
    return lax.dot_general(left, right, (((1,), (1,)), ((), ())), preferred_element_type=jnp.float32)


def rows_of_both(left, right):
    return lax.dot_general(left, right, (((0,), (0,)), ((), ())), preferred_element_type=jnp.float32)


def pair_probs(stacked_queries, keys, allowed):
    scores = rows_by_rows(keys, stacked_queries) * HD ** (-0.5)
    scores = jnp.where(allowed, scores, masked_score)
    raised = jnp.exp(scores - jnp.max(scores, 0, keepdims=True))
    return raised * (1.0 / jnp.sum(raised, 0, keepdims=True))


def allowed_pairs(column_ref, row_ref):
    same = column_ref[0] == row_ref[0]
    shape = same.shape
    causal = lax.broadcasted_iota(jnp.int32, shape, 0) <= (
        lax.broadcasted_iota(jnp.int32, shape, 1) % LEN
    )
    return same & causal


def attend_kernel(groups, pairs, column_ref, row_ref, qkv_ref, context_ref):
    allowed = allowed_pairs(column_ref, row_ref)
    for group in range(groups):
        for pair in range(pairs):
            queries, keys, values = pair_blocks(qkv_ref, 0, group, pair, pairs)
            probs = pair_probs(both_heads(queries), keys, allowed).astype(jnp.bfloat16)
            context = own_columns(rows_of_both(probs, values))
            start = (group * pairs + pair) * PAIR
            context_ref[:, start : start + PAIR] = context.astype(jnp.bfloat16)


def attend_back_kernel(groups, pairs, column_ref, row_ref, qkv_ref, d_context_ref, d_qkv_ref):
    allowed = allowed_pairs(column_ref, row_ref)
    span = pairs * PAIR
    for group in range(groups):
        for pair in range(pairs):
            queries, keys, values = pair_blocks(qkv_ref, 0, group, pair, pairs)
            start = (group * pairs + pair) * PAIR
            d_context = both_heads(d_context_ref[:, start : start + PAIR])
            queries = both_heads(queries)
            probs = pair_probs(queries, keys, allowed)
            d_probs = rows_by_rows(values, d_context)
            d_values = matmul(probs.astype(jnp.bfloat16), d_context)
            weighted = probs * d_probs
            mean = jnp.sum(weighted, 0, keepdims=True)
            d_scores = (weighted - probs * mean).astype(jnp.bfloat16)
            d_queries = own_columns(rows_of_both(d_scores, keys)) * HD ** (-0.5)
            d_keys = matmul(d_scores, queries) * HD ** (-0.5)
            start = group * 3 * span + pair * PAIR
            for part, value in enumerate((d_queries, d_keys, d_values)):
                at = start + part * span
                d_qkv_ref[:, at : at + PAIR] = value.astype(jnp.bfloat16)


def attend_call(kernel, segments, qkv, others, out_columns, groups, scale):
    count = segments.shape[0]
    columns = qkv.shape[1]
    pairs = columns // (3 * groups * PAIR)
    rows = lambda wide: pl.BlockSpec((LEN, wide), lambda i: (i, 0))
    return pl.pallas_call(
        functools.partial(kernel, groups, pairs),
        out_shape=jax.ShapeDtypeStruct((qkv.shape[0], out_columns), jnp.bfloat16),
        grid=(count,),
        in_specs=[
            pl.BlockSpec((1, LEN, 1), lambda i: (i, 0, 0)),
            pl.BlockSpec((1, 1, 2 * LEN), lambda i: (i, 0, 0)),
            rows(columns),
        ]
        + [rows(other.shape[1]) for other in others],
        out_specs=rows(out_columns),
        compiler_params=pltpu.CompilerParams(vmem_limit_bytes=VMEM_LIMIT),
        cost_estimate=pl.CostEstimate(
            flops=scale * count * 2 * LEN * LEN * columns // 3,
            bytes_accessed=scale * qkv.size * 2,
            transcendentals=count * LEN * LEN * columns // (3 * HD),
        ),
    )(segments[:, :, None], jnp.tile(segments, (1, 2))[:, None, :], qkv, *others)


class Spread:
    def __init__(self, plan, parts, split_columns):
        self.plan, self.parts, self.split_columns = plan, parts, split_columns
        self.pieces = [piece for pieces, _ in parts for piece in pieces]
        self.slots = jnp.concatenate([slots for _, slots in parts])
        self.rows = self.pieces[0].shape[1]
        widths = [pieces[0].shape[2] for pieces, _ in parts]
        self.offsets = [sum(widths[:k]) for k in range(len(widths))]
        self.stride = sum(widths)
        groups = plan.mp if split_columns else 1
        self.shape = (plan.n // groups * self.rows, groups * self.stride)
        self.aligned = self.rows % 16 == 0 and all(width % 128 == 0 for width in widths)

    def matrix(self):
        groups = self.plan.mp if self.split_columns else 1
        wholes = [
            assemble(self.plan, pieces, slots, self.split_columns).reshape(
                self.shape[0], groups, -1
            )
            for pieces, slots in self.parts
        ]
        return jnp.concatenate(wholes, 2).reshape(self.shape)

    def places(self):
        found, first = [], 0
        for (pieces, _), offset in zip(self.parts, self.offsets):
            for k, piece in enumerate(pieces):
                found = found + [(first + k, slot, offset) for slot in range(piece.shape[0])]
            first = first + len(pieces)
        return found


def spot_slice(matrix_ref, plan, device, rows, width, split_columns, offset, stride):
    block, group = spot_of(device, plan, split_columns)
    at_rows = pl.ds(pl.multiple_of(block * rows, rows), rows)
    start = offset if isinstance(group, int) else pl.multiple_of(group * stride + offset, 128)
    return matrix_ref.at[at_rows, pl.ds(start, width)]


def with_matrices(plan, body, spreads, operands, outs, steps, flops):
    sizes = [len(spread.pieces) for spread in spreads]
    total = sum(spread.slots.shape[0] for spread in spreads)

    def kernel(slots_ref, *refs):
        inputs, refs = refs[: len(operands)], refs[len(operands) :]
        sources, refs = refs[: sum(sizes)], refs[sum(sizes) :]
        results, refs = refs[: len(outs)], refs[len(outs) :]
        kept, refs = refs[: len(spreads)], refs[len(spreads) :]
        matrices, sems, kept_sems = refs[: len(spreads)], refs[len(spreads)], refs[len(spreads) + 1]
        keeps = [
            pltpu.make_async_copy(matrix, out, kept_sems.at[k])
            for k, (matrix, out) in enumerate(zip(matrices, kept))
        ]

        @pl.when(pl.program_id(0) == 0)
        def _():
            copies, first = [], 0
            for spread, matrix in zip(spreads, matrices):
                for which, slot, offset in spread.places():
                    i = len(copies)
                    spot = spot_slice(
                        matrix,
                        plan,
                        slots_ref[i],
                        spread.rows,
                        spread.pieces[which].shape[2],
                        spread.split_columns,
                        offset,
                        spread.stride,
                    )
                    source = sources[first + which].at[slot]
                    copies.append(pltpu.make_async_copy(source, spot, sems.at[i]))
                    copies[-1].start()
                first = first + len(spread.pieces)
            for copy in copies:
                copy.wait()
            for keep in keeps:
                keep.start()

        body(inputs, matrices, results)

        @pl.when(pl.program_id(0) == pl.num_programs(0) - 1)
        def _():
            for keep in keeps:
                keep.wait()

    moved_bytes = sum(2 * spread.shape[0] * spread.shape[1] for spread in spreads)
    moved_bytes += sum(array.size * array.dtype.itemsize for array, _, _ in operands)
    moved_bytes += sum(np.prod(shape) * np.dtype(dtype).itemsize for shape, dtype, _, _ in outs)
    return pl.pallas_call(
        kernel,
        out_shape=[jax.ShapeDtypeStruct(shape, dtype) for shape, dtype, _, _ in outs]
        + [jax.ShapeDtypeStruct(spread.shape, jnp.bfloat16) for spread in spreads],
        grid_spec=pltpu.PrefetchScalarGridSpec(
            num_scalar_prefetch=1,
            grid=(steps,),
            in_specs=[pl.BlockSpec(block, index) for _, block, index in operands]
            + [ANY] * sum(sizes),
            out_specs=[pl.BlockSpec(block, index) for _, _, block, index in outs]
            + [ANY] * len(spreads),
            scratch_shapes=[pltpu.VMEM(spread.shape, jnp.bfloat16) for spread in spreads]
            + [
                pltpu.SemaphoreType.DMA((total,)),
                pltpu.SemaphoreType.DMA((len(spreads),)),
            ],
        ),
        compiler_params=pltpu.CompilerParams(vmem_limit_bytes=VMEM_LIMIT),
        cost_estimate=pl.CostEstimate(
            flops=flops, bytes_accessed=int(moved_bytes), transcendentals=0
        ),
    )(
        jnp.concatenate([spread.slots for spread in spreads]),
        *[array for array, _, _ in operands],
        *[piece for spread in spreads for piece in spread.pieces],
    )


def fixed(step, *scalars):
    return (0, 0)


def by_columns(step, *scalars):
    return (0, step)


def by_rows(step, *scalars):
    return (step, 0)


def step_slice(size):
    return pl.ds(pl.multiple_of(pl.program_id(0) * size, size), size)


def project(rows, spread, block):
    count, deep = rows.shape
    wide = spread.shape[1]
    if not spread.aligned or wide % block:
        whole = spread.matrix()
        return matmul(rows, whole).astype(jnp.bfloat16), whole

    def body(inputs, matrices, results):
        product = matmul(inputs[0][...], matrices[0][:, step_slice(block)])
        results[0][...] = product.astype(jnp.bfloat16)

    return with_matrices(
        spread.plan,
        body,
        [spread],
        [(rows, (count, deep), fixed)],
        [((count, wide), jnp.bfloat16, (count, block), by_columns)],
        wide // block,
        2 * count * deep * wide,
    )


def by_blocks(body, operands, outs, steps, flops):
    moved_bytes = sum(array.size * array.dtype.itemsize for array, _, _ in operands)
    moved_bytes += sum(np.prod(shape) * np.dtype(dtype).itemsize for shape, dtype, _, _ in outs)
    return pl.pallas_call(
        body,
        out_shape=[jax.ShapeDtypeStruct(shape, dtype) for shape, dtype, _, _ in outs],
        grid=(steps,),
        in_specs=[pl.BlockSpec(block, index) for _, block, index in operands],
        out_specs=[pl.BlockSpec(block, index) for _, _, block, index in outs],
        compiler_params=pltpu.CompilerParams(vmem_limit_bytes=VMEM_LIMIT),
        cost_estimate=pl.CostEstimate(
            flops=flops, bytes_accessed=int(moved_bytes), transcendentals=0
        ),
    )(*[array for array, _, _ in operands])


def project_back(rows, matrix, block):
    count, deep = rows.shape
    wide = matrix.shape[0]
    if wide % block:
        return matmul_t(rows, matrix)

    def body(rows_ref, matrix_ref, out_ref):
        out_ref[...] = rows_by_rows(rows_ref[...], matrix_ref[...])

    return by_blocks(
        body,
        [(rows, (count, deep), fixed), (matrix, (block, deep), by_rows)],
        [((count, wide), jnp.float32, (count, block), by_columns)],
        wide // block,
        2 * count * deep * wide,
    )[0]


def gelu_and_slope(value):
    scale, cubic = (2.0 / np.pi) ** 0.5, 0.044715
    square = value * value
    bent = jnp.tanh(value * (scale + scale * cubic * square))
    half = 0.5 * bent + 0.5
    inner = value * (scale + 3.0 * scale * cubic * square)
    return value * half, half + (0.5 - 0.5 * bent * bent) * inner


def hidden_forward(rows, spread, block):
    count, deep = rows.shape
    wide = spread.shape[1]
    if not spread.aligned or wide % block:
        whole = spread.matrix()
        gelu, slope = gelu_and_slope(matmul(rows, whole))
        return gelu.astype(jnp.bfloat16), slope.astype(jnp.bfloat16), whole

    def body(inputs, matrices, results):
        up_pre = matmul(inputs[0][...], matrices[0][:, step_slice(block)])
        gelu, slope = gelu_and_slope(up_pre)
        results[0][...] = gelu.astype(jnp.bfloat16)
        results[1][...] = slope.astype(jnp.bfloat16)

    return with_matrices(
        spread.plan,
        body,
        [spread],
        [(rows, (count, deep), fixed)],
        [((count, wide), jnp.bfloat16, (count, block), by_columns)] * 2,
        wide // block,
        2 * count * deep * wide,
    )


def hidden_back(d_out, slope, matrix, block):
    count, wide = slope.shape
    if wide % block:
        d_activated = matmul_t(d_out, matrix)
        return (d_activated * slope.astype(jnp.float32)).astype(jnp.bfloat16)

    def body(d_out_ref, matrix_ref, slope_ref, out_ref):
        d_activated = rows_by_rows(d_out_ref[...], matrix_ref[...])
        out_ref[...] = (d_activated * slope_ref[...].astype(jnp.float32)).astype(jnp.bfloat16)

    return by_blocks(
        body,
        [
            (d_out, d_out.shape, fixed),
            (matrix, (block, d_out.shape[1]), by_rows),
            (slope, (count, block), by_columns),
        ],
        [((count, wide), jnp.bfloat16, (count, block), by_columns)],
        wide // block,
        2 * count * d_out.shape[1] * wide,
    )[0]


def hidden_out(activated, base, spread, block):
    count, deep = activated.shape
    wide = base.shape[1]
    if not spread.aligned or count % block:
        whole = spread.matrix()
        return base + matmul(activated, whole), whole

    def body(inputs, matrices, results):
        results[0][...] = inputs[1][...] + matmul(inputs[0][...], matrices[0][...])

    return with_matrices(
        spread.plan,
        body,
        [spread],
        [(activated, (block, deep), by_rows), (base, (block, wide), by_rows)],
        [((count, wide), jnp.float32, (block, wide), by_rows)],
        count // block,
        2 * count * deep * wide,
    )


def weight_grad(plan, left, right, rows, parts, split_columns, block):
    tokens, high = left.shape
    wide = right.shape[1]
    groups = plan.mp if split_columns else 1
    stride = wide // groups
    along = wide if split_columns else high
    unit = stride if split_columns else rows
    widths = [width for width, _, _ in parts]
    offsets = [sum(widths[:k]) for k in range(len(parts))]
    fits = along % block == 0 and (block % unit == 0 or unit % block == 0)
    if rows % 16 or any(width % 128 for width in widths) or not fits:
        whole = contract(left, right).astype(jnp.bfloat16).reshape(high, groups, stride)
        found = []
        for (width, counts, slots), offset in zip(parts, offsets):
            part = whole[:, :, offset : offset + width].reshape(high, groups * width)
            found.append(disassemble(plan, part, (rows, width), counts, slots, split_columns))
        return found
    tile = 256 if split_columns else block
    outs_of = [(width, count) for width, counts, _ in parts for count in counts]
    places = [
        (width, offset, slot)
        for (width, counts, _), offset in zip(parts, offsets)
        for count in counts
        for slot in range(count)
    ]

    def kernel(slots_ref, left_ref, right_ref, *refs):
        outs, gradient, sems = refs[: len(outs_of)], refs[len(outs_of)], refs[len(outs_of) + 1]
        step = pl.program_id(0)
        for start in range(0, high if split_columns else block, tile):
            lefts = left_ref[:, start : start + tile]
            product = rows_of_both(lefts, right_ref[...]).astype(jnp.bfloat16)
            if split_columns:
                gradient[start : start + tile, step_slice(block)] = product
            else:
                gradient[step_slice(block), :] = product
        targets = [out.at[slot] for out, (_, count) in zip(outs, outs_of) for slot in range(count)]
        copies = []
        for i, (width, offset, _) in enumerate(places):
            spot = spot_slice(
                gradient, plan, slots_ref[i], rows, width, split_columns, offset, stride
            )
            copies.append(pltpu.make_async_copy(spot, targets[i], sems.at[i]))
        for i, (width, offset, _) in enumerate(places):
            row_block, group = spot_of(slots_ref[i], plan, split_columns)
            if split_columns:
                done_in = (group * stride + offset + width - 1) // block
            else:
                done_in = (row_block * rows) // block

            @pl.when(done_in == step)
            def _(copy=copies[i]):
                copy.start()

        @pl.when(step == pl.num_programs(0) - 1)
        def _():
            for copy in copies:
                copy.wait()

    if split_columns:
        left_spec = pl.BlockSpec((tokens, high), fixed)
        right_spec = pl.BlockSpec((tokens, block), by_columns)
    else:
        left_spec = pl.BlockSpec((tokens, block), by_columns)
        right_spec = pl.BlockSpec((tokens, wide), fixed)
    flat = pl.pallas_call(
        kernel,
        out_shape=[
            jax.ShapeDtypeStruct((count, rows, width), jnp.bfloat16) for width, count in outs_of
        ],
        grid_spec=pltpu.PrefetchScalarGridSpec(
            num_scalar_prefetch=1,
            grid=(along // block,),
            in_specs=[left_spec, right_spec],
            out_specs=[ANY] * len(outs_of),
            scratch_shapes=[
                pltpu.VMEM((high, wide), jnp.bfloat16),
                pltpu.SemaphoreType.DMA((len(places),)),
            ],
        ),
        compiler_params=pltpu.CompilerParams(vmem_limit_bytes=VMEM_LIMIT),
        cost_estimate=pl.CostEstimate(
            flops=2 * tokens * high * wide,
            bytes_accessed=2 * (tokens * (high + wide) + high * wide),
            transcendentals=0,
        ),
    )(jnp.concatenate([slots for _, _, slots in parts]), left, right)
    found = []
    for _, counts, _ in parts:
        found.append(flat[: len(counts)])
        flat = flat[len(counts) :]
    return found


def adam_step(first, root, clipped, corr_first, corr_second):
    first = beta_first * first + (1.0 - beta_first) * clipped
    second = beta_second * root * root + (1.0 - beta_second) * clipped * clipped
    direction = first / corr_first / (jnp.sqrt(second / corr_second) + adam_eps)
    return first, jnp.sqrt(second), direction


def views(matrix, columns):
    width = matrix.shape[-1]
    if len(matrix.shape) == 3:
        return [((k,), 0, width) for k in range(matrix.shape[0])]
    starts = [sum(columns[:k]) for k in range(len(columns))]
    return [((), start, size) for start, size in zip(starts, columns)]


def moments_and_directions(scalars, gradients, states, masters, norms):
    count = len(masters)
    flat = [part for parts in gradients for part in parts]
    smem = pl.BlockSpec(memory_space=pltpu.SMEM)
    vmem = pl.BlockSpec(memory_space=pltpu.VMEM)

    def kernel(scalars_ref, *refs):
        parts, refs = list(refs[: len(flat)]), refs[len(flat) :]
        old, weights, refs = refs[:count], refs[count : 2 * count], refs[2 * count :]
        (norm_grad, norm_old, norm_weight), refs = refs[:3], refs[3:]
        fresh, ways, refs = refs[:count], refs[count : 2 * count], refs[2 * count :]
        norm_fresh, norm_out, squares = refs
        clip, corr_first, corr_second = scalars_ref[0], scalars_ref[1], scalars_ref[2]
        for k in range(count):
            mine = [parts.pop(0) for _ in gradients[k]]
            total = jnp.float32(0.0)
            for which, (lead, start, width) in enumerate(
                views(masters[k], [part.shape[1] for part in gradients[k]])
            ):
                columns = slice(start, start + width)
                if lead:
                    gradient = mine[0][:, which * width : (which + 1) * width]
                else:
                    gradient = mine[which][...]
                spot = lead + (slice(None), columns)
                first, root, direction = adam_step(
                    old[k][(0,) + spot],
                    old[k][(1,) + spot],
                    clip * gradient,
                    corr_first,
                    corr_second,
                )
                fresh[k][(0,) + spot] = first
                fresh[k][(1,) + spot] = root
                direction = direction + weight_decay * weights[k][spot]
                ways[k][spot] = direction
                total = total + jnp.sum(direction * direction)
            squares[k] = total
        first, root, direction = adam_step(
            norm_old[0], norm_old[1], clip * norm_grad[...], corr_first, corr_second
        )
        norm_fresh[0] = first
        norm_fresh[1] = root
        norm_out[...] = norm_weight[...] - learn_rate * direction

    like = lambda value: jax.ShapeDtypeStruct(value.shape, jnp.float32)
    found = pl.pallas_call(
        kernel,
        out_shape=[like(state) for state in states]
        + [like(master) for master in masters]
        + [like(norms[1]), like(norms[2]), jax.ShapeDtypeStruct((count,), jnp.float32)],
        in_specs=[smem] + [vmem] * (len(flat) + 2 * count + 3),
        out_specs=[vmem] * (2 * count + 2) + [smem],
        compiler_params=pltpu.CompilerParams(vmem_limit_bytes=VMEM_LIMIT),
    )(scalars, *flat, *states, *masters, *norms)
    return list(found[:count]), found[count : 2 * count], *found[2 * count :]


def new_weights(steps, masters, directions):
    count = len(masters)
    smem = pl.BlockSpec(memory_space=pltpu.SMEM)
    vmem = pl.BlockSpec(memory_space=pltpu.VMEM)

    def kernel(steps_ref, *refs):
        weights, ways, refs = refs[:count], refs[count : 2 * count], refs[2 * count :]
        for k in range(count):
            value = weights[k][...] - steps_ref[k] * ways[k][...]
            refs[k][...] = value
            if k < count - 1:
                refs[count + k][...] = value.astype(jnp.bfloat16)

    found = pl.pallas_call(
        kernel,
        out_shape=[jax.ShapeDtypeStruct(master.shape, jnp.float32) for master in masters]
        + [jax.ShapeDtypeStruct(master.shape, jnp.bfloat16) for master in masters[:-1]],
        in_specs=[smem] + [vmem] * (2 * count),
        out_specs=[vmem] * (2 * count - 1),
        compiler_params=room_for(*[(master.shape, 4, 4) for master in masters]),
    )(steps, *masters, *directions)
    return found[:count], found[count:]


BY_COLUMNS = ("entry", "up")
SPLITS = {"up": ((0, 1), (2,)), "down": ((0, 1), (2,))}


def per_device(
    plan,
    tokens,
    segment_ids,
    game_ids,
    return_bins,
    action_bins,
    reward_bins,
    valid_flags,
    step_count,
    entry_weight,
    entry_state,
    exit_weight,
    exit_state,
    up_weight,
    up_state,
    down_weight,
    down_state,
    head_weight,
    head_state,
    norm_params,
    norm_state,
):
    own_rows = tokens.shape[0]
    here = lax.axis_index("dp") * plan.mp + lax.axis_index("mp")
    row_start = lax.axis_index("mp") * own_rows
    own_seqs = own_rows // LEN
    segments = lax.dynamic_slice_in_dim(segment_ids, lax.axis_index("mp") * own_seqs, own_seqs)
    row_games = lax.dynamic_slice_in_dim(jnp.repeat(game_ids, LEN), row_start, own_rows)

    clock = Clock(step_count.astype(jnp.float32))
    masters = {"entry": entry_weight, "exit": exit_weight, "up": up_weight, "down": down_weight}
    rows_here, half_wide = entry_weight.shape[1:]
    halves = {name: value.astype(jnp.bfloat16) for name, value in masters.items()}
    entry_shard = halves["entry"].transpose(1, 0, 2).reshape(rows_here, 3 * half_wide)
    paths = {
        name: Travel("gather_" + name, gather_shards(plan, shard, split))
        for name, shard, split in (
            ("entry", entry_shard, ()),
            ("up", halves["up"], ((0, 1), (2,))),
            ("down", halves["down"], ()),
        )
    }
    game_match = (row_games[:, None] == jnp.arange(GAMES)[None, :]).astype(jnp.float32)
    flag_float = valid_flags.astype(jnp.float32)
    local_counts = jnp.sum(game_match * jnp.sum(flag_float, -1, keepdims=True), 0)
    exit_rows, wide = exit_weight.shape
    tens = jnp.floor(local_counts / 64.0)
    pair = jnp.concatenate([tens, local_counts - 64.0 * tens]).astype(jnp.bfloat16)
    below = jnp.zeros((16 - exit_rows % 16, wide), jnp.bfloat16).at[0, : 2 * GAMES].set(pair)
    gathered = lax.all_gather(jnp.concatenate([halves["exit"], below]), ("mp", "dp"), axis=0)
    exit_all = gathered[:, :exit_rows].reshape(-1, wide)
    pairs_all = jnp.sum(gathered[:, exit_rows, : 2 * GAMES].astype(jnp.float32), 0)
    counts_all = 64.0 * pairs_all[:GAMES] + pairs_all[GAMES:]
    inverse = 1.0 / (GAMES * jnp.maximum(counts_all, 1.0))
    token_scale = jnp.sum(game_match * inverse[None, :], -1)

    slots = jnp.asarray(path_table(plan), jnp.int32)[here]

    def chosen(names):
        return [paths[name] for name in names.split() if paths[name].wanted]

    def start(names, *more):
        return clock.start(chosen(names), more)

    def wait(names, *more):
        return clock.wait([path for path in chosen(names) if path.going], more)

    def finish(name):
        while paths[name].wanted:
            start(name)
            wait(name)
        return paths[name].result

    def whole(name):
        return Spread(plan, [(finish(name), slots)], name in BY_COLUMNS)


    resid, gains = start("entry", tokens.astype(jnp.float32), norm_params)
    normed_one = layer_norm(resid, gains[0], gains[3]).astype(jnp.bfloat16)
    (normed_one,) = wait("entry", normed_one)
    start("entry up")
    wait("entry up")
    start("entry up")
    wait("entry up")
    start("entry up")
    wait("entry")
    (normed_one,) = start("down", normed_one)
    projected, entry_all = project(normed_one, whole("entry"), 768)
    (projected,) = wait("up down", projected)
    (projected,) = start("up", projected)
    context = attend_call(
        attend_kernel, segments, projected, [], tokens.shape[1], plan.mp, 2
    )
    after_attn = resid + matmul(context, exit_all)
    normed_two = layer_norm(after_attn, norm_params[1], norm_params[4]).astype(jnp.bfloat16)
    after_attn, normed_two = wait("up", after_attn, normed_two)
    (normed_two,) = start("up down", normed_two)
    wait("up")
    (normed_two,) = start("", normed_two)
    activated, slope, up_all = hidden_forward(normed_two, whole("up"), 512)
    activated, slope = wait("down", activated, slope)
    late = start("down", *masters.values())
    weight_local = jnp.stack([jnp.sum(master * master) for master in late])
    (weight_local,) = wait("down", weight_local)
    start("down")
    wait("down")
    after_mlp, down_all = hidden_out(activated, after_attn, whole("down"), 320)
    final_norm = layer_norm(after_mlp, norm_params[2], norm_params[5]).astype(jnp.bfloat16)
    head_half = head_weight.astype(jnp.bfloat16)
    logits = matmul_t(final_norm, head_half)
    targets = (return_bins, action_bins, reward_bins)
    loss_local, loss_pull = jax.vjp(
        lambda values: part_loss(values, targets, valid_flags, token_scale), logits
    )
    d_logits = loss_pull(jnp.ones_like(loss_local))[0].astype(jnp.bfloat16)
    d_final = matmul(d_logits, head_half)
    d_mlp_in, _, _ = norm_back(after_mlp, norm_params[2], norm_params[5], d_final)
    d_mlp_out = d_mlp_in.astype(jnp.bfloat16)

    def leave(names, left, right, rows, widths, block):
        by_columns = names.split()[0] in ("entry_a", "up")
        parts = [(width, scatter_counts(plan), slots) for width in widths]
        found = weight_grad(plan, left, right, rows, parts, by_columns, block)
        for name, pieces in zip(names.split(), found):
            steps = scatter_shards(plan, pieces, SPLITS.get(name, ()), name == "up")
            paths[name] = Travel("scatter_" + name, steps)

    down_rows = down_weight.shape[0]
    entry_widths = (3 * half_wide * 8 // 15, 3 * half_wide - 3 * half_wide * 8 // 15)
    leave("down", activated, d_mlp_out, down_rows, [wide], 1280)
    head_rows = head_weight.shape[0]
    d_head = jnp.pad(contract(d_logits, final_norm), ((0, head_rows % 2), (0, 0)))
    paths["head"] = Travel("sum_head", total_steps(plan, d_head, halves=True))
    (d_mlp_out,) = start("down head", d_mlp_out)
    d_up_pre = hidden_back(d_mlp_out, slope, down_all, 512)
    (d_up_pre,) = wait("down head", d_up_pre)
    (d_up_pre,) = start("down head", d_up_pre)
    leave("up", normed_two, d_up_pre, rows_here, [up_weight.shape[1]], 2560)
    (d_up_pre,) = wait("down head", d_up_pre)
    (d_up_pre,) = start("down up head", d_up_pre)
    d_normed_two = project_back(d_up_pre, up_all, 256)
    d_ln_two, _, _ = norm_back(after_attn, norm_params[1], norm_params[4], d_normed_two)
    d_attn_out = (d_mlp_in + d_ln_two).astype(jnp.bfloat16)
    leave("exit", context, d_attn_out, exit_rows, [wide], 1280)
    d_context = matmul_t(d_attn_out, exit_all).astype(jnp.bfloat16)
    (d_context,) = wait("down up head", d_context)
    (d_context,) = start("down up exit", d_context)
    d_projected = attend_call(
        attend_back_kernel, segments, projected, [d_context], projected.shape[1], plan.mp, 5
    )
    (d_projected,) = wait("down up exit", d_projected)
    (d_projected,) = start("up down exit", d_projected)
    leave("entry_a entry_b", normed_one, d_projected, rows_here, entry_widths, 1920)
    (d_projected,) = wait("up down exit", d_projected)
    (d_projected,) = start("up entry_a entry_b", d_projected)
    d_normed_one = project_back(d_projected, entry_all, 256)
    reds = {"down": finish("down")}
    (d_normed_one,) = wait("up entry_a entry_b", d_normed_one)
    d_normed_one, reds = start("entry_a entry_b up head", d_normed_one, reds)
    down_square = jnp.sum(reds["down"] * reds["down"])
    _, d_gain_one, d_shift_one = norm_back(resid, norm_params[0], norm_params[3], d_normed_one)
    d_gain_one, d_shift_one, reds, down_square = wait(
        "entry_a entry_b up head", d_gain_one, d_shift_one, reds, down_square
    )
    late = start("entry_a up exit", after_mlp, d_final, after_attn, d_normed_two)
    _, d_gain_three, d_shift_three = norm_back(late[0], norm_params[2], norm_params[5], late[1])
    _, d_gain_two, d_shift_two = norm_back(late[2], norm_params[1], norm_params[4], late[3])
    late = wait("entry_a up exit", d_gain_two, d_shift_two, d_gain_three, d_shift_three)
    d_gain_two, d_shift_two, d_gain_three, d_shift_three = late
    start("entry_b entry_a head")
    reds["up"] = finish("up")
    up_square = jnp.sum(reds["up"] * reds["up"])
    reds, up_square = wait("entry_b entry_a head", reds, up_square)
    start("entry_b exit head")
    wait("entry_b exit head")
    reds["exit"] = finish("exit")
    exit_square = jnp.sum(reds["exit"] * reds["exit"])
    red_head = finish("head")[:head_rows]
    reds["entry_a"], reds["entry_b"] = finish("entry_a"), finish("entry_b")
    local_square = down_square + up_square + exit_square
    for name in ("entry_a", "entry_b"):
        local_square = local_square + jnp.sum(reds[name] * reds[name])
    masters = [entry_weight, exit_weight, up_weight, down_weight, head_weight]
    states = [entry_state, exit_state, up_state, down_state, head_state]
    wide = norm_params.shape[1]
    scalars = jnp.concatenate(
        [jnp.stack([loss_local, local_square]), weight_local, clock.token]
    )
    small, _ = total_over_devices(
        plan,
        jnp.stack(
            [
                d_gain_one,
                d_gain_two,
                d_gain_three,
                d_shift_one,
                d_shift_two,
                d_shift_three,
                jnp.pad(scalars, (0, wide - scalars.shape[0])),
            ]
        ),
    )
    red_norms = small[:6]
    loss_sum, grad_total, weight_sums = small[6, 0], small[6, 1], small[6, 2:6]
    small_square = jnp.sum(red_head * red_head) + jnp.sum(red_norms * red_norms)
    grad_norm = jnp.sqrt(grad_total + small_square)
    clip_factor = jnp.minimum(1.0, clip_limit / grad_norm)
    step_float = step_count[0].astype(jnp.float32)
    corr_first = 1.0 - jnp.power(beta_first, step_float)
    corr_second = 1.0 - jnp.power(beta_second, step_float)
    gradients = [
        [jnp.concatenate([reds["entry_a"], reds["entry_b"]], 1)],
        [reds["exit"]],
        [reds["up"]],
        [reds["down"]],
        [red_head],
    ]
    moments, directions, norm_moments, norm_new, squares = moments_and_directions(
        jnp.stack([clip_factor, corr_first, corr_second]),
        gradients,
        states,
        masters,
        (red_norms, norm_state, norm_params),
    )
    update_sums, late = total_over_devices(plan, squares[:4], (moments[4], norm_moments))
    moments[4], norm_moments = late
    weight_norms = jnp.sqrt(weight_sums)
    update_norms = jnp.sqrt(update_sums)
    head_wnorm = jnp.sqrt(jnp.sum(head_weight * head_weight))
    head_unorm = jnp.sqrt(squares[4])
    matrix_norms = jnp.stack(
        [
            jnp.concatenate([weight_norms, head_wnorm[None]]),
            jnp.concatenate([update_norms, head_unorm[None]]),
        ]
    )
    new, rounded = new_weights(
        learn_rate * (matrix_norms[0] / matrix_norms[1]), masters, directions
    )
    return (
        new[0],
        moments[0],
        rounded[0],
        new[1],
        moments[1],
        rounded[1],
        new[2],
        moments[2],
        rounded[2],
        new[3],
        moments[3],
        rounded[3],
        new[4],
        moments[4],
        norm_new,
        norm_moments,
        loss_sum,
        grad_norm,
        matrix_norms,
    )


def solution(mesh):
    in_specs = (
        P(("dp", "mp"), None),
        P("dp", None),
        P("dp"),
        P(("dp", "mp")),
        P(("dp", "mp")),
        P(("dp", "mp")),
        P(("dp", "mp"), None),
        P(),
        P(None, "dp", "mp"),
        P(None, None, "dp", "mp"),
        P(("mp", "dp"), None),
        P(None, ("mp", "dp"), None),
        P("dp", "mp"),
        P(None, "dp", "mp"),
        P(("mp", "dp"), None),
        P(None, ("mp", "dp"), None),
        P(),
        P(),
        P(),
        P(),
    )
    out_specs = (
        P(None, "dp", "mp"),
        P(None, None, "dp", "mp"),
        P(None, "dp", "mp"),
        P(("mp", "dp"), None),
        P(None, ("mp", "dp"), None),
        P(("mp", "dp"), None),
        P("dp", "mp"),
        P(None, "dp", "mp"),
        P("dp", "mp"),
        P(("mp", "dp"), None),
        P(None, ("mp", "dp"), None),
        P(("mp", "dp"), None),
        P(),
        P(),
        P(),
        P(),
        P(),
        P(),
        P(),
    )
    plan = Plan(mesh.shape["dp"], mesh.shape["mp"])
    return jax.shard_map(
        functools.partial(per_device, plan), mesh=mesh, in_specs=in_specs, out_specs=out_specs, check_vma=False
    )
```

```python
import functools

import jax
import jax.numpy as jnp
import numpy as np
from jax import lax
from jax.experimental import pallas as pl
from jax.experimental.pallas import tpu as pltpu
from jax.sharding import PartitionSpec as P

HD = 64
RB = 120
AB = 18
WB = 4
GAMES = 41
LEN = 160


clip_limit = 0.05
learn_rate = 0.5
beta_first = 0.5
beta_second = 0.5
weight_decay = 0.01
adam_eps = 1e-08
norm_eps = 1e-05
masked_score = -1e30


def layer_norm(rows, gain, shift):
    centred = rows - jnp.mean(rows, -1, keepdims=True)
    spread = jnp.mean(centred * centred, -1, keepdims=True)
    return centred * lax.rsqrt(spread + norm_eps) * gain + shift


def norm_back(rows, gain, shift, upstream):
    _, pullback = jax.vjp(layer_norm, rows, gain, shift)
    return pullback(upstream)


def matmul(left, right):
    return jnp.dot(left, right, preferred_element_type=jnp.float32)


def matmul_t(left, right):
    return jnp.einsum("ti,ji->tj", left, right, preferred_element_type=jnp.float32)


def contract(left, right):
    return jnp.einsum("ti,tj->ij", left, right, preferred_element_type=jnp.float32)


AXES = ("dp", "mp")
VMEM_LIMIT = 60 * 2**20
ANY = pl.BlockSpec(memory_space=pl.ANY)


def room_for(*buffers):
    need = sum(int(np.prod(shape)) * size * copies for shape, size, copies in buffers)
    room = min(60 * 2**20, need + need // 8 + 8 * 2**20)
    return pltpu.CompilerParams(vmem_limit_bytes=int(room))


class Plan:
    def __init__(self, dp, mp):
        self.dp, self.mp = dp, mp
        self.core = 2 if dp % 2 == 0 else 1
        self.y = 2 if dp % (2 * self.core) == 0 else 1
        self.z = dp // (self.core * self.y)
        self.n = dp * mp
        self.grid = np.arange(self.n).reshape(self.z, self.y, self.core, mp)
        self.place = [tuple(int(v) for v in np.argwhere(self.grid == i)[0]) for i in range(self.n)]

    def pairs(self, move):
        found = []
        for i, spot in enumerate(self.place):
            target = move(*spot)
            if target is not None and 0 <= target[0] < self.z:
                found.append((i, int(self.grid[target])))
        return found

    def flip_core(self):
        return self.pairs(lambda z, y, c, x: (z, y, 1 - c, x))

    def flip_first(self):
        return self.pairs(lambda z, y, c, x: (z, 1 - y, c, x) if c == 0 else (z, y, c, 1 - x))

    def flip_second(self):
        return self.pairs(lambda z, y, c, x: (z, y, c, 1 - x) if c == 0 else (z, 1 - y, c, x))

    def flip_z(self, bits):
        return self.pairs(lambda z, y, c, x: (z ^ bits, y, c, x))

    def z_moves(self):
        return [self.flip_z(bits) for bits in range(1, self.z)]

    def z_groups(self, split):
        return split if split and self.z == 4 else (tuple(range(self.z - 1)),)


def moved(table, pairs):
    got = np.full_like(table, -1)
    for source, target in pairs:
        got[target] = table[source]
    return got


def send(value, pairs):
    return lax.ppermute(value, AXES, pairs)


def add_all(parts, dtype=jnp.bfloat16):
    total = parts[0].astype(jnp.float32)
    for part in parts[1:]:
        total = total + part.astype(jnp.float32)
    return total.astype(dtype)


class Sum:
    def __init__(self, terms, count):
        self.terms, self.count = terms, count
        self.shape = terms[0][0].shape[1:]


def make_sums(sums):
    if not sums:
        return []
    arrays = [array for job in sums for array, _ in job.terms]
    parts = [job.count // 2 if job.count % 2 == 0 else job.count for job in sums]
    in_specs, out_specs = [], []
    for job, part in zip(sums, parts):
        moves = int(part < job.count)

        def spec(offset, part=part, moves=moves, shape=job.shape):
            return pl.BlockSpec(
                (part,) + shape, lambda i, at=offset // part: (at + moves * i, 0, 0)
            )

        in_specs = in_specs + [spec(offset) for _, offset in job.terms]
        out_specs.append(spec(0))

    def kernel(*refs):
        outs, first = refs[len(arrays) :], 0
        for job, part, out in zip(sums, parts, outs):
            mine = refs[first : first + len(job.terms)]
            first = first + len(job.terms)

            def add(mine=mine, out=out):
                out[...] = add_all([ref[...] for ref in mine])

            if part < job.count:
                add()
            else:
                pl.when(pl.program_id(0) == 0)(add)

    size = sum(job.count * np.prod(job.shape) * (len(job.terms) + 1) for job in sums)
    return pl.pallas_call(
        kernel,
        out_shape=[jax.ShapeDtypeStruct((job.count,) + job.shape, jnp.bfloat16) for job in sums],
        grid=(2,),
        in_specs=in_specs,
        out_specs=out_specs,
        compiler_params=pltpu.CompilerParams(vmem_limit_bytes=VMEM_LIMIT),
        cost_estimate=pl.CostEstimate(
            flops=int(size), bytes_accessed=int(2 * size), transcendentals=0
        ),
    )(*arrays)


class Travel:
    def __init__(self, name, steps, quiet=False):
        self.name, self.steps, self.quiet = name, steps, quiet
        self.result, self.going = None, None
        self.wanted = next(steps)


class Clock:
    def __init__(self, token):
        self.token = token

    def through(self, values):
        flat, tree = jax.tree.flatten(values)
        passed = lax.optimization_barrier(tuple(flat) + (self.token,))
        self.token = passed[-1]
        return jax.tree.unflatten(tree, passed[:-1])

    def start(self, travels, more=()):
        wanted = [[v for v, _ in travel.wanted] for travel in travels]
        made = list(make_sums([v for want in wanted for v in want if isinstance(v, Sum)]))
        wanted = [[made.pop(0) if isinstance(v, Sum) else v for v in want] for want in wanted]
        values, more = self.through((wanted, more))
        for travel, ready in zip(travels, values):
            with jax.named_scope(travel.name):
                travel.going = [send(v, pairs) for v, (_, pairs) in zip(ready, travel.wanted)]
        return more

    def wait(self, travels, more=()):
        loud = [travel for travel in travels if not travel.quiet]
        arrived, more = self.through(([travel.going for travel in loud], more))
        for travel, got in zip(loud, arrived):
            travel.going = got
        for travel in travels:
            got, travel.going = travel.going, None
            try:
                travel.wanted = travel.steps.send(got)
            except StopIteration as end:
                travel.wanted, travel.result = None, end.value
        return more


def path_table(plan):
    first, second, core = plan.flip_first(), plan.flip_second(), plan.flip_core()
    own = np.arange(plan.n)[:, None]
    line = np.concatenate([own] + [moved(own, pairs) for pairs in plan.z_moves()], 1)
    near, side = moved(line, first), moved(line, second)
    table = np.concatenate([line, near, side, moved(near, second)], 1)
    return np.concatenate([table, moved(table, core)], 1)


def gather_shards(plan, shard, split=()):
    first, second, core = plan.flip_first(), plan.flip_second(), plan.flip_core()
    moves, got = plan.z_moves(), {}
    for group in plan.z_groups(split):
        arrived = yield [(shard[None], moves[k]) for k in group]
        got.update(zip(group, arrived))
    line = jnp.concatenate([shard[None]] + [got[k] for k in range(len(moves))])
    near, side = yield [(line, first), (line, second)]
    far, line_twin, near_twin = yield [(near, second), (line, core), (near, core)]
    side_twin, far_twin = yield [(side, core), (far, core)]
    return [line, near, side, far, line_twin, near_twin, side_twin, far_twin]


def scatter_counts(plan):
    return [4 * plan.z, 3 * plan.z, plan.z]


def scatter_shards(plan, pieces, split=(), apart=False):
    first, second, core = plan.flip_first(), plan.flip_second(), plan.flip_core()
    own, rest_twin, far_twin = pieces
    size = plan.z
    far_got, rest_got = yield [(far_twin, core), (rest_twin, core)]
    (far_got,) = yield [(Sum([(own, 3 * size), (far_got, 0)], size), second)]
    near_sum = Sum([(own, size), (rest_got, size), (far_got, 0)], size)
    side_sum = Sum([(own, 2 * size), (rest_got, 2 * size)], size)
    if apart:
        (near_got,) = yield [(near_sum, first)]
        (side_got,) = yield [(side_sum, second)]
    else:
        near_got, side_got = yield [(near_sum, first), (side_sum, second)]
    terms = [own, rest_got, near_got, side_got]
    moves, arrived = plan.z_moves(), []
    for group in plan.z_groups(split):
        arrived += yield [(Sum([(term, k + 1) for term in terms], 1), moves[k]) for k in group]
    return add_all([term[:1] for term in terms] + arrived, jnp.float32)[0]


def total_steps(plan, value, halves=False):
    if halves:
        half = value.shape[0] // 2
        upper = lax.axis_index("dp") % 2 == 1
        keep = jnp.where(upper, value[half:], value[:half])
        (got,) = yield [(jnp.where(upper, value[:half], value[half:]), plan.flip_core())]
        value = keep + got
    else:
        (got,) = yield [(value, plan.flip_core())]
        value = value + got
    moves, bit = [], 1
    while bit < plan.z:
        moves.append(plan.flip_z(bit))
        bit *= 2
    moves.append(plan.pairs(lambda z, y, c, x: (z, y, c, 1 - x)))
    moves.append(plan.pairs(lambda z, y, c, x: (z, 1 - y, c, x)))
    for pairs in moves:
        (got,) = yield [(value, pairs)]
        value = value + got
    if halves:
        (got,) = yield [(value, plan.flip_core())]
        return jnp.where(upper, jnp.concatenate([got, value]), jnp.concatenate([value, got]))
    return value


def total_over_devices(plan, value, more=()):
    travel, clock = Travel("small_sum", total_steps(plan, value)), None
    while travel.wanted:
        with jax.named_scope(travel.name):
            got = [send(v, pairs) for v, pairs in travel.wanted]
        if clock is None:
            clock = Clock(got[0])
            more = clock.through(more)
            got = [clock.token]
        try:
            travel.wanted = travel.steps.send(got)
        except StopIteration as end:
            travel.wanted, travel.result = None, end.value
    return travel.result, more


def slot_counts(pieces):
    counts = [piece.shape[0] for piece in pieces]
    return counts, [sum(counts[:i]) for i in range(len(counts))]


def spot_of(device, plan, split_columns):
    if split_columns:
        return device // plan.mp, device % plan.mp
    return (device % plan.mp) * plan.dp + device // plan.mp, 0


def assemble(plan, pieces, slots, split_columns):
    counts, offsets = slot_counts(pieces)
    total = sum(counts)
    rows, width = pieces[0].shape[1:]
    groups = plan.mp if split_columns else 1
    blocks = total // groups
    if rows % 16 and groups > 1 or width % 128:
        stacked = jnp.concatenate(pieces)
        stacked = lax.fori_loop(
            0,
            total,
            lambda i, held: lax.dynamic_update_index_in_dim(held, stacked[i], slots[i], 0),
            stacked,
        ).reshape(plan.dp, plan.mp, rows, width)
        if split_columns:
            return stacked.transpose(0, 2, 1, 3).reshape(plan.dp * rows, plan.mp * width)
        return stacked.transpose(1, 0, 2, 3).reshape(total * rows, width)
    depth = 8

    def kernel(slots_ref, *refs):
        sources, out = refs[: len(pieces)], refs[len(pieces)]
        held, in_sems, out_sems = refs[len(pieces) + 1 :]
        steps = [(a, s) for a in range(len(pieces)) for s in range(counts[a])]
        reads, writes = [], []
        for i, (a, s) in enumerate(steps):
            block, group = spot_of(slots_ref[i], plan, split_columns)
            columns = pl.ds(pl.multiple_of(group * width, 128), width)
            reads.append(pltpu.make_async_copy(sources[a].at[s], held.at[i], in_sems.at[i]))
            writes.append(
                pltpu.make_async_copy(held.at[i], out.at[block, :, columns], out_sems.at[i])
            )
        for i in range(total):
            reads[i].start()
        for i in range(total):
            reads[i].wait()
            writes[i].start()
        for i in range(total):
            writes[i].wait()

    whole = pl.pallas_call(
        kernel,
        out_shape=jax.ShapeDtypeStruct((blocks, rows, groups * width), pieces[0].dtype),
        grid_spec=pltpu.PrefetchScalarGridSpec(
            num_scalar_prefetch=1,
            grid=(1,),
            in_specs=[ANY] * len(pieces),
            out_specs=ANY,
            scratch_shapes=[
                pltpu.VMEM((total, rows, width), pieces[0].dtype),
                pltpu.SemaphoreType.DMA((total,)),
                pltpu.SemaphoreType.DMA((total,)),
            ],
        ),
        compiler_params=pltpu.CompilerParams(vmem_limit_bytes=VMEM_LIMIT),
        cost_estimate=pl.CostEstimate(
            flops=0, bytes_accessed=4 * total * rows * width, transcendentals=0
        ),
    )(slots, *pieces)
    return whole.reshape(blocks * rows, groups * width)


def disassemble(plan, whole, shard_shape, counts, slots, split_columns):
    total = sum(counts)
    rows, width = shard_shape
    groups = plan.mp if split_columns else 1
    offsets = [sum(counts[:i]) for i in range(len(counts))]
    if rows % 16 and groups > 1 or width % 128:
        if split_columns:
            shards = whole.reshape(plan.dp, rows, plan.mp, width).transpose(0, 2, 1, 3)
        else:
            shards = whole.reshape(plan.mp, plan.dp, rows, width).transpose(1, 0, 2, 3)
        source = shards.reshape(total, rows, width)
        shards = lax.fori_loop(
            0,
            total,
            lambda i, held: lax.dynamic_update_index_in_dim(held, source[slots[i]], i, 0),
            source,
        )
        return [shards[o : o + c] for o, c in zip(offsets, counts)]
    blocks = total // groups

    def kernel(slots_ref, source, *refs):
        outs = refs[: len(counts)]
        held, in_sems, out_sems = refs[len(counts) :]
        steps = [(a, s) for a in range(len(counts)) for s in range(counts[a])]
        reads, writes = [], []
        for i, (a, s) in enumerate(steps):
            block, group = spot_of(slots_ref[i], plan, split_columns)
            columns = pl.ds(pl.multiple_of(group * width, 128), width)
            reads.append(
                pltpu.make_async_copy(source.at[block, :, columns], held.at[i], in_sems.at[i])
            )
            writes.append(pltpu.make_async_copy(held.at[i], outs[a].at[s], out_sems.at[i]))
        for i in range(total):
            reads[i].start()
        for i in range(total):
            reads[i].wait()
            writes[i].start()
        for i in range(total):
            writes[i].wait()

    return pl.pallas_call(
        kernel,
        out_shape=[jax.ShapeDtypeStruct((c, rows, width), whole.dtype) for c in counts],
        grid_spec=pltpu.PrefetchScalarGridSpec(
            num_scalar_prefetch=1,
            grid=(1,),
            in_specs=[ANY],
            out_specs=[ANY] * len(counts),
            scratch_shapes=[
                pltpu.VMEM((total, rows, width), whole.dtype),
                pltpu.SemaphoreType.DMA((total,)),
                pltpu.SemaphoreType.DMA((total,)),
            ],
        ),
        compiler_params=pltpu.CompilerParams(vmem_limit_bytes=VMEM_LIMIT),
        cost_estimate=pl.CostEstimate(
            flops=0, bytes_accessed=4 * total * rows * width, transcendentals=0
        ),
    )(slots, whole.reshape(blocks, rows, groups * width))


PAIR = 2 * HD


def pair_blocks(ref, offset, group, pair, pairs):
    start = group * 3 * pairs * PAIR + pair * PAIR
    span = pairs * PAIR
    return [ref[:, start + part * span : start + part * span + PAIR] for part in range(3)]


def both_heads(block):
    low_lane = lax.broadcasted_iota(jnp.int32, block.shape, 1) < HD
    zero = jnp.zeros_like(block)
    return jnp.concatenate([jnp.where(low_lane, block, zero), jnp.where(low_lane, zero, block)])


def own_columns(stacked):
    rows = stacked.shape[0] // 2
    low_lane = lax.broadcasted_iota(jnp.int32, (rows, PAIR), 1) < HD
    return jnp.where(low_lane, stacked[:rows], stacked[rows:])


def rows_by_rows(left, right):
    return lax.dot_general(left, right, (((1,), (1,)), ((), ())), preferred_element_type=jnp.float32)


def rows_of_both(left, right):
    return lax.dot_general(left, right, (((0,), (0,)), ((), ())), preferred_element_type=jnp.float32)


def pair_probs(stacked_queries, keys, allowed):
    scores = rows_by_rows(keys, stacked_queries) * HD ** (-0.5)
    scores = jnp.where(allowed, scores, masked_score)
    raised = jnp.exp(scores - jnp.max(scores, 0, keepdims=True))
    return raised * (1.0 / jnp.sum(raised, 0, keepdims=True))


def allowed_pairs(column_ref, row_ref):
    same = column_ref[0] == row_ref[0]
    shape = same.shape
    causal = lax.broadcasted_iota(jnp.int32, shape, 0) <= (
        lax.broadcasted_iota(jnp.int32, shape, 1) % LEN
    )
    return same & causal


def attend_kernel(groups, pairs, column_ref, row_ref, qkv_ref, context_ref):
    allowed = allowed_pairs(column_ref, row_ref)
    for group in range(groups):
        for pair in range(pairs):
            queries, keys, values = pair_blocks(qkv_ref, 0, group, pair, pairs)
            probs = pair_probs(both_heads(queries), keys, allowed).astype(jnp.bfloat16)
            context = own_columns(rows_of_both(probs, values))
            start = (group * pairs + pair) * PAIR
            context_ref[:, start : start + PAIR] = context.astype(jnp.bfloat16)


def attend_back_kernel(groups, pairs, column_ref, row_ref, qkv_ref, d_context_ref, d_qkv_ref):
    allowed = allowed_pairs(column_ref, row_ref)
    span = pairs * PAIR
    for group in range(groups):
        for pair in range(pairs):
            queries, keys, values = pair_blocks(qkv_ref, 0, group, pair, pairs)
            start = (group * pairs + pair) * PAIR
            d_context = both_heads(d_context_ref[:, start : start + PAIR])
            queries = both_heads(queries)
            probs = pair_probs(queries, keys, allowed)
            d_probs = rows_by_rows(values, d_context)
            d_values = matmul(probs.astype(jnp.bfloat16), d_context)
            weighted = probs * d_probs
            mean = jnp.sum(weighted, 0, keepdims=True)
            d_scores = (weighted - probs * mean).astype(jnp.bfloat16)
            d_queries = own_columns(rows_of_both(d_scores, keys)) * HD ** (-0.5)
            d_keys = matmul(d_scores, queries) * HD ** (-0.5)
            start = group * 3 * span + pair * PAIR
            for part, value in enumerate((d_queries, d_keys, d_values)):
                at = start + part * span
                d_qkv_ref[:, at : at + PAIR] = value.astype(jnp.bfloat16)


def attend_call(kernel, segments, qkv, others, out_columns, groups, scale):
    count = segments.shape[0]
    columns = qkv.shape[1]
    pairs = columns // (3 * groups * PAIR)
    rows = lambda wide: pl.BlockSpec((LEN, wide), lambda i: (i, 0))
    return pl.pallas_call(
        functools.partial(kernel, groups, pairs),
        out_shape=jax.ShapeDtypeStruct((qkv.shape[0], out_columns), jnp.bfloat16),
        grid=(count,),
        in_specs=[
            pl.BlockSpec((1, LEN, 1), lambda i: (i, 0, 0)),
            pl.BlockSpec((1, 1, 2 * LEN), lambda i: (i, 0, 0)),
            rows(columns),
        ]
        + [rows(other.shape[1]) for other in others],
        out_specs=rows(out_columns),
        compiler_params=pltpu.CompilerParams(vmem_limit_bytes=VMEM_LIMIT),
        cost_estimate=pl.CostEstimate(
            flops=scale * count * 2 * LEN * LEN * columns // 3,
            bytes_accessed=scale * qkv.size * 2,
            transcendentals=count * LEN * LEN * columns // (3 * HD),
        ),
    )(segments[:, :, None], jnp.tile(segments, (1, 2))[:, None, :], qkv, *others)


class Spread:
    def __init__(self, plan, parts, split_columns):
        self.plan, self.parts, self.split_columns = plan, parts, split_columns
        self.pieces = [piece for pieces, _ in parts for piece in pieces]
        self.slots = jnp.concatenate([slots for _, slots in parts])
        self.rows = self.pieces[0].shape[1]
        widths = [pieces[0].shape[2] for pieces, _ in parts]
        self.offsets = [sum(widths[:k]) for k in range(len(widths))]
        self.stride = sum(widths)
        groups = plan.mp if split_columns else 1
        self.shape = (plan.n // groups * self.rows, groups * self.stride)
        self.aligned = self.rows % 16 == 0 and all(width % 128 == 0 for width in widths)

    def matrix(self):
        groups = self.plan.mp if self.split_columns else 1
        wholes = [
            assemble(self.plan, pieces, slots, self.split_columns).reshape(
                self.shape[0], groups, -1
            )
            for pieces, slots in self.parts
        ]
        return jnp.concatenate(wholes, 2).reshape(self.shape)

    def places(self):
        found, first = [], 0
        for (pieces, _), offset in zip(self.parts, self.offsets):
            for k, piece in enumerate(pieces):
                found = found + [(first + k, slot, offset) for slot in range(piece.shape[0])]
            first = first + len(pieces)
        return found


def spot_slice(matrix_ref, plan, device, rows, width, split_columns, offset, stride):
    block, group = spot_of(device, plan, split_columns)
    at_rows = pl.ds(pl.multiple_of(block * rows, rows), rows)
    start = offset if isinstance(group, int) else pl.multiple_of(group * stride + offset, 128)
    return matrix_ref.at[at_rows, pl.ds(start, width)]


def with_matrices(plan, body, spreads, operands, outs, steps, flops):
    sizes = [len(spread.pieces) for spread in spreads]
    total = sum(spread.slots.shape[0] for spread in spreads)

    def kernel(slots_ref, *refs):
        inputs, refs = refs[: len(operands)], refs[len(operands) :]
        sources, refs = refs[: sum(sizes)], refs[sum(sizes) :]
        results, refs = refs[: len(outs)], refs[len(outs) :]
        kept, refs = refs[: len(spreads)], refs[len(spreads) :]
        matrices, sems, kept_sems = refs[: len(spreads)], refs[len(spreads)], refs[len(spreads) + 1]
        keeps = [
            pltpu.make_async_copy(matrix, out, kept_sems.at[k])
            for k, (matrix, out) in enumerate(zip(matrices, kept))
        ]

        @pl.when(pl.program_id(0) == 0)
        def _():
            copies, first = [], 0
            for spread, matrix in zip(spreads, matrices):
                for which, slot, offset in spread.places():
                    i = len(copies)
                    spot = spot_slice(
                        matrix,
                        plan,
                        slots_ref[i],
                        spread.rows,
                        spread.pieces[which].shape[2],
                        spread.split_columns,
                        offset,
                        spread.stride,
                    )
                    source = sources[first + which].at[slot]
                    copies.append(pltpu.make_async_copy(source, spot, sems.at[i]))
                    copies[-1].start()
                first = first + len(spread.pieces)
            for copy in copies:
                copy.wait()
            for keep in keeps:
                keep.start()

        body(inputs, matrices, results)

        @pl.when(pl.program_id(0) == pl.num_programs(0) - 1)
        def _():
            for keep in keeps:
                keep.wait()

    moved_bytes = sum(2 * spread.shape[0] * spread.shape[1] for spread in spreads)
    moved_bytes += sum(array.size * array.dtype.itemsize for array, _, _ in operands)
    moved_bytes += sum(np.prod(shape) * np.dtype(dtype).itemsize for shape, dtype, _, _ in outs)
    return pl.pallas_call(
        kernel,
        out_shape=[jax.ShapeDtypeStruct(shape, dtype) for shape, dtype, _, _ in outs]
        + [jax.ShapeDtypeStruct(spread.shape, jnp.bfloat16) for spread in spreads],
        grid_spec=pltpu.PrefetchScalarGridSpec(
            num_scalar_prefetch=1,
            grid=(steps,),
            in_specs=[pl.BlockSpec(block, index) for _, block, index in operands]
            + [ANY] * sum(sizes),
            out_specs=[pl.BlockSpec(block, index) for _, _, block, index in outs]
            + [ANY] * len(spreads),
            scratch_shapes=[pltpu.VMEM(spread.shape, jnp.bfloat16) for spread in spreads]
            + [
                pltpu.SemaphoreType.DMA((total,)),
                pltpu.SemaphoreType.DMA((len(spreads),)),
            ],
        ),
        compiler_params=pltpu.CompilerParams(vmem_limit_bytes=VMEM_LIMIT),
        cost_estimate=pl.CostEstimate(
            flops=flops, bytes_accessed=int(moved_bytes), transcendentals=0
        ),
    )(
        jnp.concatenate([spread.slots for spread in spreads]),
        *[array for array, _, _ in operands],
        *[piece for spread in spreads for piece in spread.pieces],
    )


def fixed(step, *scalars):
    return (0, 0)


def by_columns(step, *scalars):
    return (0, step)


def by_rows(step, *scalars):
    return (step, 0)


def step_slice(size):
    return pl.ds(pl.multiple_of(pl.program_id(0) * size, size), size)


def project(rows, spread, block):
    count, deep = rows.shape
    wide = spread.shape[1]
    if not spread.aligned or wide % block:
        whole = spread.matrix()
        return matmul(rows, whole).astype(jnp.bfloat16), whole

    def body(inputs, matrices, results):
        product = matmul(inputs[0][...], matrices[0][:, step_slice(block)])
        results[0][...] = product.astype(jnp.bfloat16)

    return with_matrices(
        spread.plan,
        body,
        [spread],
        [(rows, (count, deep), fixed)],
        [((count, wide), jnp.bfloat16, (count, block), by_columns)],
        wide // block,
        2 * count * deep * wide,
    )


def by_blocks(body, operands, outs, steps, flops):
    moved_bytes = sum(array.size * array.dtype.itemsize for array, _, _ in operands)
    moved_bytes += sum(np.prod(shape) * np.dtype(dtype).itemsize for shape, dtype, _, _ in outs)
    return pl.pallas_call(
        body,
        out_shape=[jax.ShapeDtypeStruct(shape, dtype) for shape, dtype, _, _ in outs],
        grid=(steps,),
        in_specs=[
            pl.BlockSpec(block, index, pipeline_mode=pl.Buffered(1 if index is fixed else 2))
            for _, block, index in operands
        ],
        out_specs=[pl.BlockSpec(block, index) for _, _, block, index in outs],
        compiler_params=pltpu.CompilerParams(vmem_limit_bytes=VMEM_LIMIT),
        cost_estimate=pl.CostEstimate(
            flops=flops, bytes_accessed=int(moved_bytes), transcendentals=0
        ),
    )(*[array for array, _, _ in operands])


def project_back(rows, matrix, block):
    count, deep = rows.shape
    wide = matrix.shape[0]
    if wide % block:
        return matmul_t(rows, matrix)

    def body(rows_ref, matrix_ref, out_ref):
        out_ref[...] = rows_by_rows(rows_ref[...], matrix_ref[...])

    return by_blocks(
        body,
        [(rows, (count, deep), fixed), (matrix, (block, deep), by_rows)],
        [((count, wide), jnp.float32, (count, block), by_columns)],
        wide // block,
        2 * count * deep * wide,
    )[0]


def gelu_and_slope(value):
    scale, cubic = (2.0 / np.pi) ** 0.5, 0.044715
    square = value * value
    bent = jnp.tanh(value * (scale + scale * cubic * square))
    half = 0.5 * bent + 0.5
    inner = value * (scale + 3.0 * scale * cubic * square)
    return value * half, half + (0.5 - 0.5 * bent * bent) * inner


def hidden_forward(rows, spread, block):
    count, deep = rows.shape
    wide = spread.shape[1]
    if not spread.aligned or wide % block:
        whole = spread.matrix()
        gelu, slope = gelu_and_slope(matmul(rows, whole))
        return gelu.astype(jnp.bfloat16), slope.astype(jnp.bfloat16), whole

    def body(inputs, matrices, results):
        up_pre = matmul(inputs[0][...], matrices[0][:, step_slice(block)])
        gelu, slope = gelu_and_slope(up_pre)
        results[0][...] = gelu.astype(jnp.bfloat16)
        results[1][...] = slope.astype(jnp.bfloat16)

    return with_matrices(
        spread.plan,
        body,
        [spread],
        [(rows, (count, deep), fixed)],
        [((count, wide), jnp.bfloat16, (count, block), by_columns)] * 2,
        wide // block,
        2 * count * deep * wide,
    )


def hidden_back(d_out, slope, matrix, block):
    count, wide = slope.shape
    if wide % block:
        d_activated = matmul_t(d_out, matrix)
        return (d_activated * slope.astype(jnp.float32)).astype(jnp.bfloat16)

    def body(d_out_ref, matrix_ref, slope_ref, out_ref):
        d_activated = rows_by_rows(d_out_ref[...], matrix_ref[...])
        out_ref[...] = (d_activated * slope_ref[...].astype(jnp.float32)).astype(jnp.bfloat16)

    return by_blocks(
        body,
        [
            (d_out, d_out.shape, fixed),
            (matrix, (block, d_out.shape[1]), by_rows),
            (slope, (count, block), by_columns),
        ],
        [((count, wide), jnp.bfloat16, (count, block), by_columns)],
        wide // block,
        2 * count * d_out.shape[1] * wide,
    )[0]


def heads_and_back(after, head, gain, shift, scales, targets):
    centred = after - jnp.mean(after, -1, keepdims=True)
    inverse = lax.rsqrt(jnp.mean(centred * centred, -1, keepdims=True) + norm_eps)
    unit = centred * inverse
    final = (unit * gain + shift).astype(jnp.bfloat16)
    logits = rows_by_rows(final, head)
    lane = lax.broadcasted_iota(jnp.int32, logits.shape, 1)
    edges = (0, RB, RB + AB, RB + AB + WB)
    inside = [(lane >= edges[k]) & (lane < edges[k + 1]) for k in range(3)]
    tops = [
        jnp.max(jnp.where(mask, logits, masked_score), -1, keepdims=True) for mask in inside
    ]

    def spread_over(columns, other):
        value = jnp.where(inside[2], columns[2], other)
        return jnp.where(inside[0], columns[0], jnp.where(inside[1], columns[1], value))

    lowered = spread_over([logits - top for top in tops], masked_score)
    raised = jnp.exp(lowered)
    totals = [jnp.sum(jnp.where(mask, raised, 0.0), -1, keepdims=True) for mask in inside]
    picked = [lane == targets[:, k : k + 1] for k in range(3)]
    loss = jnp.float32(0.0)
    for k in range(3):
        found = jnp.sum(jnp.where(picked[k], lowered, 0.0), -1, keepdims=True)
        loss = loss + jnp.sum(scales[:, k : k + 1] * (jnp.log(totals[k]) - found))
    hot = jnp.where(picked[0] | picked[1] | picked[2], 1.0, 0.0)
    shares = raised * spread_over([1.0 / total for total in totals], 0.0) - hot
    d_logits = (shares * spread_over([scales[:, k : k + 1] for k in range(3)], 0.0)).astype(
        jnp.bfloat16
    )
    d_unit = matmul(d_logits, head) * gain
    leaning = jnp.mean(d_unit * unit, -1, keepdims=True)
    d_after = inverse * (d_unit - jnp.mean(d_unit, -1, keepdims=True) - unit * leaning)
    return final, d_logits, loss, d_after


def context_back(d_up_pre, up, after, gain, d_later, exit_all, block):
    count, deep = d_up_pre.shape
    wide = up.shape[0]
    rows = (block, wide)

    def body(d_up_ref, up_ref, after_ref, gain_ref, later_ref, exit_ref, *outs):
        d_normed = rows_by_rows(d_up_ref[...], up_ref[...])
        outs[0][...] = d_normed
        after_rows = after_ref[...]
        centred = after_rows - jnp.mean(after_rows, -1, keepdims=True)
        inverse = lax.rsqrt(jnp.mean(centred * centred, -1, keepdims=True) + norm_eps)
        unit = centred * inverse
        d_unit = d_normed * gain_ref[...]
        leaning = jnp.mean(d_unit * unit, -1, keepdims=True)
        d_norm = inverse * (d_unit - jnp.mean(d_unit, -1, keepdims=True) - unit * leaning)
        d_out = (later_ref[...] + d_norm).astype(jnp.bfloat16)
        outs[1][...] = d_out
        outs[2][...] = rows_by_rows(d_out, exit_ref[...]).astype(jnp.bfloat16)

    return by_blocks(
        body,
        [
            (d_up_pre, (block, deep), by_rows),
            (up, up.shape, fixed),
            (after, rows, by_rows),
            (gain, gain.shape, fixed),
            (d_later, rows, by_rows),
            (exit_all, exit_all.shape, fixed),
        ],
        [
            ((count, wide), jnp.float32, rows, by_rows),
            ((count, wide), jnp.bfloat16, rows, by_rows),
            ((count, wide), jnp.bfloat16, rows, by_rows),
        ],
        count // block,
        2 * count * wide * (deep + wide),
    )


def hidden_out(activated, base, spread, head, gain, shift, scales, targets, block):
    count, deep = activated.shape
    wide = base.shape[1]
    lanes = head.shape[0]
    if not spread.aligned or count % block:
        whole = spread.matrix()
        after = base + matmul(activated, whole)
        final, d_logits, loss, d_after = heads_and_back(after, head, gain, shift, scales, targets)
        return after, final, d_logits, d_after, d_after.astype(jnp.bfloat16), loss[None], whole

    def body(inputs, matrices, results):
        after = inputs[1][...] + matmul(inputs[0][...], matrices[0][...])
        results[0][...] = after
        final, d_logits, loss, d_after = heads_and_back(
            after,
            inputs[2][...],
            inputs[3][...],
            inputs[4][...],
            inputs[5][...],
            inputs[6][...],
        )
        results[1][...] = final
        results[2][...] = d_logits
        results[3][...] = d_after
        results[4][...] = d_after.astype(jnp.bfloat16)
        results[5][...] = jnp.full(results[5].shape, loss)

    rows = (block, wide)
    return with_matrices(
        spread.plan,
        body,
        [spread],
        [
            (activated, (block, deep), by_rows),
            (base, rows, by_rows),
            (head, head.shape, fixed),
            (gain, gain.shape, fixed),
            (shift, shift.shape, fixed),
            (scales, (block, 3), by_rows),
            (targets, (block, 3), by_rows),
        ],
        [
            ((count, wide), jnp.float32, rows, by_rows),
            ((count, wide), jnp.bfloat16, rows, by_rows),
            ((count, lanes), jnp.bfloat16, (block, lanes), by_rows),
            ((count, wide), jnp.float32, rows, by_rows),
            ((count, wide), jnp.bfloat16, rows, by_rows),
            ((8 * (count // block), 128), jnp.float32, (8, 128), by_rows),
        ],
        count // block,
        2 * count * deep * wide,
    )


def weight_grad(plan, left, right, rows, parts, split_columns, block):
    tokens, high = left.shape
    wide = right.shape[1]
    groups = plan.mp if split_columns else 1
    stride = wide // groups
    along = wide if split_columns else high
    unit = stride if split_columns else rows
    widths = [width for width, _, _ in parts]
    offsets = [sum(widths[:k]) for k in range(len(parts))]
    fits = along % block == 0 and (block % unit == 0 or unit % block == 0)
    if rows % 16 or any(width % 128 for width in widths) or not fits:
        whole = contract(left, right).astype(jnp.bfloat16).reshape(high, groups, stride)
        found = []
        for (width, counts, slots), offset in zip(parts, offsets):
            part = whole[:, :, offset : offset + width].reshape(high, groups * width)
            found.append(disassemble(plan, part, (rows, width), counts, slots, split_columns))
        return found
    tile = 256 if split_columns else block
    outs_of = [(width, count) for width, counts, _ in parts for count in counts]
    places = [
        (width, offset, slot)
        for (width, counts, _), offset in zip(parts, offsets)
        for count in counts
        for slot in range(count)
    ]

    def kernel(slots_ref, left_ref, right_ref, *refs):
        outs, gradient, sems = refs[: len(outs_of)], refs[len(outs_of)], refs[len(outs_of) + 1]
        step = pl.program_id(0)
        for start in range(0, high if split_columns else block, tile):
            lefts = left_ref[:, start : start + tile]
            product = rows_of_both(lefts, right_ref[...]).astype(jnp.bfloat16)
            if split_columns:
                gradient[start : start + tile, step_slice(block)] = product
            else:
                gradient[step_slice(block), :] = product
        targets = [out.at[slot] for out, (_, count) in zip(outs, outs_of) for slot in range(count)]
        copies = []
        for i, (width, offset, _) in enumerate(places):
            spot = spot_slice(
                gradient, plan, slots_ref[i], rows, width, split_columns, offset, stride
            )
            copies.append(pltpu.make_async_copy(spot, targets[i], sems.at[i]))
        for i, (width, offset, _) in enumerate(places):
            row_block, group = spot_of(slots_ref[i], plan, split_columns)
            if split_columns:
                done_in = (group * stride + offset + width - 1) // block
            else:
                done_in = (row_block * rows) // block

            @pl.when(done_in == step)
            def _(copy=copies[i]):
                copy.start()

        @pl.when(step == pl.num_programs(0) - 1)
        def _():
            for copy in copies:
                copy.wait()

    if split_columns:
        left_spec = pl.BlockSpec((tokens, high), fixed)
        right_spec = pl.BlockSpec((tokens, block), by_columns)
    else:
        left_spec = pl.BlockSpec((tokens, block), by_columns)
        right_spec = pl.BlockSpec((tokens, wide), fixed)
    flat = pl.pallas_call(
        kernel,
        out_shape=[
            jax.ShapeDtypeStruct((count, rows, width), jnp.bfloat16) for width, count in outs_of
        ],
        grid_spec=pltpu.PrefetchScalarGridSpec(
            num_scalar_prefetch=1,
            grid=(along // block,),
            in_specs=[left_spec, right_spec],
            out_specs=[ANY] * len(outs_of),
            scratch_shapes=[
                pltpu.VMEM((high, wide), jnp.bfloat16),
                pltpu.SemaphoreType.DMA((len(places),)),
            ],
        ),
        compiler_params=pltpu.CompilerParams(vmem_limit_bytes=VMEM_LIMIT),
        cost_estimate=pl.CostEstimate(
            flops=2 * tokens * high * wide,
            bytes_accessed=2 * (tokens * (high + wide) + high * wide),
            transcendentals=0,
        ),
    )(jnp.concatenate([slots for _, _, slots in parts]), left, right)
    found = []
    for _, counts, _ in parts:
        found.append(flat[: len(counts)])
        flat = flat[len(counts) :]
    return found


def adam_step(first, root, clipped, corr_first, corr_second):
    first = beta_first * first + (1.0 - beta_first) * clipped
    second = beta_second * root * root + (1.0 - beta_second) * clipped * clipped
    direction = first / corr_first / (jnp.sqrt(second / corr_second) + adam_eps)
    return first, jnp.sqrt(second), direction


def views(matrix, columns):
    width = matrix.shape[-1]
    if len(matrix.shape) == 3:
        return [((k,), 0, width) for k in range(matrix.shape[0])]
    starts = [sum(columns[:k]) for k in range(len(columns))]
    return [((), start, size) for start, size in zip(starts, columns)]


LOSS, SQUARE, WEIGHTS, GRAD_NORM = 0, 1, 2, 5


def number_at(row, place):
    lane = lax.broadcasted_iota(jnp.int32, row.shape, 1)
    return jnp.sum(jnp.where(lane == place, row, 0.0), keepdims=True)


def row_of(numbers):
    lane = lax.broadcasted_iota(jnp.int32, (1, 128), 1)
    row = jnp.zeros((1, 128), jnp.float32)
    for place, number in numbers.items():
        row = jnp.where(lane == place, number, row)
    return row


def moments_and_directions(corrections, small, gradients, states, masters, norms):
    count = len(masters)
    flat = [part for parts in gradients for part in parts]
    smem = pl.BlockSpec(memory_space=pltpu.SMEM)
    vmem = pl.BlockSpec(memory_space=pltpu.VMEM)

    def kernel(corrections_ref, small_ref, *refs):
        parts, refs = list(refs[: len(flat)]), refs[len(flat) :]
        old, weights, refs = refs[:count], refs[count : 2 * count], refs[2 * count :]
        (norm_old, norm_weight), refs = refs[:2], refs[2:]
        fresh, ways, refs = refs[:count], refs[count : 2 * count], refs[2 * count :]
        norm_fresh, norm_out, row_ref = refs
        corr_first, corr_second = corrections_ref[0], corrections_ref[1]
        head_grad, norm_grad = parts[-1][...], small_ref[:6]
        square = number_at(small_ref[6:7], SQUARE)
        square = square + jnp.sum(head_grad * head_grad, keepdims=True)
        grad_norm = jnp.sqrt(square + jnp.sum(norm_grad * norm_grad, keepdims=True))
        clip = jnp.minimum(1.0, clip_limit / grad_norm)
        numbers = {GRAD_NORM: grad_norm}
        for k in range(count):
            mine = [parts.pop(0) for _ in gradients[k]]
            total = jnp.zeros((1, 1), jnp.float32)
            for which, (lead, start, width) in enumerate(
                views(masters[k], [part.shape[1] for part in gradients[k]])
            ):
                columns = slice(start, start + width)
                if lead:
                    gradient = mine[0][:, which * width : (which + 1) * width]
                else:
                    gradient = mine[which][...]
                spot = lead + (slice(None), columns)
                first, root, direction = adam_step(
                    old[k][(0,) + spot],
                    old[k][(1,) + spot],
                    clip * gradient,
                    corr_first,
                    corr_second,
                )
                fresh[k][(0,) + spot] = first
                fresh[k][(1,) + spot] = root
                direction = direction + weight_decay * weights[k][spot]
                ways[k][spot] = direction
                total = total + jnp.sum(direction * direction, keepdims=True)
            numbers[k] = total
        first, root, direction = adam_step(
            norm_old[0], norm_old[1], clip * norm_grad, corr_first, corr_second
        )
        norm_fresh[0] = first
        norm_fresh[1] = root
        norm_out[...] = norm_weight[...] - learn_rate * direction
        row_ref[...] = row_of(numbers)

    like = lambda value: jax.ShapeDtypeStruct(value.shape, jnp.float32)
    found = pl.pallas_call(
        kernel,
        out_shape=[like(state) for state in states]
        + [like(master) for master in masters]
        + [like(norms[0]), like(norms[1]), jax.ShapeDtypeStruct((1, 128), jnp.float32)],
        in_specs=[smem] + [vmem] * (len(flat) + 2 * count + 3),
        out_specs=[vmem] * (2 * count + 3),
        compiler_params=pltpu.CompilerParams(vmem_limit_bytes=VMEM_LIMIT),
    )(corrections, small, *flat, *states, *masters, *norms)
    return list(found[:count]), found[count : 2 * count], *found[2 * count :]


def new_weights(head_square, small, row, summed, masters, directions):
    count = len(masters)
    smem = pl.BlockSpec(memory_space=pltpu.SMEM)
    vmem = pl.BlockSpec(memory_space=pltpu.VMEM)

    def kernel(head_ref, small_ref, row_ref, summed_ref, *refs):
        weights, ways, refs = refs[:count], refs[count : 2 * count], refs[2 * count :]
        weight_norms, update_norms = {}, {}
        for k in range(count):
            if k < count - 1:
                weight_norms[k] = jnp.sqrt(number_at(small_ref[6:7], WEIGHTS + k))
                update_norms[k] = jnp.sqrt(number_at(summed_ref[...], k))
            else:
                weight_norms[k] = jnp.sqrt(jnp.full((1, 1), head_ref[0]))
                update_norms[k] = jnp.sqrt(number_at(row_ref[...], k))
            step = learn_rate * (weight_norms[k] / update_norms[k])
            value = weights[k][...] - step * ways[k][...]
            refs[k][...] = value
            if k < count - 1:
                refs[count + k][...] = value.astype(jnp.bfloat16)
        refs[-1][0:1] = row_of(weight_norms)
        refs[-1][1:2] = row_of(update_norms)

    found = pl.pallas_call(
        kernel,
        out_shape=[jax.ShapeDtypeStruct(master.shape, jnp.float32) for master in masters]
        + [jax.ShapeDtypeStruct(master.shape, jnp.bfloat16) for master in masters[:-1]]
        + [jax.ShapeDtypeStruct((2, 128), jnp.float32)],
        in_specs=[smem] + [vmem] * (3 + 2 * count),
        out_specs=[vmem] * (2 * count),
        compiler_params=pltpu.CompilerParams(vmem_limit_bytes=VMEM_LIMIT),
    )(head_square, small, row, summed, *masters, *directions)
    return found[:count], found[count:-1], found[-1]


BY_COLUMNS = ("entry", "up")
SPLITS = {"up": ((0, 1), (2,)), "down": ((0, 1), (2,))}


def per_device(
    plan,
    tokens,
    segment_ids,
    game_ids,
    return_bins,
    action_bins,
    reward_bins,
    valid_flags,
    step_count,
    entry_weight,
    entry_state,
    exit_weight,
    exit_state,
    up_weight,
    up_state,
    down_weight,
    down_state,
    head_weight,
    head_state,
    norm_params,
    norm_state,
):
    own_rows = tokens.shape[0]
    here = lax.axis_index("dp") * plan.mp + lax.axis_index("mp")
    row_start = lax.axis_index("mp") * own_rows
    own_seqs = own_rows // LEN
    segments = lax.dynamic_slice_in_dim(segment_ids, lax.axis_index("mp") * own_seqs, own_seqs)
    row_games = lax.dynamic_slice_in_dim(jnp.repeat(game_ids, LEN), row_start, own_rows)

    clock = Clock(step_count.astype(jnp.float32))
    masters = {"entry": entry_weight, "exit": exit_weight, "up": up_weight, "down": down_weight}
    rows_here, half_wide = entry_weight.shape[1:]
    halves = {name: value.astype(jnp.bfloat16) for name, value in masters.items()}
    entry_shard = halves["entry"].transpose(1, 0, 2).reshape(rows_here, 3 * half_wide)
    paths = {
        name: Travel("gather_" + name, gather_shards(plan, shard, split))
        for name, shard, split in (
            ("entry", entry_shard, ()),
            ("up", halves["up"], ((0, 1), (2,))),
            ("down", halves["down"], ()),
        )
    }
    game_match = (row_games[:, None] == jnp.arange(GAMES)[None, :]).astype(jnp.float32)
    flag_float = valid_flags.astype(jnp.float32)
    local_counts = jnp.sum(game_match * jnp.sum(flag_float, -1, keepdims=True), 0)
    exit_rows, wide = exit_weight.shape
    tens = jnp.floor(local_counts / 64.0)
    pair = jnp.concatenate([tens, local_counts - 64.0 * tens]).astype(jnp.bfloat16)
    below = jnp.zeros((16 - exit_rows % 16, wide), jnp.bfloat16).at[0, : 2 * GAMES].set(pair)
    gathered = lax.all_gather(jnp.concatenate([halves["exit"], below]), ("mp", "dp"), axis=0)
    exit_all = gathered[:, :exit_rows].reshape(-1, wide)
    pairs_all = jnp.sum(gathered[:, exit_rows, : 2 * GAMES].astype(jnp.float32), 0)
    counts_all = 64.0 * pairs_all[:GAMES] + pairs_all[GAMES:]
    inverse = 1.0 / (GAMES * jnp.maximum(counts_all, 1.0))
    token_scale = jnp.sum(game_match * inverse[None, :], -1)

    slots = jnp.asarray(path_table(plan), jnp.int32)[here]

    def chosen(names):
        return [paths[name] for name in names.split() if paths[name].wanted]

    def start(names, *more):
        return clock.start(chosen(names), more)

    def wait(names, *more):
        return clock.wait([path for path in chosen(names) if path.going], more)

    def finish(name):
        while paths[name].wanted:
            start(name)
            wait(name)
        return paths[name].result

    def whole(name):
        return Spread(plan, [(finish(name), slots)], name in BY_COLUMNS)


    resid, gains = start("entry", tokens.astype(jnp.float32), norm_params)
    normed_one = layer_norm(resid, gains[0], gains[3]).astype(jnp.bfloat16)
    (normed_one,) = wait("entry", normed_one)
    start("entry up")
    wait("entry up")
    start("entry up")
    wait("entry up")
    start("entry up")
    wait("entry")
    (normed_one,) = start("down", normed_one)
    projected, entry_all = project(normed_one, whole("entry"), 768)
    (projected,) = wait("up down", projected)
    (projected,) = start("up", projected)
    context = attend_call(
        attend_kernel, segments, projected, [], tokens.shape[1], plan.mp, 2
    )
    after_attn = resid + matmul(context, exit_all)
    normed_two = layer_norm(after_attn, norm_params[1], norm_params[4]).astype(jnp.bfloat16)
    after_attn, normed_two = wait("up", after_attn, normed_two)
    (normed_two,) = start("up down", normed_two)
    wait("up")
    (normed_two,) = start("", normed_two)
    activated, slope, up_all = hidden_forward(normed_two, whole("up"), 512)
    activated, slope = wait("down", activated, slope)
    head_rows = head_weight.shape[0]
    head_half = jnp.pad(head_weight.astype(jnp.bfloat16), ((0, -head_rows % 128), (0, 0)))
    targets = jnp.stack([return_bins, action_bins + RB, reward_bins + (RB + AB)], 1)
    scales = flag_float * token_scale[:, None]
    late = start("down", *masters.values())
    weight_local = jnp.stack([jnp.sum(master * master) for master in late])
    weight_local, head_half, targets, scales = wait(
        "down", weight_local, head_half, targets, scales
    )
    start("down")
    wait("down")
    after_mlp, final_norm, d_logits, d_mlp_in, d_mlp_out, losses, down_all = hidden_out(
        activated,
        after_attn,
        whole("down"),
        head_half,
        norm_params[2:3],
        norm_params[5:6],
        scales,
        targets,
        320,
    )
    loss_local = jnp.sum(losses.reshape(-1, 8, 128)[:, 0, 0]) if losses.ndim > 1 else losses[0]

    def leave(names, left, right, rows, widths, block):
        by_columns = names.split()[0] in ("entry_a", "up")
        parts = [(width, scatter_counts(plan), slots) for width in widths]
        found = weight_grad(plan, left, right, rows, parts, by_columns, block)
        for name, pieces in zip(names.split(), found):
            steps = scatter_shards(plan, pieces, SPLITS.get(name, ()), name == "up")
            paths[name] = Travel("scatter_" + name, steps)

    down_rows = down_weight.shape[0]
    entry_widths = (3 * half_wide * 8 // 15, 3 * half_wide - 3 * half_wide * 8 // 15)
    leave("down", activated, d_mlp_out, down_rows, [wide], 1280)
    d_head = contract(d_logits, final_norm)[: head_rows + head_rows % 2]
    paths["head"] = Travel("sum_head", total_steps(plan, d_head, halves=True))
    (d_mlp_out,) = start("down head", d_mlp_out)
    d_up_pre = hidden_back(d_mlp_out, slope, down_all, 512)
    (d_up_pre,) = wait("down head", d_up_pre)
    (d_up_pre,) = start("down head", d_up_pre)
    leave("up", normed_two, d_up_pre, rows_here, [up_weight.shape[1]], 2560)
    (d_up_pre,) = wait("down head", d_up_pre)
    (d_up_pre,) = start("down up head", d_up_pre)
    d_normed_two, d_attn_out, d_context = context_back(
        d_up_pre, up_all, after_attn, norm_params[1:2], d_mlp_in, exit_all, 320
    )
    leave("exit", context, d_attn_out, exit_rows, [wide], 1280)
    (d_context,) = wait("down up head", d_context)
    (d_context,) = start("down up exit", d_context)
    d_projected = attend_call(
        attend_back_kernel, segments, projected, [d_context], projected.shape[1], plan.mp, 5
    )
    (d_projected,) = wait("down up exit", d_projected)
    (d_projected,) = start("up down exit", d_projected)
    leave("entry_a entry_b", normed_one, d_projected, rows_here, entry_widths, 1920)
    (d_projected,) = wait("up down exit", d_projected)
    (d_projected,) = start("up entry_a entry_b", d_projected)
    d_normed_one = project_back(d_projected, entry_all, 256)
    reds = {"down": finish("down")}
    (d_normed_one,) = wait("up entry_a entry_b", d_normed_one)
    d_normed_one, reds = start("entry_a entry_b up head", d_normed_one, reds)
    down_square = jnp.sum(reds["down"] * reds["down"])
    _, d_gain_one, d_shift_one = norm_back(resid, norm_params[0], norm_params[3], d_normed_one)
    d_gain_one, d_shift_one, reds, down_square = wait(
        "entry_a entry_b up head", d_gain_one, d_shift_one, reds, down_square
    )
    late = start("entry_a up exit", after_mlp, d_logits, after_attn, d_normed_two)
    d_final = matmul(late[1], head_half)
    _, d_gain_three, d_shift_three = norm_back(late[0], norm_params[2], norm_params[5], d_final)
    _, d_gain_two, d_shift_two = norm_back(late[2], norm_params[1], norm_params[4], late[3])
    late = wait("entry_a up exit", d_gain_two, d_shift_two, d_gain_three, d_shift_three)
    d_gain_two, d_shift_two, d_gain_three, d_shift_three = late
    start("entry_b entry_a head")
    reds["up"] = finish("up")
    up_square = jnp.sum(reds["up"] * reds["up"])
    reds, up_square = wait("entry_b entry_a head", reds, up_square)
    start("entry_b exit head")
    wait("entry_b exit head")
    reds["exit"] = finish("exit")
    exit_square = jnp.sum(reds["exit"] * reds["exit"])
    red_head = finish("head")[:head_rows]
    reds["entry_a"], reds["entry_b"] = finish("entry_a"), finish("entry_b")
    local_square = down_square + up_square + exit_square
    for name in ("entry_a", "entry_b"):
        local_square = local_square + jnp.sum(reds[name] * reds[name])
    masters = [entry_weight, exit_weight, up_weight, down_weight, head_weight]
    states = [entry_state, exit_state, up_state, down_state, head_state]
    wide = norm_params.shape[1]
    scalars = jnp.concatenate(
        [jnp.stack([loss_local, local_square]), weight_local, clock.token]
    )
    small, _ = total_over_devices(
        plan,
        jnp.stack(
            [
                d_gain_one,
                d_gain_two,
                d_gain_three,
                d_shift_one,
                d_shift_two,
                d_shift_three,
                jnp.pad(scalars, (0, wide - scalars.shape[0])),
            ]
        ),
    )
    step_float = step_count.astype(jnp.float32)
    corrections = jnp.concatenate(
        [1.0 - jnp.power(beta_first, step_float), 1.0 - jnp.power(beta_second, step_float)]
    )
    gradients = [
        [jnp.concatenate([reds["entry_a"], reds["entry_b"]], 1)],
        [reds["exit"]],
        [reds["up"]],
        [reds["down"]],
        [red_head],
    ]
    moments, directions, norm_moments, norm_new, row = moments_and_directions(
        corrections, small, gradients, states, masters, (norm_state, norm_params)
    )
    summed, late = total_over_devices(plan, row, (moments[4], norm_moments))
    moments[4], norm_moments = late
    new, rounded, norms = new_weights(
        jnp.sum(head_weight * head_weight)[None], small, row, summed, masters, directions
    )
    loss_sum, grad_norm, matrix_norms = small[6, LOSS], row[0, GRAD_NORM], norms[:, :5]
    return (
        new[0],
        moments[0],
        rounded[0],
        new[1],
        moments[1],
        rounded[1],
        new[2],
        moments[2],
        rounded[2],
        new[3],
        moments[3],
        rounded[3],
        new[4],
        moments[4],
        norm_new,
        norm_moments,
        loss_sum,
        grad_norm,
        matrix_norms,
    )


def solution(mesh):
    in_specs = (
        P(("dp", "mp"), None),
        P("dp", None),
        P("dp"),
        P(("dp", "mp")),
        P(("dp", "mp")),
        P(("dp", "mp")),
        P(("dp", "mp"), None),
        P(),
        P(None, "dp", "mp"),
        P(None, None, "dp", "mp"),
        P(("mp", "dp"), None),
        P(None, ("mp", "dp"), None),
        P("dp", "mp"),
        P(None, "dp", "mp"),
        P(("mp", "dp"), None),
        P(None, ("mp", "dp"), None),
        P(),
        P(),
        P(),
        P(),
    )
    out_specs = (
        P(None, "dp", "mp"),
        P(None, None, "dp", "mp"),
        P(None, "dp", "mp"),
        P(("mp", "dp"), None),
        P(None, ("mp", "dp"), None),
        P(("mp", "dp"), None),
        P("dp", "mp"),
        P(None, "dp", "mp"),
        P("dp", "mp"),
        P(("mp", "dp"), None),
        P(None, ("mp", "dp"), None),
        P(("mp", "dp"), None),
        P(),
        P(),
        P(),
        P(),
        P(),
        P(),
        P(),
    )
    plan = Plan(mesh.shape["dp"], mesh.shape["mp"])
    return jax.shard_map(
        functools.partial(per_device, plan), mesh=mesh, in_specs=in_specs, out_specs=out_specs, check_vma=False
    )
```

```python
import functools

import jax
import jax.numpy as jnp
import numpy as np
from jax import lax
from jax.experimental import pallas as pl
from jax.experimental.pallas import tpu as pltpu
from jax.sharding import PartitionSpec as P

HD = 64
RB = 120
AB = 18
WB = 4
GAMES = 41
LEN = 160


clip_limit = 0.05
learn_rate = 0.5
beta_first = 0.5
beta_second = 0.5
weight_decay = 0.01
adam_eps = 1e-08
norm_eps = 1e-05
masked_score = -1e30


def layer_norm(rows, gain, shift):
    centred = rows - jnp.mean(rows, -1, keepdims=True)
    spread = jnp.mean(centred * centred, -1, keepdims=True)
    return centred * lax.rsqrt(spread + norm_eps) * gain + shift


def norm_back(rows, gain, shift, upstream):
    _, pullback = jax.vjp(layer_norm, rows, gain, shift)
    return pullback(upstream)


def matmul(left, right):
    return jnp.dot(left, right, preferred_element_type=jnp.float32)


def matmul_t(left, right):
    return jnp.einsum("ti,ji->tj", left, right, preferred_element_type=jnp.float32)


def contract(left, right):
    return jnp.einsum("ti,tj->ij", left, right, preferred_element_type=jnp.float32)


AXES = ("dp", "mp")
VMEM_LIMIT = 60 * 2**20
ANY = pl.BlockSpec(memory_space=pl.ANY)


def room_for(*buffers):
    need = sum(int(np.prod(shape)) * size * copies for shape, size, copies in buffers)
    room = min(60 * 2**20, need + need // 8 + 8 * 2**20)
    return pltpu.CompilerParams(vmem_limit_bytes=int(room))


class Plan:
    def __init__(self, dp, mp):
        self.dp, self.mp = dp, mp
        self.core = 2 if dp % 2 == 0 else 1
        self.y = 2 if dp % (2 * self.core) == 0 else 1
        self.z = dp // (self.core * self.y)
        self.n = dp * mp
        self.grid = np.arange(self.n).reshape(self.z, self.y, self.core, mp)
        self.place = [tuple(int(v) for v in np.argwhere(self.grid == i)[0]) for i in range(self.n)]

    def pairs(self, move):
        found = []
        for i, spot in enumerate(self.place):
            target = move(*spot)
            if target is not None and 0 <= target[0] < self.z:
                found.append((i, int(self.grid[target])))
        return found

    def flip_core(self):
        return self.pairs(lambda z, y, c, x: (z, y, 1 - c, x))

    def flip_first(self):
        return self.pairs(lambda z, y, c, x: (z, 1 - y, c, x) if c == 0 else (z, y, c, 1 - x))

    def flip_second(self):
        return self.pairs(lambda z, y, c, x: (z, y, c, 1 - x) if c == 0 else (z, 1 - y, c, x))

    def flip_z(self, bits):
        return self.pairs(lambda z, y, c, x: (z ^ bits, y, c, x))

    def z_moves(self):
        return [self.flip_z(bits) for bits in range(1, self.z)]

    def z_groups(self, split):
        return split if split and self.z == 4 else (tuple(range(self.z - 1)),)


def moved(table, pairs):
    got = np.full_like(table, -1)
    for source, target in pairs:
        got[target] = table[source]
    return got


def send(value, pairs):
    return lax.ppermute(value, AXES, pairs)


def add_all(parts, dtype=jnp.bfloat16):
    total = parts[0].astype(jnp.float32)
    for part in parts[1:]:
        total = total + part.astype(jnp.float32)
    return total.astype(dtype)


class Sum:
    def __init__(self, terms, count):
        self.terms, self.count = terms, count
        self.shape = terms[0][0].shape[1:]


def make_sums(sums):
    if not sums:
        return []
    arrays = [array for job in sums for array, _ in job.terms]
    parts = [job.count // 2 if job.count % 2 == 0 else job.count for job in sums]
    in_specs, out_specs = [], []
    for job, part in zip(sums, parts):
        moves = int(part < job.count)

        def spec(offset, part=part, moves=moves, shape=job.shape):
            return pl.BlockSpec(
                (part,) + shape, lambda i, at=offset // part: (at + moves * i, 0, 0)
            )

        in_specs = in_specs + [spec(offset) for _, offset in job.terms]
        out_specs.append(spec(0))

    def kernel(*refs):
        outs, first = refs[len(arrays) :], 0
        for job, part, out in zip(sums, parts, outs):
            mine = refs[first : first + len(job.terms)]
            first = first + len(job.terms)

            def add(mine=mine, out=out):
                out[...] = add_all([ref[...] for ref in mine])

            if part < job.count:
                add()
            else:
                pl.when(pl.program_id(0) == 0)(add)

    size = sum(job.count * np.prod(job.shape) * (len(job.terms) + 1) for job in sums)
    return pl.pallas_call(
        kernel,
        out_shape=[jax.ShapeDtypeStruct((job.count,) + job.shape, jnp.bfloat16) for job in sums],
        grid=(2,),
        in_specs=in_specs,
        out_specs=out_specs,
        compiler_params=pltpu.CompilerParams(vmem_limit_bytes=VMEM_LIMIT),
        cost_estimate=pl.CostEstimate(
            flops=int(size), bytes_accessed=int(2 * size), transcendentals=0
        ),
    )(*arrays)


class Travel:
    def __init__(self, name, steps, quiet=False):
        self.name, self.steps, self.quiet = name, steps, quiet
        self.result, self.going = None, None
        self.wanted = next(steps)


class Clock:
    def __init__(self, token):
        self.token = token

    def through(self, values):
        flat, tree = jax.tree.flatten(values)
        passed = lax.optimization_barrier(tuple(flat) + (self.token,))
        self.token = passed[-1]
        return jax.tree.unflatten(tree, passed[:-1])

    def start(self, travels, more=()):
        wanted = [[v for v, _ in travel.wanted] for travel in travels]
        made = list(make_sums([v for want in wanted for v in want if isinstance(v, Sum)]))
        wanted = [[made.pop(0) if isinstance(v, Sum) else v for v in want] for want in wanted]
        values, more = self.through((wanted, more))
        for travel, ready in zip(travels, values):
            with jax.named_scope(travel.name):
                travel.going = [send(v, pairs) for v, (_, pairs) in zip(ready, travel.wanted)]
        return more

    def wait(self, travels, more=()):
        loud = [travel for travel in travels if not travel.quiet]
        arrived, more = self.through(([travel.going for travel in loud], more))
        for travel, got in zip(loud, arrived):
            travel.going = got
        for travel in travels:
            got, travel.going = travel.going, None
            try:
                travel.wanted = travel.steps.send(got)
            except StopIteration as end:
                travel.wanted, travel.result = None, end.value
        return more


def path_table(plan):
    first, second, core = plan.flip_first(), plan.flip_second(), plan.flip_core()
    own = np.arange(plan.n)[:, None]
    line = np.concatenate([own] + [moved(own, pairs) for pairs in plan.z_moves()], 1)
    near, side = moved(line, first), moved(line, second)
    table = np.concatenate([line, near, side, moved(near, second)], 1)
    return np.concatenate([table, moved(table, core)], 1)


def gather_shards(plan, shard, split=()):
    first, second, core = plan.flip_first(), plan.flip_second(), plan.flip_core()
    moves, got = plan.z_moves(), {}
    for group in plan.z_groups(split):
        arrived = yield [(shard[None], moves[k]) for k in group]
        got.update(zip(group, arrived))
    line = jnp.concatenate([shard[None]] + [got[k] for k in range(len(moves))])
    near, side = yield [(line, first), (line, second)]
    far, line_twin, near_twin = yield [(near, second), (line, core), (near, core)]
    side_twin, far_twin = yield [(side, core), (far, core)]
    return [line, near, side, far, line_twin, near_twin, side_twin, far_twin]


def scatter_counts(plan):
    return [4 * plan.z, 3 * plan.z, plan.z]


def scatter_shards(plan, pieces, split=(), apart=False):
    first, second, core = plan.flip_first(), plan.flip_second(), plan.flip_core()
    own, rest_twin, far_twin = pieces
    size = plan.z
    far_got, rest_got = yield [(far_twin, core), (rest_twin, core)]
    (far_got,) = yield [(Sum([(own, 3 * size), (far_got, 0)], size), second)]
    near_sum = Sum([(own, size), (rest_got, size), (far_got, 0)], size)
    side_sum = Sum([(own, 2 * size), (rest_got, 2 * size)], size)
    if apart:
        (near_got,) = yield [(near_sum, first)]
        (side_got,) = yield [(side_sum, second)]
    else:
        near_got, side_got = yield [(near_sum, first), (side_sum, second)]
    terms = [own, rest_got, near_got, side_got]
    moves, arrived = plan.z_moves(), []
    for group in plan.z_groups(split):
        arrived += yield [(Sum([(term, k + 1) for term in terms], 1), moves[k]) for k in group]
    return add_all([term[:1] for term in terms] + arrived, jnp.float32)[0]


def total_steps(plan, value, halves=False):
    if halves:
        half = value.shape[0] // 2
        upper = lax.axis_index("dp") % 2 == 1
        keep = jnp.where(upper, value[half:], value[:half])
        (got,) = yield [(jnp.where(upper, value[:half], value[half:]), plan.flip_core())]
        value = keep + got
    else:
        (got,) = yield [(value, plan.flip_core())]
        value = value + got
    moves, bit = [], 1
    while bit < plan.z:
        moves.append(plan.flip_z(bit))
        bit *= 2
    moves.append(plan.pairs(lambda z, y, c, x: (z, y, c, 1 - x)))
    moves.append(plan.pairs(lambda z, y, c, x: (z, 1 - y, c, x)))
    for pairs in moves:
        (got,) = yield [(value, pairs)]
        value = value + got
    if halves:
        (got,) = yield [(value, plan.flip_core())]
        return jnp.where(upper, jnp.concatenate([got, value]), jnp.concatenate([value, got]))
    return value


def total_over_devices(plan, value, more=()):
    travel, clock = Travel("small_sum", total_steps(plan, value)), None
    while travel.wanted:
        with jax.named_scope(travel.name):
            got = [send(v, pairs) for v, pairs in travel.wanted]
        if clock is None:
            clock = Clock(got[0])
            more = clock.through(more)
            got = [clock.token]
        try:
            travel.wanted = travel.steps.send(got)
        except StopIteration as end:
            travel.wanted, travel.result = None, end.value
    return travel.result, more


def slot_counts(pieces):
    counts = [piece.shape[0] for piece in pieces]
    return counts, [sum(counts[:i]) for i in range(len(counts))]


def spot_of(device, plan, split_columns):
    if split_columns:
        return device // plan.mp, device % plan.mp
    return (device % plan.mp) * plan.dp + device // plan.mp, 0


def assemble(plan, pieces, slots, split_columns):
    counts, offsets = slot_counts(pieces)
    total = sum(counts)
    rows, width = pieces[0].shape[1:]
    groups = plan.mp if split_columns else 1
    blocks = total // groups
    if rows % 16 and groups > 1 or width % 128:
        stacked = jnp.concatenate(pieces)
        stacked = lax.fori_loop(
            0,
            total,
            lambda i, held: lax.dynamic_update_index_in_dim(held, stacked[i], slots[i], 0),
            stacked,
        ).reshape(plan.dp, plan.mp, rows, width)
        if split_columns:
            return stacked.transpose(0, 2, 1, 3).reshape(plan.dp * rows, plan.mp * width)
        return stacked.transpose(1, 0, 2, 3).reshape(total * rows, width)
    depth = 8

    def kernel(slots_ref, *refs):
        sources, out = refs[: len(pieces)], refs[len(pieces)]
        held, in_sems, out_sems = refs[len(pieces) + 1 :]
        steps = [(a, s) for a in range(len(pieces)) for s in range(counts[a])]
        reads, writes = [], []
        for i, (a, s) in enumerate(steps):
            block, group = spot_of(slots_ref[i], plan, split_columns)
            columns = pl.ds(pl.multiple_of(group * width, 128), width)
            reads.append(pltpu.make_async_copy(sources[a].at[s], held.at[i], in_sems.at[i]))
            writes.append(
                pltpu.make_async_copy(held.at[i], out.at[block, :, columns], out_sems.at[i])
            )
        for i in range(total):
            reads[i].start()
        for i in range(total):
            reads[i].wait()
            writes[i].start()
        for i in range(total):
            writes[i].wait()

    whole = pl.pallas_call(
        kernel,
        out_shape=jax.ShapeDtypeStruct((blocks, rows, groups * width), pieces[0].dtype),
        grid_spec=pltpu.PrefetchScalarGridSpec(
            num_scalar_prefetch=1,
            grid=(1,),
            in_specs=[ANY] * len(pieces),
            out_specs=ANY,
            scratch_shapes=[
                pltpu.VMEM((total, rows, width), pieces[0].dtype),
                pltpu.SemaphoreType.DMA((total,)),
                pltpu.SemaphoreType.DMA((total,)),
            ],
        ),
        compiler_params=pltpu.CompilerParams(vmem_limit_bytes=VMEM_LIMIT),
        cost_estimate=pl.CostEstimate(
            flops=0, bytes_accessed=4 * total * rows * width, transcendentals=0
        ),
    )(slots, *pieces)
    return whole.reshape(blocks * rows, groups * width)


def disassemble(plan, whole, shard_shape, counts, slots, split_columns):
    total = sum(counts)
    rows, width = shard_shape
    groups = plan.mp if split_columns else 1
    offsets = [sum(counts[:i]) for i in range(len(counts))]
    if rows % 16 and groups > 1 or width % 128:
        if split_columns:
            shards = whole.reshape(plan.dp, rows, plan.mp, width).transpose(0, 2, 1, 3)
        else:
            shards = whole.reshape(plan.mp, plan.dp, rows, width).transpose(1, 0, 2, 3)
        source = shards.reshape(total, rows, width)
        shards = lax.fori_loop(
            0,
            total,
            lambda i, held: lax.dynamic_update_index_in_dim(held, source[slots[i]], i, 0),
            source,
        )
        return [shards[o : o + c] for o, c in zip(offsets, counts)]
    blocks = total // groups

    def kernel(slots_ref, source, *refs):
        outs = refs[: len(counts)]
        held, in_sems, out_sems = refs[len(counts) :]
        steps = [(a, s) for a in range(len(counts)) for s in range(counts[a])]
        reads, writes = [], []
        for i, (a, s) in enumerate(steps):
            block, group = spot_of(slots_ref[i], plan, split_columns)
            columns = pl.ds(pl.multiple_of(group * width, 128), width)
            reads.append(
                pltpu.make_async_copy(source.at[block, :, columns], held.at[i], in_sems.at[i])
            )
            writes.append(pltpu.make_async_copy(held.at[i], outs[a].at[s], out_sems.at[i]))
        for i in range(total):
            reads[i].start()
        for i in range(total):
            reads[i].wait()
            writes[i].start()
        for i in range(total):
            writes[i].wait()

    return pl.pallas_call(
        kernel,
        out_shape=[jax.ShapeDtypeStruct((c, rows, width), whole.dtype) for c in counts],
        grid_spec=pltpu.PrefetchScalarGridSpec(
            num_scalar_prefetch=1,
            grid=(1,),
            in_specs=[ANY],
            out_specs=[ANY] * len(counts),
            scratch_shapes=[
                pltpu.VMEM((total, rows, width), whole.dtype),
                pltpu.SemaphoreType.DMA((total,)),
                pltpu.SemaphoreType.DMA((total,)),
            ],
        ),
        compiler_params=pltpu.CompilerParams(vmem_limit_bytes=VMEM_LIMIT),
        cost_estimate=pl.CostEstimate(
            flops=0, bytes_accessed=4 * total * rows * width, transcendentals=0
        ),
    )(slots, whole.reshape(blocks, rows, groups * width))


PAIR = 2 * HD


def pair_blocks(ref, offset, group, pair, pairs):
    start = group * 3 * pairs * PAIR + pair * PAIR
    span = pairs * PAIR
    return [ref[:, start + part * span : start + part * span + PAIR] for part in range(3)]


def both_heads(block):
    low_lane = lax.broadcasted_iota(jnp.int32, block.shape, 1) < HD
    zero = jnp.zeros_like(block)
    return jnp.concatenate([jnp.where(low_lane, block, zero), jnp.where(low_lane, zero, block)])


def own_columns(stacked):
    rows = stacked.shape[0] // 2
    low_lane = lax.broadcasted_iota(jnp.int32, (rows, PAIR), 1) < HD
    return jnp.where(low_lane, stacked[:rows], stacked[rows:])


def rows_by_rows(left, right):
    return lax.dot_general(left, right, (((1,), (1,)), ((), ())), preferred_element_type=jnp.float32)


def rows_of_both(left, right):
    return lax.dot_general(left, right, (((0,), (0,)), ((), ())), preferred_element_type=jnp.float32)


def pair_probs(stacked_queries, keys, allowed):
    scores = rows_by_rows(keys, stacked_queries) * HD ** (-0.5)
    scores = jnp.where(allowed, scores, masked_score)
    raised = jnp.exp(scores - jnp.max(scores, 0, keepdims=True))
    return raised * (1.0 / jnp.sum(raised, 0, keepdims=True))


def allowed_pairs(column_ref, row_ref):
    same = column_ref[0] == row_ref[0]
    shape = same.shape
    causal = lax.broadcasted_iota(jnp.int32, shape, 0) <= (
        lax.broadcasted_iota(jnp.int32, shape, 1) % LEN
    )
    return same & causal


def attend_kernel(groups, pairs, column_ref, row_ref, qkv_ref, context_ref):
    allowed = allowed_pairs(column_ref, row_ref)
    for group in range(groups):
        for pair in range(pairs):
            queries, keys, values = pair_blocks(qkv_ref, 0, group, pair, pairs)
            probs = pair_probs(both_heads(queries), keys, allowed).astype(jnp.bfloat16)
            context = own_columns(rows_of_both(probs, values))
            start = (group * pairs + pair) * PAIR
            context_ref[:, start : start + PAIR] = context.astype(jnp.bfloat16)


def attend_back_kernel(groups, pairs, column_ref, row_ref, qkv_ref, d_context_ref, d_qkv_ref):
    allowed = allowed_pairs(column_ref, row_ref)
    span = pairs * PAIR
    for group in range(groups):
        for pair in range(pairs):
            queries, keys, values = pair_blocks(qkv_ref, 0, group, pair, pairs)
            start = (group * pairs + pair) * PAIR
            d_context = both_heads(d_context_ref[:, start : start + PAIR])
            queries = both_heads(queries)
            probs = pair_probs(queries, keys, allowed)
            d_probs = rows_by_rows(values, d_context)
            d_values = matmul(probs.astype(jnp.bfloat16), d_context)
            weighted = probs * d_probs
            mean = jnp.sum(weighted, 0, keepdims=True)
            d_scores = (weighted - probs * mean).astype(jnp.bfloat16)
            d_queries = own_columns(rows_of_both(d_scores, keys)) * HD ** (-0.5)
            d_keys = matmul(d_scores, queries) * HD ** (-0.5)
            start = group * 3 * span + pair * PAIR
            for part, value in enumerate((d_queries, d_keys, d_values)):
                at = start + part * span
                d_qkv_ref[:, at : at + PAIR] = value.astype(jnp.bfloat16)


def attend_call(kernel, segments, qkv, others, out_columns, groups, scale):
    count = segments.shape[0]
    columns = qkv.shape[1]
    pairs = columns // (3 * groups * PAIR)
    rows = lambda wide: pl.BlockSpec((LEN, wide), lambda i: (i, 0))
    return pl.pallas_call(
        functools.partial(kernel, groups, pairs),
        out_shape=jax.ShapeDtypeStruct((qkv.shape[0], out_columns), jnp.bfloat16),
        grid=(count,),
        in_specs=[
            pl.BlockSpec((1, LEN, 1), lambda i: (i, 0, 0)),
            pl.BlockSpec((1, 1, 2 * LEN), lambda i: (i, 0, 0)),
            rows(columns),
        ]
        + [rows(other.shape[1]) for other in others],
        out_specs=rows(out_columns),
        compiler_params=pltpu.CompilerParams(vmem_limit_bytes=VMEM_LIMIT),
        cost_estimate=pl.CostEstimate(
            flops=scale * count * 2 * LEN * LEN * columns // 3,
            bytes_accessed=scale * qkv.size * 2,
            transcendentals=count * LEN * LEN * columns // (3 * HD),
        ),
    )(segments[:, :, None], jnp.tile(segments, (1, 2))[:, None, :], qkv, *others)


class Spread:
    def __init__(self, plan, parts, split_columns):
        self.plan, self.parts, self.split_columns = plan, parts, split_columns
        self.pieces = [piece for pieces, _ in parts for piece in pieces]
        self.slots = jnp.concatenate([slots for _, slots in parts])
        self.rows = self.pieces[0].shape[1]
        widths = [pieces[0].shape[2] for pieces, _ in parts]
        self.offsets = [sum(widths[:k]) for k in range(len(widths))]
        self.stride = sum(widths)
        groups = plan.mp if split_columns else 1
        self.shape = (plan.n // groups * self.rows, groups * self.stride)
        self.aligned = self.rows % 16 == 0 and all(width % 128 == 0 for width in widths)

    def matrix(self):
        groups = self.plan.mp if self.split_columns else 1
        wholes = [
            assemble(self.plan, pieces, slots, self.split_columns).reshape(
                self.shape[0], groups, -1
            )
            for pieces, slots in self.parts
        ]
        return jnp.concatenate(wholes, 2).reshape(self.shape)

    def places(self):
        found, first = [], 0
        for (pieces, _), offset in zip(self.parts, self.offsets):
            for k, piece in enumerate(pieces):
                found = found + [(first + k, slot, offset) for slot in range(piece.shape[0])]
            first = first + len(pieces)
        return found


def spot_slice(matrix_ref, plan, device, rows, width, split_columns, offset, stride):
    block, group = spot_of(device, plan, split_columns)
    at_rows = pl.ds(pl.multiple_of(block * rows, rows), rows)
    start = offset if isinstance(group, int) else pl.multiple_of(group * stride + offset, 128)
    return matrix_ref.at[at_rows, pl.ds(start, width)]


def with_matrices(plan, body, spreads, operands, outs, steps, flops):
    sizes = [len(spread.pieces) for spread in spreads]
    total = sum(spread.slots.shape[0] for spread in spreads)

    def kernel(slots_ref, *refs):
        inputs, refs = refs[: len(operands)], refs[len(operands) :]
        sources, refs = refs[: sum(sizes)], refs[sum(sizes) :]
        results, refs = refs[: len(outs)], refs[len(outs) :]
        kept, refs = refs[: len(spreads)], refs[len(spreads) :]
        matrices, sems, kept_sems = refs[: len(spreads)], refs[len(spreads)], refs[len(spreads) + 1]
        keeps = [
            pltpu.make_async_copy(matrix, out, kept_sems.at[k])
            for k, (matrix, out) in enumerate(zip(matrices, kept))
        ]

        @pl.when(pl.program_id(0) == 0)
        def _():
            copies, first = [], 0
            for spread, matrix in zip(spreads, matrices):
                for which, slot, offset in spread.places():
                    i = len(copies)
                    spot = spot_slice(
                        matrix,
                        plan,
                        slots_ref[i],
                        spread.rows,
                        spread.pieces[which].shape[2],
                        spread.split_columns,
                        offset,
                        spread.stride,
                    )
                    source = sources[first + which].at[slot]
                    copies.append(pltpu.make_async_copy(source, spot, sems.at[i]))
                    copies[-1].start()
                first = first + len(spread.pieces)
            for copy in copies:
                copy.wait()
            for keep in keeps:
                keep.start()

        body(inputs, matrices, results)

        @pl.when(pl.program_id(0) == pl.num_programs(0) - 1)
        def _():
            for keep in keeps:
                keep.wait()

    moved_bytes = sum(2 * spread.shape[0] * spread.shape[1] for spread in spreads)
    moved_bytes += sum(array.size * array.dtype.itemsize for array, _, _ in operands)
    moved_bytes += sum(np.prod(shape) * np.dtype(dtype).itemsize for shape, dtype, _, _ in outs)
    return pl.pallas_call(
        kernel,
        out_shape=[jax.ShapeDtypeStruct(shape, dtype) for shape, dtype, _, _ in outs]
        + [jax.ShapeDtypeStruct(spread.shape, jnp.bfloat16) for spread in spreads],
        grid_spec=pltpu.PrefetchScalarGridSpec(
            num_scalar_prefetch=1,
            grid=(steps,),
            in_specs=[pl.BlockSpec(block, index) for _, block, index in operands]
            + [ANY] * sum(sizes),
            out_specs=[pl.BlockSpec(block, index) for _, _, block, index in outs]
            + [ANY] * len(spreads),
            scratch_shapes=[pltpu.VMEM(spread.shape, jnp.bfloat16) for spread in spreads]
            + [
                pltpu.SemaphoreType.DMA((total,)),
                pltpu.SemaphoreType.DMA((len(spreads),)),
            ],
        ),
        compiler_params=pltpu.CompilerParams(vmem_limit_bytes=VMEM_LIMIT),
        cost_estimate=pl.CostEstimate(
            flops=flops, bytes_accessed=int(moved_bytes), transcendentals=0
        ),
    )(
        jnp.concatenate([spread.slots for spread in spreads]),
        *[array for array, _, _ in operands],
        *[piece for spread in spreads for piece in spread.pieces],
    )


def fixed(step, *scalars):
    return (0, 0)


def by_columns(step, *scalars):
    return (0, step)


def by_rows(step, *scalars):
    return (step, 0)


def step_slice(size):
    return pl.ds(pl.multiple_of(pl.program_id(0) * size, size), size)


def project(rows, spread, block):
    count, deep = rows.shape
    wide = spread.shape[1]
    if not spread.aligned or wide % block:
        whole = spread.matrix()
        return matmul(rows, whole).astype(jnp.bfloat16), whole

    def body(inputs, matrices, results):
        product = matmul(inputs[0][...], matrices[0][:, step_slice(block)])
        results[0][...] = product.astype(jnp.bfloat16)

    return with_matrices(
        spread.plan,
        body,
        [spread],
        [(rows, (count, deep), fixed)],
        [((count, wide), jnp.bfloat16, (count, block), by_columns)],
        wide // block,
        2 * count * deep * wide,
    )


def by_blocks(body, operands, outs, steps, flops):
    moved_bytes = sum(array.size * array.dtype.itemsize for array, _, _ in operands)
    moved_bytes += sum(np.prod(shape) * np.dtype(dtype).itemsize for shape, dtype, _, _ in outs)
    return pl.pallas_call(
        body,
        out_shape=[jax.ShapeDtypeStruct(shape, dtype) for shape, dtype, _, _ in outs],
        grid=(steps,),
        in_specs=[
            pl.BlockSpec(block, index, pipeline_mode=pl.Buffered(1 if index is fixed else 2))
            for _, block, index in operands
        ],
        out_specs=[pl.BlockSpec(block, index) for _, _, block, index in outs],
        compiler_params=pltpu.CompilerParams(vmem_limit_bytes=VMEM_LIMIT),
        cost_estimate=pl.CostEstimate(
            flops=flops, bytes_accessed=int(moved_bytes), transcendentals=0
        ),
    )(*[array for array, _, _ in operands])


def project_back(rows, matrix, block):
    count, deep = rows.shape
    wide = matrix.shape[0]
    if wide % block:
        return matmul_t(rows, matrix)

    def body(rows_ref, matrix_ref, out_ref):
        out_ref[...] = rows_by_rows(rows_ref[...], matrix_ref[...])

    return by_blocks(
        body,
        [(rows, (count, deep), fixed), (matrix, (block, deep), by_rows)],
        [((count, wide), jnp.float32, (count, block), by_columns)],
        wide // block,
        2 * count * deep * wide,
    )[0]


def gelu_and_slope(value):
    scale, cubic = (2.0 / np.pi) ** 0.5, 0.044715
    square = value * value
    bent = jnp.tanh(value * (scale + scale * cubic * square))
    half = 0.5 * bent + 0.5
    inner = value * (scale + 3.0 * scale * cubic * square)
    return value * half, half + (0.5 - 0.5 * bent * bent) * inner


def hidden_forward(rows, spread, block):
    count, deep = rows.shape
    wide = spread.shape[1]
    if not spread.aligned or wide % block:
        whole = spread.matrix()
        gelu, slope = gelu_and_slope(matmul(rows, whole))
        return gelu.astype(jnp.bfloat16), slope.astype(jnp.bfloat16), whole

    def body(inputs, matrices, results):
        up_pre = matmul(inputs[0][...], matrices[0][:, step_slice(block)])
        gelu, slope = gelu_and_slope(up_pre)
        results[0][...] = gelu.astype(jnp.bfloat16)
        results[1][...] = slope.astype(jnp.bfloat16)

    return with_matrices(
        spread.plan,
        body,
        [spread],
        [(rows, (count, deep), fixed)],
        [((count, wide), jnp.bfloat16, (count, block), by_columns)] * 2,
        wide // block,
        2 * count * deep * wide,
    )


def hidden_back(d_out, slope, matrix, block):
    count, wide = slope.shape
    if wide % block:
        d_activated = matmul_t(d_out, matrix)
        return (d_activated * slope.astype(jnp.float32)).astype(jnp.bfloat16)

    def body(d_out_ref, matrix_ref, slope_ref, out_ref):
        d_activated = rows_by_rows(d_out_ref[...], matrix_ref[...])
        out_ref[...] = (d_activated * slope_ref[...].astype(jnp.float32)).astype(jnp.bfloat16)

    return by_blocks(
        body,
        [
            (d_out, d_out.shape, fixed),
            (matrix, (block, d_out.shape[1]), by_rows),
            (slope, (count, block), by_columns),
        ],
        [((count, wide), jnp.bfloat16, (count, block), by_columns)],
        wide // block,
        2 * count * d_out.shape[1] * wide,
    )[0]


def heads_and_back(after, head, gain, shift, scales, targets):
    centred = after - jnp.mean(after, -1, keepdims=True)
    inverse = lax.rsqrt(jnp.mean(centred * centred, -1, keepdims=True) + norm_eps)
    unit = centred * inverse
    final = (unit * gain + shift).astype(jnp.bfloat16)
    logits = rows_by_rows(final, head)
    lane = lax.broadcasted_iota(jnp.int32, logits.shape, 1)
    edges = (0, RB, RB + AB, RB + AB + WB)
    inside = [(lane >= edges[k]) & (lane < edges[k + 1]) for k in range(3)]
    tops = [
        jnp.max(jnp.where(mask, logits, masked_score), -1, keepdims=True) for mask in inside
    ]

    def spread_over(columns, other):
        value = jnp.where(inside[2], columns[2], other)
        return jnp.where(inside[0], columns[0], jnp.where(inside[1], columns[1], value))

    lowered = spread_over([logits - top for top in tops], masked_score)
    raised = jnp.exp(lowered)
    totals = [jnp.sum(jnp.where(mask, raised, 0.0), -1, keepdims=True) for mask in inside]
    picked = [lane == targets[:, k : k + 1] for k in range(3)]
    loss = jnp.float32(0.0)
    for k in range(3):
        found = jnp.sum(jnp.where(picked[k], lowered, 0.0), -1, keepdims=True)
        loss = loss + jnp.sum(scales[:, k : k + 1] * (jnp.log(totals[k]) - found))
    hot = jnp.where(picked[0] | picked[1] | picked[2], 1.0, 0.0)
    shares = raised * spread_over([1.0 / total for total in totals], 0.0) - hot
    d_logits = (shares * spread_over([scales[:, k : k + 1] for k in range(3)], 0.0)).astype(
        jnp.bfloat16
    )
    d_unit = matmul(d_logits, head) * gain
    leaning = jnp.mean(d_unit * unit, -1, keepdims=True)
    d_after = inverse * (d_unit - jnp.mean(d_unit, -1, keepdims=True) - unit * leaning)
    return final, d_logits, loss, d_after


def context_back(d_up_pre, up, after, gain, d_later, exit_all, block):
    count, deep = d_up_pre.shape
    wide = up.shape[0]
    rows = (block, wide)

    def body(d_up_ref, up_ref, after_ref, gain_ref, later_ref, exit_ref, *outs):
        d_normed = rows_by_rows(d_up_ref[...], up_ref[...])
        outs[0][...] = d_normed
        after_rows = after_ref[...]
        centred = after_rows - jnp.mean(after_rows, -1, keepdims=True)
        inverse = lax.rsqrt(jnp.mean(centred * centred, -1, keepdims=True) + norm_eps)
        unit = centred * inverse
        d_unit = d_normed * gain_ref[...]
        leaning = jnp.mean(d_unit * unit, -1, keepdims=True)
        d_norm = inverse * (d_unit - jnp.mean(d_unit, -1, keepdims=True) - unit * leaning)
        d_out = (later_ref[...] + d_norm).astype(jnp.bfloat16)
        outs[1][...] = d_out
        outs[2][...] = rows_by_rows(d_out, exit_ref[...]).astype(jnp.bfloat16)

    return by_blocks(
        body,
        [
            (d_up_pre, (block, deep), by_rows),
            (up, up.shape, fixed),
            (after, rows, by_rows),
            (gain, gain.shape, fixed),
            (d_later, rows, by_rows),
            (exit_all, exit_all.shape, fixed),
        ],
        [
            ((count, wide), jnp.float32, rows, by_rows),
            ((count, wide), jnp.bfloat16, rows, by_rows),
            ((count, wide), jnp.bfloat16, rows, by_rows),
        ],
        count // block,
        2 * count * wide * (deep + wide),
    )


def hidden_out(activated, base, spread, head, gain, shift, scales, targets, block):
    count, deep = activated.shape
    wide = base.shape[1]
    lanes = head.shape[0]
    if not spread.aligned or count % block:
        whole = spread.matrix()
        after = base + matmul(activated, whole)
        final, d_logits, loss, d_after = heads_and_back(after, head, gain, shift, scales, targets)
        return after, final, d_logits, d_after, d_after.astype(jnp.bfloat16), loss[None], whole

    def body(inputs, matrices, results):
        after = inputs[1][...] + matmul(inputs[0][...], matrices[0][...])
        results[0][...] = after
        final, d_logits, loss, d_after = heads_and_back(
            after,
            inputs[2][...],
            inputs[3][...],
            inputs[4][...],
            inputs[5][...],
            inputs[6][...],
        )
        results[1][...] = final
        results[2][...] = d_logits
        results[3][...] = d_after
        results[4][...] = d_after.astype(jnp.bfloat16)
        results[5][...] = jnp.full(results[5].shape, loss)

    rows = (block, wide)
    return with_matrices(
        spread.plan,
        body,
        [spread],
        [
            (activated, (block, deep), by_rows),
            (base, rows, by_rows),
            (head, head.shape, fixed),
            (gain, gain.shape, fixed),
            (shift, shift.shape, fixed),
            (scales, (block, 3), by_rows),
            (targets, (block, 3), by_rows),
        ],
        [
            ((count, wide), jnp.float32, rows, by_rows),
            ((count, wide), jnp.bfloat16, rows, by_rows),
            ((count, lanes), jnp.bfloat16, (block, lanes), by_rows),
            ((count, wide), jnp.float32, rows, by_rows),
            ((count, wide), jnp.bfloat16, rows, by_rows),
            ((8 * (count // block), 128), jnp.float32, (8, 128), by_rows),
        ],
        count // block,
        2 * count * deep * wide,
    )


def weight_grad(plan, left, right, rows, parts, split_columns, block):
    tokens, high = left.shape
    wide = right.shape[1]
    groups = plan.mp if split_columns else 1
    stride = wide // groups
    along = wide if split_columns else high
    unit = stride if split_columns else rows
    widths = [width for width, _, _ in parts]
    offsets = [sum(widths[:k]) for k in range(len(parts))]
    fits = along % block == 0 and (block % unit == 0 or unit % block == 0)
    if rows % 16 or any(width % 128 for width in widths) or not fits:
        whole = contract(left, right).astype(jnp.bfloat16).reshape(high, groups, stride)
        found = []
        for (width, counts, slots), offset in zip(parts, offsets):
            part = whole[:, :, offset : offset + width].reshape(high, groups * width)
            found.append(disassemble(plan, part, (rows, width), counts, slots, split_columns))
        return found
    tile = 256 if split_columns else block
    outs_of = [(width, count) for width, counts, _ in parts for count in counts]
    places = [
        (width, offset, slot)
        for (width, counts, _), offset in zip(parts, offsets)
        for count in counts
        for slot in range(count)
    ]

    def kernel(slots_ref, left_ref, right_ref, *refs):
        outs, gradient, sems = refs[: len(outs_of)], refs[len(outs_of)], refs[len(outs_of) + 1]
        step = pl.program_id(0)
        for start in range(0, high if split_columns else block, tile):
            lefts = left_ref[:, start : start + tile]
            product = rows_of_both(lefts, right_ref[...]).astype(jnp.bfloat16)
            if split_columns:
                gradient[start : start + tile, step_slice(block)] = product
            else:
                gradient[step_slice(block), :] = product
        targets = [out.at[slot] for out, (_, count) in zip(outs, outs_of) for slot in range(count)]
        copies = []
        for i, (width, offset, _) in enumerate(places):
            spot = spot_slice(
                gradient, plan, slots_ref[i], rows, width, split_columns, offset, stride
            )
            copies.append(pltpu.make_async_copy(spot, targets[i], sems.at[i]))
        for i, (width, offset, _) in enumerate(places):
            row_block, group = spot_of(slots_ref[i], plan, split_columns)
            if split_columns:
                done_in = (group * stride + offset + width - 1) // block
            else:
                done_in = (row_block * rows) // block

            @pl.when(done_in == step)
            def _(copy=copies[i]):
                copy.start()

        @pl.when(step == pl.num_programs(0) - 1)
        def _():
            for copy in copies:
                copy.wait()

    if split_columns:
        left_spec = pl.BlockSpec((tokens, high), fixed)
        right_spec = pl.BlockSpec((tokens, block), by_columns)
    else:
        left_spec = pl.BlockSpec((tokens, block), by_columns)
        right_spec = pl.BlockSpec((tokens, wide), fixed)
    flat = pl.pallas_call(
        kernel,
        out_shape=[
            jax.ShapeDtypeStruct((count, rows, width), jnp.bfloat16) for width, count in outs_of
        ],
        grid_spec=pltpu.PrefetchScalarGridSpec(
            num_scalar_prefetch=1,
            grid=(along // block,),
            in_specs=[left_spec, right_spec],
            out_specs=[ANY] * len(outs_of),
            scratch_shapes=[
                pltpu.VMEM((high, wide), jnp.bfloat16),
                pltpu.SemaphoreType.DMA((len(places),)),
            ],
        ),
        compiler_params=pltpu.CompilerParams(vmem_limit_bytes=VMEM_LIMIT),
        cost_estimate=pl.CostEstimate(
            flops=2 * tokens * high * wide,
            bytes_accessed=2 * (tokens * (high + wide) + high * wide),
            transcendentals=0,
        ),
    )(jnp.concatenate([slots for _, _, slots in parts]), left, right)
    found = []
    for _, counts, _ in parts:
        found.append(flat[: len(counts)])
        flat = flat[len(counts) :]
    return found


def adam_step(first, root, clipped, corr_first, corr_second):
    first = beta_first * first + (1.0 - beta_first) * clipped
    second = beta_second * root * root + (1.0 - beta_second) * clipped * clipped
    direction = first / corr_first / (jnp.sqrt(second / corr_second) + adam_eps)
    return first, jnp.sqrt(second), direction


def views(matrix, columns):
    width = matrix.shape[-1]
    if len(matrix.shape) == 3:
        return [((k,), 0, width) for k in range(matrix.shape[0])]
    starts = [sum(columns[:k]) for k in range(len(columns))]
    return [((), start, size) for start, size in zip(starts, columns)]


LOSS, SQUARE, WEIGHTS, GRAD_NORM = 0, 1, 2, 5


def number_at(row, place):
    lane = lax.broadcasted_iota(jnp.int32, row.shape, 1)
    return jnp.sum(jnp.where(lane == place, row, 0.0), keepdims=True)


def row_of(numbers):
    lane = lax.broadcasted_iota(jnp.int32, (1, 128), 1)
    row = jnp.zeros((1, 128), jnp.float32)
    for place, number in numbers.items():
        row = jnp.where(lane == place, number, row)
    return row


def moments_and_directions(corrections, small, gradients, states, masters, norms):
    count = len(masters)
    flat = [part for parts in gradients for part in parts]
    smem = pl.BlockSpec(memory_space=pltpu.SMEM)
    vmem = pl.BlockSpec(memory_space=pltpu.VMEM)

    def kernel(corrections_ref, small_ref, *refs):
        parts, refs = list(refs[: len(flat)]), refs[len(flat) :]
        old, weights, refs = refs[:count], refs[count : 2 * count], refs[2 * count :]
        (norm_old, norm_weight), refs = refs[:2], refs[2:]
        fresh, ways, refs = refs[:count], refs[count : 2 * count], refs[2 * count :]
        norm_fresh, norm_out, row_ref = refs
        corr_first, corr_second = corrections_ref[0], corrections_ref[1]
        head_grad, norm_grad = parts[-1][...], small_ref[:6]
        square = number_at(small_ref[6:7], SQUARE)
        square = square + jnp.sum(head_grad * head_grad, keepdims=True)
        grad_norm = jnp.sqrt(square + jnp.sum(norm_grad * norm_grad, keepdims=True))
        clip = jnp.minimum(1.0, clip_limit / grad_norm)
        numbers = {GRAD_NORM: grad_norm}
        for k in range(count):
            mine = [parts.pop(0) for _ in gradients[k]]
            total = jnp.zeros((1, 1), jnp.float32)
            for which, (lead, start, width) in enumerate(
                views(masters[k], [part.shape[1] for part in gradients[k]])
            ):
                columns = slice(start, start + width)
                if lead:
                    gradient = mine[0][:, which * width : (which + 1) * width]
                else:
                    gradient = mine[which][...]
                spot = lead + (slice(None), columns)
                first, root, direction = adam_step(
                    old[k][(0,) + spot],
                    old[k][(1,) + spot],
                    clip * gradient,
                    corr_first,
                    corr_second,
                )
                if k < count - 1:
                    fresh[k][(0,) + spot] = first
                    fresh[k][(1,) + spot] = root
                else:
                    fresh[k][:, 0, :] = first
                    fresh[k][:, 1, :] = root
                direction = direction + weight_decay * weights[k][spot]
                ways[k][spot] = direction
                total = total + jnp.sum(direction * direction, keepdims=True)
            numbers[k] = total
        first, root, direction = adam_step(
            norm_old[0], norm_old[1], clip * norm_grad, corr_first, corr_second
        )
        norm_fresh[0] = first
        norm_fresh[1] = root
        norm_out[...] = norm_weight[...] - learn_rate * direction
        row_ref[...] = row_of(numbers)

    like = lambda value: jax.ShapeDtypeStruct(value.shape, jnp.float32)
    head_rows, wide = masters[-1].shape
    found = pl.pallas_call(
        kernel,
        out_shape=[like(state) for state in states[:-1]]
        + [jax.ShapeDtypeStruct((head_rows, 2, wide), jnp.float32)]
        + [like(master) for master in masters]
        + [like(norms[0]), like(norms[1]), jax.ShapeDtypeStruct((1, 128), jnp.float32)],
        in_specs=[smem] + [vmem] * (len(flat) + 2 * count + 3),
        out_specs=[vmem] * (2 * count + 3),
        compiler_params=pltpu.CompilerParams(vmem_limit_bytes=VMEM_LIMIT),
    )(corrections, small, *flat, *states, *masters, *norms)
    fresh = list(found[: count - 1]) + [found[count - 1].transpose(1, 0, 2)]
    return fresh, found[count : 2 * count], *found[2 * count :]


def new_weights(head_square, small, row, summed, masters, directions):
    count = len(masters)
    smem = pl.BlockSpec(memory_space=pltpu.SMEM)
    vmem = pl.BlockSpec(memory_space=pltpu.VMEM)

    def kernel(head_ref, small_ref, row_ref, summed_ref, *refs):
        weights, ways, refs = refs[:count], refs[count : 2 * count], refs[2 * count :]
        weight_norms, update_norms = {}, {}
        for k in range(count):
            if k < count - 1:
                weight_norms[k] = jnp.sqrt(number_at(small_ref[6:7], WEIGHTS + k))
                update_norms[k] = jnp.sqrt(number_at(summed_ref[...], k))
            else:
                weight_norms[k] = jnp.sqrt(jnp.full((1, 1), head_ref[0]))
                update_norms[k] = jnp.sqrt(number_at(row_ref[...], k))
            step = learn_rate * (weight_norms[k] / update_norms[k])
            value = weights[k][...] - step * ways[k][...]
            refs[k][...] = value
            if k < count - 1:
                refs[count + k][...] = value.astype(jnp.bfloat16)
        refs[-1][0:1] = row_of(weight_norms)
        refs[-1][1:2] = row_of(update_norms)

    found = pl.pallas_call(
        kernel,
        out_shape=[jax.ShapeDtypeStruct(master.shape, jnp.float32) for master in masters]
        + [jax.ShapeDtypeStruct(master.shape, jnp.bfloat16) for master in masters[:-1]]
        + [jax.ShapeDtypeStruct((2, 128), jnp.float32)],
        in_specs=[smem] + [vmem] * (3 + 2 * count),
        out_specs=[vmem] * (2 * count),
        compiler_params=pltpu.CompilerParams(vmem_limit_bytes=VMEM_LIMIT),
    )(head_square, small, row, summed, *masters, *directions)
    return found[:count], found[count:-1], found[-1]


BY_COLUMNS = ("entry", "up")
SPLITS = {"up": ((0, 1), (2,)), "down": ((0, 1), (2,))}


def per_device(
    plan,
    tokens,
    segment_ids,
    game_ids,
    return_bins,
    action_bins,
    reward_bins,
    valid_flags,
    step_count,
    entry_weight,
    entry_state,
    exit_weight,
    exit_state,
    up_weight,
    up_state,
    down_weight,
    down_state,
    head_weight,
    head_state,
    norm_params,
    norm_state,
):
    own_rows = tokens.shape[0]
    here = lax.axis_index("dp") * plan.mp + lax.axis_index("mp")
    row_start = lax.axis_index("mp") * own_rows
    own_seqs = own_rows // LEN
    segments = lax.dynamic_slice_in_dim(segment_ids, lax.axis_index("mp") * own_seqs, own_seqs)
    row_games = lax.dynamic_slice_in_dim(jnp.repeat(game_ids, LEN), row_start, own_rows)

    clock = Clock(step_count.astype(jnp.float32))
    masters = {"entry": entry_weight, "exit": exit_weight, "up": up_weight, "down": down_weight}
    rows_here, half_wide = entry_weight.shape[1:]
    halves = {name: value.astype(jnp.bfloat16) for name, value in masters.items()}
    entry_shard = halves["entry"].transpose(1, 0, 2).reshape(rows_here, 3 * half_wide)
    paths = {
        name: Travel("gather_" + name, gather_shards(plan, shard, split))
        for name, shard, split in (
            ("entry", entry_shard, ()),
            ("up", halves["up"], ((0, 1), (2,))),
            ("down", halves["down"], ((0, 1), (2,))),
        )
    }
    game_match = (row_games[:, None] == jnp.arange(GAMES)[None, :]).astype(jnp.float32)
    flag_float = valid_flags.astype(jnp.float32)
    local_counts = jnp.sum(game_match * jnp.sum(flag_float, -1, keepdims=True), 0)
    exit_rows, wide = exit_weight.shape
    tens = jnp.floor(local_counts / 64.0)
    pair = jnp.concatenate([tens, local_counts - 64.0 * tens]).astype(jnp.bfloat16)
    below = jnp.zeros((16 - exit_rows % 16, wide), jnp.bfloat16).at[0, : 2 * GAMES].set(pair)
    exit_shard = jnp.concatenate([halves["exit"], below])
    slots = jnp.asarray(path_table(plan), jnp.int32)[here]

    def chosen(names):
        return [paths[name] for name in names.split() if paths[name].wanted]

    def start(names, *more):
        return clock.start(chosen(names), more)

    def wait(names, *more):
        return clock.wait([path for path in chosen(names) if path.going], more)

    def finish(name):
        while paths[name].wanted:
            start(name)
            wait(name)
        return paths[name].result

    def whole(name):
        return Spread(plan, [(finish(name), slots)], name in BY_COLUMNS)


    resid, gains = start("entry", tokens.astype(jnp.float32), norm_params)
    normed_one = layer_norm(resid, gains[0], gains[3]).astype(jnp.bfloat16)
    (normed_one,) = wait("entry", normed_one)
    (exit_shard,) = start("entry up", exit_shard)
    gathered = lax.all_gather(exit_shard, ("mp", "dp"), axis=0)
    exit_all = gathered[:, :exit_rows].reshape(-1, wide)
    pairs_all = jnp.sum(gathered[:, exit_rows, : 2 * GAMES].astype(jnp.float32), 0)
    counts_all = 64.0 * pairs_all[:GAMES] + pairs_all[GAMES:]
    inverse = 1.0 / (GAMES * jnp.maximum(counts_all, 1.0))
    token_scale = jnp.sum(game_match * inverse[None, :], -1)
    wait("entry up")
    start("entry up")
    wait("entry up")
    start("entry up")
    wait("entry")
    (normed_one,) = start("down", normed_one)
    projected, entry_all = project(normed_one, whole("entry"), 768)
    (projected,) = wait("up down", projected)
    (projected,) = start("up down", projected)
    context = attend_call(
        attend_kernel, segments, projected, [], tokens.shape[1], plan.mp, 2
    )
    after_attn = resid + matmul(context, exit_all)
    normed_two = layer_norm(after_attn, norm_params[1], norm_params[4]).astype(jnp.bfloat16)
    after_attn, normed_two = wait("up down", after_attn, normed_two)
    (normed_two,) = start("up down", normed_two)
    wait("up")
    (normed_two,) = start("", normed_two)
    activated, slope, up_all = hidden_forward(normed_two, whole("up"), 512)
    activated, slope = wait("down", activated, slope)
    head_rows = head_weight.shape[0]
    head_half = jnp.pad(head_weight.astype(jnp.bfloat16), ((0, -head_rows % 128), (0, 0)))
    targets = jnp.stack([return_bins, action_bins + RB, reward_bins + (RB + AB)], 1)
    scales = flag_float * token_scale[:, None]
    late = start("down", *masters.values())
    weight_local = jnp.stack([jnp.sum(master * master) for master in late])
    weight_local, head_half, targets, scales = wait(
        "down", weight_local, head_half, targets, scales
    )
    start("down")
    wait("down")
    after_mlp, final_norm, d_logits, d_mlp_in, d_mlp_out, losses, down_all = hidden_out(
        activated,
        after_attn,
        whole("down"),
        head_half,
        norm_params[2:3],
        norm_params[5:6],
        scales,
        targets,
        320,
    )
    loss_local = jnp.sum(losses.reshape(-1, 8, 128)[:, 0, 0]) if losses.ndim > 1 else losses[0]

    def leave(names, left, right, rows, widths, block):
        by_columns = names.split()[0] in ("entry_a", "up")
        parts = [(width, scatter_counts(plan), slots) for width in widths]
        found = weight_grad(plan, left, right, rows, parts, by_columns, block)
        for name, pieces in zip(names.split(), found):
            steps = scatter_shards(plan, pieces, SPLITS.get(name, ()), name == "up")
            paths[name] = Travel("scatter_" + name, steps)

    down_rows = down_weight.shape[0]
    entry_widths = (3 * half_wide * 8 // 15, 3 * half_wide - 3 * half_wide * 8 // 15)
    leave("down", activated, d_mlp_out, down_rows, [wide], 1280)
    d_head = contract(d_logits, final_norm)[: head_rows + head_rows % 2]
    paths["head"] = Travel("sum_head", total_steps(plan, d_head, halves=True))
    (d_mlp_out,) = start("down head", d_mlp_out)
    d_up_pre = hidden_back(d_mlp_out, slope, down_all, 512)
    (d_up_pre,) = wait("down head", d_up_pre)
    (d_up_pre,) = start("down head", d_up_pre)
    leave("up", normed_two, d_up_pre, rows_here, [up_weight.shape[1]], 2560)
    (d_up_pre,) = wait("down head", d_up_pre)
    (d_up_pre,) = start("down up head", d_up_pre)
    d_normed_two, d_attn_out, d_context = context_back(
        d_up_pre, up_all, after_attn, norm_params[1:2], d_mlp_in, exit_all, 320
    )
    leave("exit", context, d_attn_out, exit_rows, [wide], 1280)
    (d_context,) = wait("down up head", d_context)
    (d_context,) = start("down up exit", d_context)
    d_projected = attend_call(
        attend_back_kernel, segments, projected, [d_context], projected.shape[1], plan.mp, 5
    )
    (d_projected,) = wait("down up exit", d_projected)
    (d_projected,) = start("up down exit", d_projected)
    leave("entry_a entry_b", normed_one, d_projected, rows_here, entry_widths, 1920)
    (d_projected,) = wait("up down exit", d_projected)
    (d_projected,) = start("up entry_a entry_b", d_projected)
    d_normed_one = project_back(d_projected, entry_all, 256)
    reds = {"down": finish("down")}
    (d_normed_one,) = wait("up entry_a entry_b", d_normed_one)
    d_normed_one, reds = start("entry_a entry_b up head", d_normed_one, reds)
    down_square = jnp.sum(reds["down"] * reds["down"])
    _, d_gain_one, d_shift_one = norm_back(resid, norm_params[0], norm_params[3], d_normed_one)
    d_gain_one, d_shift_one, reds, down_square = wait(
        "entry_a entry_b up head", d_gain_one, d_shift_one, reds, down_square
    )
    late = start("entry_a up exit", after_mlp, d_logits, after_attn, d_normed_two)
    d_final = matmul(late[1], head_half)
    _, d_gain_three, d_shift_three = norm_back(late[0], norm_params[2], norm_params[5], d_final)
    _, d_gain_two, d_shift_two = norm_back(late[2], norm_params[1], norm_params[4], late[3])
    late = wait("entry_a up exit", d_gain_two, d_shift_two, d_gain_three, d_shift_three)
    d_gain_two, d_shift_two, d_gain_three, d_shift_three = late
    start("entry_b entry_a head")
    reds["up"] = finish("up")
    up_square = jnp.sum(reds["up"] * reds["up"])
    reds, up_square = wait("entry_b entry_a head", reds, up_square)
    start("entry_b exit head")
    reds["entry_a"] = finish("entry_a")
    entry_square = jnp.sum(reds["entry_a"] * reds["entry_a"])
    reds, entry_square = wait("entry_b exit head", reds, entry_square)
    reds["exit"] = finish("exit")
    exit_square = jnp.sum(reds["exit"] * reds["exit"])
    red_head = finish("head")[:head_rows]
    reds["entry_b"] = finish("entry_b")
    local_square = down_square + up_square + exit_square + entry_square
    local_square = local_square + jnp.sum(reds["entry_b"] * reds["entry_b"])
    masters = [entry_weight, exit_weight, up_weight, down_weight, head_weight]
    states = [entry_state, exit_state, up_state, down_state, head_state]
    wide = norm_params.shape[1]
    scalars = jnp.concatenate(
        [jnp.stack([loss_local, local_square]), weight_local, clock.token]
    )
    small, _ = total_over_devices(
        plan,
        jnp.stack(
            [
                d_gain_one,
                d_gain_two,
                d_gain_three,
                d_shift_one,
                d_shift_two,
                d_shift_three,
                jnp.pad(scalars, (0, wide - scalars.shape[0])),
            ]
        ),
    )
    step_float = step_count.astype(jnp.float32)
    corrections = jnp.concatenate(
        [1.0 - jnp.power(beta_first, step_float), 1.0 - jnp.power(beta_second, step_float)]
    )
    gradients = [
        [jnp.concatenate([reds["entry_a"], reds["entry_b"]], 1)],
        [reds["exit"]],
        [reds["up"]],
        [reds["down"]],
        [red_head],
    ]
    moments, directions, norm_moments, norm_new, row = moments_and_directions(
        corrections, small, gradients, states, masters, (norm_state, norm_params)
    )
    summed, late = total_over_devices(plan, row, (moments[4], norm_moments))
    moments[4], norm_moments = late
    new, rounded, norms = new_weights(
        jnp.sum(head_weight * head_weight)[None], small, row, summed, masters, directions
    )
    loss_sum, grad_norm, matrix_norms = small[6, LOSS], row[0, GRAD_NORM], norms[:, :5]
    return (
        new[0],
        moments[0],
        rounded[0],
        new[1],
        moments[1],
        rounded[1],
        new[2],
        moments[2],
        rounded[2],
        new[3],
        moments[3],
        rounded[3],
        new[4],
        moments[4],
        norm_new,
        norm_moments,
        loss_sum,
        grad_norm,
        matrix_norms,
    )


def solution(mesh):
    in_specs = (
        P(("dp", "mp"), None),
        P("dp", None),
        P("dp"),
        P(("dp", "mp")),
        P(("dp", "mp")),
        P(("dp", "mp")),
        P(("dp", "mp"), None),
        P(),
        P(None, "dp", "mp"),
        P(None, None, "dp", "mp"),
        P(("mp", "dp"), None),
        P(None, ("mp", "dp"), None),
        P("dp", "mp"),
        P(None, "dp", "mp"),
        P(("mp", "dp"), None),
        P(None, ("mp", "dp"), None),
        P(),
        P(),
        P(),
        P(),
    )
    out_specs = (
        P(None, "dp", "mp"),
        P(None, None, "dp", "mp"),
        P(None, "dp", "mp"),
        P(("mp", "dp"), None),
        P(None, ("mp", "dp"), None),
        P(("mp", "dp"), None),
        P("dp", "mp"),
        P(None, "dp", "mp"),
        P("dp", "mp"),
        P(("mp", "dp"), None),
        P(None, ("mp", "dp"), None),
        P(("mp", "dp"), None),
        P(),
        P(),
        P(),
        P(),
        P(),
        P(),
        P(),
    )
    plan = Plan(mesh.shape["dp"], mesh.shape["mp"])
    return jax.shard_map(
        functools.partial(per_device, plan), mesh=mesh, in_specs=in_specs, out_specs=out_specs, check_vma=False
    )
```

```python
import functools

import jax
import jax.numpy as jnp
import numpy as np
from jax import lax
from jax.experimental import pallas as pl
from jax.experimental.pallas import tpu as pltpu
from jax.sharding import PartitionSpec as P

HD = 64
RB = 120
AB = 18
WB = 4
GAMES = 41
LEN = 160


clip_limit = 0.05
learn_rate = 0.5
beta_first = 0.5
beta_second = 0.5
weight_decay = 0.01
adam_eps = 1e-08
norm_eps = 1e-05
masked_score = -1e30


def layer_norm(rows, gain, shift):
    centred = rows - jnp.mean(rows, -1, keepdims=True)
    spread = jnp.mean(centred * centred, -1, keepdims=True)
    return centred * lax.rsqrt(spread + norm_eps) * gain + shift


def norm_back(rows, gain, shift, upstream):
    _, pullback = jax.vjp(layer_norm, rows, gain, shift)
    return pullback(upstream)


def matmul(left, right):
    return jnp.dot(left, right, preferred_element_type=jnp.float32)


def matmul_t(left, right):
    return jnp.einsum("ti,ji->tj", left, right, preferred_element_type=jnp.float32)


def contract(left, right):
    return jnp.einsum("ti,tj->ij", left, right, preferred_element_type=jnp.float32)


AXES = ("dp", "mp")
VMEM_LIMIT = 60 * 2**20
ANY = pl.BlockSpec(memory_space=pl.ANY)


def room_for(*buffers):
    need = sum(int(np.prod(shape)) * size * copies for shape, size, copies in buffers)
    room = min(60 * 2**20, need + need // 8 + 8 * 2**20)
    return pltpu.CompilerParams(vmem_limit_bytes=int(room))


class Plan:
    def __init__(self, dp, mp):
        self.dp, self.mp = dp, mp
        self.core = 2 if dp % 2 == 0 else 1
        self.y = 2 if dp % (2 * self.core) == 0 else 1
        self.z = dp // (self.core * self.y)
        self.n = dp * mp
        self.grid = np.arange(self.n).reshape(self.z, self.y, self.core, mp)
        self.place = [tuple(int(v) for v in np.argwhere(self.grid == i)[0]) for i in range(self.n)]

    def pairs(self, move):
        found = []
        for i, spot in enumerate(self.place):
            target = move(*spot)
            if target is not None and 0 <= target[0] < self.z:
                found.append((i, int(self.grid[target])))
        return found

    def flip_core(self):
        return self.pairs(lambda z, y, c, x: (z, y, 1 - c, x))

    def flip_first(self):
        return self.pairs(lambda z, y, c, x: (z, 1 - y, c, x) if c == 0 else (z, y, c, 1 - x))

    def flip_second(self):
        return self.pairs(lambda z, y, c, x: (z, y, c, 1 - x) if c == 0 else (z, 1 - y, c, x))

    def flip_z(self, bits):
        return self.pairs(lambda z, y, c, x: (z ^ bits, y, c, x))

    def z_moves(self):
        return [self.flip_z(bits) for bits in range(1, self.z)]

    def z_groups(self, split):
        return split if split and self.z == 4 else (tuple(range(self.z - 1)),)


def moved(table, pairs):
    got = np.full_like(table, -1)
    for source, target in pairs:
        got[target] = table[source]
    return got


def send(value, pairs):
    return lax.ppermute(value, AXES, pairs)


def add_all(parts, dtype=jnp.bfloat16):
    total = parts[0].astype(jnp.float32)
    for part in parts[1:]:
        total = total + part.astype(jnp.float32)
    return total.astype(dtype)


class Sum:
    def __init__(self, terms, count):
        self.terms, self.count = terms, count
        self.shape = terms[0][0].shape[1:]


def make_sums(sums):
    if not sums:
        return []
    arrays = [array for job in sums for array, _ in job.terms]
    parts = [job.count // 2 if job.count % 2 == 0 else job.count for job in sums]
    in_specs, out_specs = [], []
    for job, part in zip(sums, parts):
        moves = int(part < job.count)

        def spec(offset, part=part, moves=moves, shape=job.shape):
            return pl.BlockSpec(
                (part,) + shape, lambda i, at=offset // part: (at + moves * i, 0, 0)
            )

        in_specs = in_specs + [spec(offset) for _, offset in job.terms]
        out_specs.append(spec(0))

    def kernel(*refs):
        outs, first = refs[len(arrays) :], 0
        for job, part, out in zip(sums, parts, outs):
            mine = refs[first : first + len(job.terms)]
            first = first + len(job.terms)

            def add(mine=mine, out=out):
                out[...] = add_all([ref[...] for ref in mine])

            if part < job.count:
                add()
            else:
                pl.when(pl.program_id(0) == 0)(add)

    size = sum(job.count * np.prod(job.shape) * (len(job.terms) + 1) for job in sums)
    return pl.pallas_call(
        kernel,
        out_shape=[jax.ShapeDtypeStruct((job.count,) + job.shape, jnp.bfloat16) for job in sums],
        grid=(2,),
        in_specs=in_specs,
        out_specs=out_specs,
        compiler_params=pltpu.CompilerParams(vmem_limit_bytes=VMEM_LIMIT),
        cost_estimate=pl.CostEstimate(
            flops=int(size), bytes_accessed=int(2 * size), transcendentals=0
        ),
    )(*arrays)


class Travel:
    def __init__(self, name, steps, quiet=False):
        self.name, self.steps, self.quiet = name, steps, quiet
        self.result, self.going = None, None
        self.wanted = next(steps)


class Clock:
    def __init__(self, token):
        self.token = token

    def through(self, values):
        flat, tree = jax.tree.flatten(values)
        passed = lax.optimization_barrier(tuple(flat) + (self.token,))
        self.token = passed[-1]
        return jax.tree.unflatten(tree, passed[:-1])

    def start(self, travels, more=()):
        wanted = [[v for v, _ in travel.wanted] for travel in travels]
        made = list(make_sums([v for want in wanted for v in want if isinstance(v, Sum)]))
        wanted = [[made.pop(0) if isinstance(v, Sum) else v for v in want] for want in wanted]
        values, more = self.through((wanted, more))
        for travel, ready in zip(travels, values):
            with jax.named_scope(travel.name):
                travel.going = [send(v, pairs) for v, (_, pairs) in zip(ready, travel.wanted)]
        return more

    def wait(self, travels, more=()):
        loud = [travel for travel in travels if not travel.quiet]
        arrived, more = self.through(([travel.going for travel in loud], more))
        for travel, got in zip(loud, arrived):
            travel.going = got
        for travel in travels:
            got, travel.going = travel.going, None
            try:
                travel.wanted = travel.steps.send(got)
            except StopIteration as end:
                travel.wanted, travel.result = None, end.value
        return more


def path_table(plan):
    first, second, core = plan.flip_first(), plan.flip_second(), plan.flip_core()
    own = np.arange(plan.n)[:, None]
    line = np.concatenate([own] + [moved(own, pairs) for pairs in plan.z_moves()], 1)
    near, side = moved(line, first), moved(line, second)
    table = np.concatenate([line, near, side, moved(near, second)], 1)
    return np.concatenate([table, moved(table, core)], 1)


def gather_shards(plan, shard, split=()):
    first, second, core = plan.flip_first(), plan.flip_second(), plan.flip_core()
    moves, got = plan.z_moves(), {}
    for group in plan.z_groups(split):
        arrived = yield [(shard[None], moves[k]) for k in group]
        got.update(zip(group, arrived))
    line = jnp.concatenate([shard[None]] + [got[k] for k in range(len(moves))])
    near, side = yield [(line, first), (line, second)]
    far, line_twin, near_twin = yield [(near, second), (line, core), (near, core)]
    side_twin, far_twin = yield [(side, core), (far, core)]
    return [line, near, side, far, line_twin, near_twin, side_twin, far_twin]


def scatter_counts(plan):
    return [4 * plan.z, 3 * plan.z, plan.z]


def scatter_shards(plan, pieces, split=(), apart=False):
    first, second, core = plan.flip_first(), plan.flip_second(), plan.flip_core()
    own, rest_twin, far_twin = pieces
    size = plan.z
    far_got, rest_got = yield [(far_twin, core), (rest_twin, core)]
    (far_got,) = yield [(Sum([(own, 3 * size), (far_got, 0)], size), second)]
    near_sum = Sum([(own, size), (rest_got, size), (far_got, 0)], size)
    side_sum = Sum([(own, 2 * size), (rest_got, 2 * size)], size)
    if apart:
        (near_got,) = yield [(near_sum, first)]
        (side_got,) = yield [(side_sum, second)]
    else:
        near_got, side_got = yield [(near_sum, first), (side_sum, second)]
    terms = [own, rest_got, near_got, side_got]
    moves, arrived = plan.z_moves(), []
    for group in plan.z_groups(split):
        arrived += yield [(Sum([(term, k + 1) for term in terms], 1), moves[k]) for k in group]
    return add_all([term[:1] for term in terms] + arrived, jnp.float32)[0]


def total_steps(plan, value, halves=False):
    if halves:
        half = value.shape[0] // 2
        upper = lax.axis_index("dp") % 2 == 1
        keep = jnp.where(upper, value[half:], value[:half])
        (got,) = yield [(jnp.where(upper, value[:half], value[half:]), plan.flip_core())]
        value = keep + got
    else:
        (got,) = yield [(value, plan.flip_core())]
        value = value + got
    moves, bit = [], 1
    while bit < plan.z:
        moves.append(plan.flip_z(bit))
        bit *= 2
    moves.append(plan.pairs(lambda z, y, c, x: (z, y, c, 1 - x)))
    moves.append(plan.pairs(lambda z, y, c, x: (z, 1 - y, c, x)))
    for pairs in moves:
        (got,) = yield [(value, pairs)]
        value = value + got
    if halves:
        (got,) = yield [(value, plan.flip_core())]
        return jnp.where(upper, jnp.concatenate([got, value]), jnp.concatenate([value, got]))
    return value


def total_over_devices(plan, value, more=()):
    travel, clock = Travel("small_sum", total_steps(plan, value)), None
    while travel.wanted:
        with jax.named_scope(travel.name):
            got = [send(v, pairs) for v, pairs in travel.wanted]
        if clock is None:
            clock = Clock(got[0])
            more = clock.through(more)
            got = [clock.token]
        try:
            travel.wanted = travel.steps.send(got)
        except StopIteration as end:
            travel.wanted, travel.result = None, end.value
    return travel.result, more


def slot_counts(pieces):
    counts = [piece.shape[0] for piece in pieces]
    return counts, [sum(counts[:i]) for i in range(len(counts))]


def spot_of(device, plan, split_columns):
    if split_columns:
        return device // plan.mp, device % plan.mp
    return (device % plan.mp) * plan.dp + device // plan.mp, 0


def assemble(plan, pieces, slots, split_columns):
    counts, offsets = slot_counts(pieces)
    total = sum(counts)
    rows, width = pieces[0].shape[1:]
    groups = plan.mp if split_columns else 1
    blocks = total // groups
    if rows % 16 and groups > 1 or width % 128:
        stacked = jnp.concatenate(pieces)
        stacked = lax.fori_loop(
            0,
            total,
            lambda i, held: lax.dynamic_update_index_in_dim(held, stacked[i], slots[i], 0),
            stacked,
        ).reshape(plan.dp, plan.mp, rows, width)
        if split_columns:
            return stacked.transpose(0, 2, 1, 3).reshape(plan.dp * rows, plan.mp * width)
        return stacked.transpose(1, 0, 2, 3).reshape(total * rows, width)
    depth = 8

    def kernel(slots_ref, *refs):
        sources, out = refs[: len(pieces)], refs[len(pieces)]
        held, in_sems, out_sems = refs[len(pieces) + 1 :]
        steps = [(a, s) for a in range(len(pieces)) for s in range(counts[a])]
        reads, writes = [], []
        for i, (a, s) in enumerate(steps):
            block, group = spot_of(slots_ref[i], plan, split_columns)
            columns = pl.ds(pl.multiple_of(group * width, 128), width)
            reads.append(pltpu.make_async_copy(sources[a].at[s], held.at[i], in_sems.at[i]))
            writes.append(
                pltpu.make_async_copy(held.at[i], out.at[block, :, columns], out_sems.at[i])
            )
        for i in range(total):
            reads[i].start()
        for i in range(total):
            reads[i].wait()
            writes[i].start()
        for i in range(total):
            writes[i].wait()

    whole = pl.pallas_call(
        kernel,
        out_shape=jax.ShapeDtypeStruct((blocks, rows, groups * width), pieces[0].dtype),
        grid_spec=pltpu.PrefetchScalarGridSpec(
            num_scalar_prefetch=1,
            grid=(1,),
            in_specs=[ANY] * len(pieces),
            out_specs=ANY,
            scratch_shapes=[
                pltpu.VMEM((total, rows, width), pieces[0].dtype),
                pltpu.SemaphoreType.DMA((total,)),
                pltpu.SemaphoreType.DMA((total,)),
            ],
        ),
        compiler_params=pltpu.CompilerParams(vmem_limit_bytes=VMEM_LIMIT),
        cost_estimate=pl.CostEstimate(
            flops=0, bytes_accessed=4 * total * rows * width, transcendentals=0
        ),
    )(slots, *pieces)
    return whole.reshape(blocks * rows, groups * width)


def disassemble(plan, whole, shard_shape, counts, slots, split_columns):
    total = sum(counts)
    rows, width = shard_shape
    groups = plan.mp if split_columns else 1
    offsets = [sum(counts[:i]) for i in range(len(counts))]
    if rows % 16 and groups > 1 or width % 128:
        if split_columns:
            shards = whole.reshape(plan.dp, rows, plan.mp, width).transpose(0, 2, 1, 3)
        else:
            shards = whole.reshape(plan.mp, plan.dp, rows, width).transpose(1, 0, 2, 3)
        source = shards.reshape(total, rows, width)
        shards = lax.fori_loop(
            0,
            total,
            lambda i, held: lax.dynamic_update_index_in_dim(held, source[slots[i]], i, 0),
            source,
        )
        return [shards[o : o + c] for o, c in zip(offsets, counts)]
    blocks = total // groups

    def kernel(slots_ref, source, *refs):
        outs = refs[: len(counts)]
        held, in_sems, out_sems = refs[len(counts) :]
        steps = [(a, s) for a in range(len(counts)) for s in range(counts[a])]
        reads, writes = [], []
        for i, (a, s) in enumerate(steps):
            block, group = spot_of(slots_ref[i], plan, split_columns)
            columns = pl.ds(pl.multiple_of(group * width, 128), width)
            reads.append(
                pltpu.make_async_copy(source.at[block, :, columns], held.at[i], in_sems.at[i])
            )
            writes.append(pltpu.make_async_copy(held.at[i], outs[a].at[s], out_sems.at[i]))
        for i in range(total):
            reads[i].start()
        for i in range(total):
            reads[i].wait()
            writes[i].start()
        for i in range(total):
            writes[i].wait()

    return pl.pallas_call(
        kernel,
        out_shape=[jax.ShapeDtypeStruct((c, rows, width), whole.dtype) for c in counts],
        grid_spec=pltpu.PrefetchScalarGridSpec(
            num_scalar_prefetch=1,
            grid=(1,),
            in_specs=[ANY],
            out_specs=[ANY] * len(counts),
            scratch_shapes=[
                pltpu.VMEM((total, rows, width), whole.dtype),
                pltpu.SemaphoreType.DMA((total,)),
                pltpu.SemaphoreType.DMA((total,)),
            ],
        ),
        compiler_params=pltpu.CompilerParams(vmem_limit_bytes=VMEM_LIMIT),
        cost_estimate=pl.CostEstimate(
            flops=0, bytes_accessed=4 * total * rows * width, transcendentals=0
        ),
    )(slots, whole.reshape(blocks, rows, groups * width))


PAIR = 2 * HD


def pair_blocks(ref, offset, group, pair, pairs):
    start = group * 3 * pairs * PAIR + pair * PAIR
    span = pairs * PAIR
    return [ref[:, start + part * span : start + part * span + PAIR] for part in range(3)]


def both_heads(block):
    low_lane = lax.broadcasted_iota(jnp.int32, block.shape, 1) < HD
    zero = jnp.zeros_like(block)
    return jnp.concatenate([jnp.where(low_lane, block, zero), jnp.where(low_lane, zero, block)])


def own_columns(stacked):
    rows = stacked.shape[0] // 2
    low_lane = lax.broadcasted_iota(jnp.int32, (rows, PAIR), 1) < HD
    return jnp.where(low_lane, stacked[:rows], stacked[rows:])


def rows_by_rows(left, right):
    return lax.dot_general(left, right, (((1,), (1,)), ((), ())), preferred_element_type=jnp.float32)


def rows_of_both(left, right):
    return lax.dot_general(left, right, (((0,), (0,)), ((), ())), preferred_element_type=jnp.float32)


def pair_probs(stacked_queries, keys, allowed):
    scores = rows_by_rows(keys, stacked_queries) * HD ** (-0.5)
    scores = jnp.where(allowed, scores, masked_score)
    raised = jnp.exp(scores - jnp.max(scores, 0, keepdims=True))
    return raised * (1.0 / jnp.sum(raised, 0, keepdims=True))


def allowed_pairs(column_ref, row_ref):
    same = column_ref[0] == row_ref[0]
    shape = same.shape
    causal = lax.broadcasted_iota(jnp.int32, shape, 0) <= (
        lax.broadcasted_iota(jnp.int32, shape, 1) % LEN
    )
    return same & causal


def attend_kernel(groups, pairs, column_ref, row_ref, qkv_ref, context_ref):
    allowed = allowed_pairs(column_ref, row_ref)
    for group in range(groups):
        for pair in range(pairs):
            queries, keys, values = pair_blocks(qkv_ref, 0, group, pair, pairs)
            probs = pair_probs(both_heads(queries), keys, allowed).astype(jnp.bfloat16)
            context = own_columns(rows_of_both(probs, values))
            start = (group * pairs + pair) * PAIR
            context_ref[:, start : start + PAIR] = context.astype(jnp.bfloat16)


def attend_back_kernel(groups, pairs, column_ref, row_ref, qkv_ref, d_context_ref, d_qkv_ref):
    allowed = allowed_pairs(column_ref, row_ref)
    span = pairs * PAIR
    for group in range(groups):
        for pair in range(pairs):
            queries, keys, values = pair_blocks(qkv_ref, 0, group, pair, pairs)
            start = (group * pairs + pair) * PAIR
            d_context = both_heads(d_context_ref[:, start : start + PAIR])
            queries = both_heads(queries)
            probs = pair_probs(queries, keys, allowed)
            d_probs = rows_by_rows(values, d_context)
            d_values = matmul(probs.astype(jnp.bfloat16), d_context)
            weighted = probs * d_probs
            mean = jnp.sum(weighted, 0, keepdims=True)
            d_scores = (weighted - probs * mean).astype(jnp.bfloat16)
            d_queries = own_columns(rows_of_both(d_scores, keys)) * HD ** (-0.5)
            d_keys = matmul(d_scores, queries) * HD ** (-0.5)
            start = group * 3 * span + pair * PAIR
            for part, value in enumerate((d_queries, d_keys, d_values)):
                at = start + part * span
                d_qkv_ref[:, at : at + PAIR] = value.astype(jnp.bfloat16)


def attend_call(kernel, segments, qkv, others, out_columns, groups, scale):
    count = segments.shape[0]
    columns = qkv.shape[1]
    pairs = columns // (3 * groups * PAIR)
    rows = lambda wide: pl.BlockSpec((LEN, wide), lambda i: (i, 0))
    return pl.pallas_call(
        functools.partial(kernel, groups, pairs),
        out_shape=jax.ShapeDtypeStruct((qkv.shape[0], out_columns), jnp.bfloat16),
        grid=(count,),
        in_specs=[
            pl.BlockSpec((1, LEN, 1), lambda i: (i, 0, 0)),
            pl.BlockSpec((1, 1, 2 * LEN), lambda i: (i, 0, 0)),
            rows(columns),
        ]
        + [rows(other.shape[1]) for other in others],
        out_specs=rows(out_columns),
        compiler_params=pltpu.CompilerParams(vmem_limit_bytes=VMEM_LIMIT),
        cost_estimate=pl.CostEstimate(
            flops=scale * count * 2 * LEN * LEN * columns // 3,
            bytes_accessed=scale * qkv.size * 2,
            transcendentals=count * LEN * LEN * columns // (3 * HD),
        ),
    )(segments[:, :, None], jnp.tile(segments, (1, 2))[:, None, :], qkv, *others)


class Spread:
    def __init__(self, plan, parts, split_columns):
        self.plan, self.parts, self.split_columns = plan, parts, split_columns
        self.pieces = [piece for pieces, _ in parts for piece in pieces]
        self.slots = jnp.concatenate([slots for _, slots in parts])
        self.rows = self.pieces[0].shape[1]
        widths = [pieces[0].shape[2] for pieces, _ in parts]
        self.offsets = [sum(widths[:k]) for k in range(len(widths))]
        self.stride = sum(widths)
        groups = plan.mp if split_columns else 1
        self.shape = (plan.n // groups * self.rows, groups * self.stride)
        self.aligned = self.rows % 16 == 0 and all(width % 128 == 0 for width in widths)

    def matrix(self):
        groups = self.plan.mp if self.split_columns else 1
        wholes = [
            assemble(self.plan, pieces, slots, self.split_columns).reshape(
                self.shape[0], groups, -1
            )
            for pieces, slots in self.parts
        ]
        return jnp.concatenate(wholes, 2).reshape(self.shape)

    def places(self):
        found, first = [], 0
        for (pieces, _), offset in zip(self.parts, self.offsets):
            for k, piece in enumerate(pieces):
                found = found + [(first + k, slot, offset) for slot in range(piece.shape[0])]
            first = first + len(pieces)
        return found


def spot_slice(matrix_ref, plan, device, rows, width, split_columns, offset, stride):
    block, group = spot_of(device, plan, split_columns)
    at_rows = pl.ds(pl.multiple_of(block * rows, rows), rows)
    start = offset if isinstance(group, int) else pl.multiple_of(group * stride + offset, 128)
    return matrix_ref.at[at_rows, pl.ds(start, width)]


def with_matrices(plan, body, spreads, operands, outs, steps, flops):
    sizes = [len(spread.pieces) for spread in spreads]
    total = sum(spread.slots.shape[0] for spread in spreads)

    def kernel(slots_ref, *refs):
        inputs, refs = refs[: len(operands)], refs[len(operands) :]
        sources, refs = refs[: sum(sizes)], refs[sum(sizes) :]
        results, refs = refs[: len(outs)], refs[len(outs) :]
        kept, refs = refs[: len(spreads)], refs[len(spreads) :]
        matrices, sems, kept_sems = refs[: len(spreads)], refs[len(spreads)], refs[len(spreads) + 1]
        keeps = [
            pltpu.make_async_copy(matrix, out, kept_sems.at[k])
            for k, (matrix, out) in enumerate(zip(matrices, kept))
        ]

        @pl.when(pl.program_id(0) == 0)
        def _():
            copies, first = [], 0
            for spread, matrix in zip(spreads, matrices):
                for which, slot, offset in spread.places():
                    i = len(copies)
                    spot = spot_slice(
                        matrix,
                        plan,
                        slots_ref[i],
                        spread.rows,
                        spread.pieces[which].shape[2],
                        spread.split_columns,
                        offset,
                        spread.stride,
                    )
                    source = sources[first + which].at[slot]
                    copies.append(pltpu.make_async_copy(source, spot, sems.at[i]))
                    copies[-1].start()
                first = first + len(spread.pieces)
            for copy in copies:
                copy.wait()
            for keep in keeps:
                keep.start()

        body(inputs, matrices, results)

        @pl.when(pl.program_id(0) == pl.num_programs(0) - 1)
        def _():
            for keep in keeps:
                keep.wait()

    moved_bytes = sum(2 * spread.shape[0] * spread.shape[1] for spread in spreads)
    moved_bytes += sum(array.size * array.dtype.itemsize for array, _, _ in operands)
    moved_bytes += sum(np.prod(shape) * np.dtype(dtype).itemsize for shape, dtype, _, _ in outs)
    return pl.pallas_call(
        kernel,
        out_shape=[jax.ShapeDtypeStruct(shape, dtype) for shape, dtype, _, _ in outs]
        + [jax.ShapeDtypeStruct(spread.shape, jnp.bfloat16) for spread in spreads],
        grid_spec=pltpu.PrefetchScalarGridSpec(
            num_scalar_prefetch=1,
            grid=(steps,),
            in_specs=[pl.BlockSpec(block, index) for _, block, index in operands]
            + [ANY] * sum(sizes),
            out_specs=[pl.BlockSpec(block, index) for _, _, block, index in outs]
            + [ANY] * len(spreads),
            scratch_shapes=[pltpu.VMEM(spread.shape, jnp.bfloat16) for spread in spreads]
            + [
                pltpu.SemaphoreType.DMA((total,)),
                pltpu.SemaphoreType.DMA((len(spreads),)),
            ],
        ),
        compiler_params=pltpu.CompilerParams(vmem_limit_bytes=VMEM_LIMIT),
        cost_estimate=pl.CostEstimate(
            flops=flops, bytes_accessed=int(moved_bytes), transcendentals=0
        ),
    )(
        jnp.concatenate([spread.slots for spread in spreads]),
        *[array for array, _, _ in operands],
        *[piece for spread in spreads for piece in spread.pieces],
    )


def fixed(step, *scalars):
    return (0, 0)


def by_columns(step, *scalars):
    return (0, step)


def by_rows(step, *scalars):
    return (step, 0)


def step_slice(size):
    return pl.ds(pl.multiple_of(pl.program_id(0) * size, size), size)


def project(rows, spread, block):
    count, deep = rows.shape
    wide = spread.shape[1]
    if not spread.aligned or wide % block:
        whole = spread.matrix()
        return matmul(rows, whole).astype(jnp.bfloat16), whole

    def body(inputs, matrices, results):
        product = matmul(inputs[0][...], matrices[0][:, step_slice(block)])
        results[0][...] = product.astype(jnp.bfloat16)

    return with_matrices(
        spread.plan,
        body,
        [spread],
        [(rows, (count, deep), fixed)],
        [((count, wide), jnp.bfloat16, (count, block), by_columns)],
        wide // block,
        2 * count * deep * wide,
    )


def by_blocks(body, operands, outs, steps, flops):
    moved_bytes = sum(array.size * array.dtype.itemsize for array, _, _ in operands)
    moved_bytes += sum(np.prod(shape) * np.dtype(dtype).itemsize for shape, dtype, _, _ in outs)
    return pl.pallas_call(
        body,
        out_shape=[jax.ShapeDtypeStruct(shape, dtype) for shape, dtype, _, _ in outs],
        grid=(steps,),
        in_specs=[
            pl.BlockSpec(block, index, pipeline_mode=pl.Buffered(1 if index is fixed else 2))
            for _, block, index in operands
        ],
        out_specs=[pl.BlockSpec(block, index) for _, _, block, index in outs],
        compiler_params=pltpu.CompilerParams(vmem_limit_bytes=VMEM_LIMIT),
        cost_estimate=pl.CostEstimate(
            flops=flops, bytes_accessed=int(moved_bytes), transcendentals=0
        ),
    )(*[array for array, _, _ in operands])


def project_back(rows, matrix, block):
    count, deep = rows.shape
    wide = matrix.shape[0]
    if wide % block:
        return matmul_t(rows, matrix)

    def body(rows_ref, matrix_ref, out_ref):
        out_ref[...] = rows_by_rows(rows_ref[...], matrix_ref[...])

    return by_blocks(
        body,
        [(rows, (count, deep), fixed), (matrix, (block, deep), by_rows)],
        [((count, wide), jnp.float32, (count, block), by_columns)],
        wide // block,
        2 * count * deep * wide,
    )[0]


def gelu_and_slope(value):
    scale, cubic = (2.0 / np.pi) ** 0.5, 0.044715
    square = value * value
    bent = jnp.tanh(value * (scale + scale * cubic * square))
    half = 0.5 * bent + 0.5
    inner = value * (scale + 3.0 * scale * cubic * square)
    return value * half, half + (0.5 - 0.5 * bent * bent) * inner


def hidden_forward(rows, spread, block):
    count, deep = rows.shape
    wide = spread.shape[1]
    if not spread.aligned or wide % block:
        whole = spread.matrix()
        gelu, slope = gelu_and_slope(matmul(rows, whole))
        return gelu.astype(jnp.bfloat16), slope.astype(jnp.bfloat16), whole

    def body(inputs, matrices, results):
        up_pre = matmul(inputs[0][...], matrices[0][:, step_slice(block)])
        gelu, slope = gelu_and_slope(up_pre)
        results[0][...] = gelu.astype(jnp.bfloat16)
        results[1][...] = slope.astype(jnp.bfloat16)

    return with_matrices(
        spread.plan,
        body,
        [spread],
        [(rows, (count, deep), fixed)],
        [((count, wide), jnp.bfloat16, (count, block), by_columns)] * 2,
        wide // block,
        2 * count * deep * wide,
    )


def hidden_back(d_out, slope, matrix, block):
    count, wide = slope.shape
    if wide % block:
        d_activated = matmul_t(d_out, matrix)
        return (d_activated * slope.astype(jnp.float32)).astype(jnp.bfloat16)

    def body(d_out_ref, matrix_ref, slope_ref, out_ref):
        d_activated = rows_by_rows(d_out_ref[...], matrix_ref[...])
        out_ref[...] = (d_activated * slope_ref[...].astype(jnp.float32)).astype(jnp.bfloat16)

    return by_blocks(
        body,
        [
            (d_out, d_out.shape, fixed),
            (matrix, (block, d_out.shape[1]), by_rows),
            (slope, (count, block), by_columns),
        ],
        [((count, wide), jnp.bfloat16, (count, block), by_columns)],
        wide // block,
        2 * count * d_out.shape[1] * wide,
    )[0]


def heads_and_back(after, head, gain, shift, scales, targets):
    centred = after - jnp.mean(after, -1, keepdims=True)
    inverse = lax.rsqrt(jnp.mean(centred * centred, -1, keepdims=True) + norm_eps)
    unit = centred * inverse
    final = (unit * gain + shift).astype(jnp.bfloat16)
    logits = rows_by_rows(final, head)
    lane = lax.broadcasted_iota(jnp.int32, logits.shape, 1)
    edges = (0, RB, RB + AB, RB + AB + WB)
    inside = [(lane >= edges[k]) & (lane < edges[k + 1]) for k in range(3)]
    tops = [
        jnp.max(jnp.where(mask, logits, masked_score), -1, keepdims=True) for mask in inside
    ]

    def spread_over(columns, other):
        value = jnp.where(inside[2], columns[2], other)
        return jnp.where(inside[0], columns[0], jnp.where(inside[1], columns[1], value))

    lowered = spread_over([logits - top for top in tops], masked_score)
    raised = jnp.exp(lowered)
    totals = [jnp.sum(jnp.where(mask, raised, 0.0), -1, keepdims=True) for mask in inside]
    picked = [lane == targets[:, k : k + 1] for k in range(3)]
    loss = jnp.float32(0.0)
    for k in range(3):
        found = jnp.sum(jnp.where(picked[k], lowered, 0.0), -1, keepdims=True)
        loss = loss + jnp.sum(scales[:, k : k + 1] * (jnp.log(totals[k]) - found))
    hot = jnp.where(picked[0] | picked[1] | picked[2], 1.0, 0.0)
    shares = raised * spread_over([1.0 / total for total in totals], 0.0) - hot
    d_logits = (shares * spread_over([scales[:, k : k + 1] for k in range(3)], 0.0)).astype(
        jnp.bfloat16
    )
    d_unit = matmul(d_logits, head) * gain
    leaning = jnp.mean(d_unit * unit, -1, keepdims=True)
    d_after = inverse * (d_unit - jnp.mean(d_unit, -1, keepdims=True) - unit * leaning)
    return final, d_logits, loss, d_after


def context_back(d_up_pre, up, after, gain, d_later, exit_all, block):
    count, deep = d_up_pre.shape
    wide = up.shape[0]
    rows = (block, wide)

    def body(d_up_ref, up_ref, after_ref, gain_ref, later_ref, exit_ref, *outs):
        d_normed = rows_by_rows(d_up_ref[...], up_ref[...])
        outs[0][...] = d_normed
        after_rows = after_ref[...]
        centred = after_rows - jnp.mean(after_rows, -1, keepdims=True)
        inverse = lax.rsqrt(jnp.mean(centred * centred, -1, keepdims=True) + norm_eps)
        unit = centred * inverse
        d_unit = d_normed * gain_ref[...]
        leaning = jnp.mean(d_unit * unit, -1, keepdims=True)
        d_norm = inverse * (d_unit - jnp.mean(d_unit, -1, keepdims=True) - unit * leaning)
        d_out = (later_ref[...] + d_norm).astype(jnp.bfloat16)
        outs[1][...] = d_out
        outs[2][...] = rows_by_rows(d_out, exit_ref[...]).astype(jnp.bfloat16)

    return by_blocks(
        body,
        [
            (d_up_pre, (block, deep), by_rows),
            (up, up.shape, fixed),
            (after, rows, by_rows),
            (gain, gain.shape, fixed),
            (d_later, rows, by_rows),
            (exit_all, exit_all.shape, fixed),
        ],
        [
            ((count, wide), jnp.float32, rows, by_rows),
            ((count, wide), jnp.bfloat16, rows, by_rows),
            ((count, wide), jnp.bfloat16, rows, by_rows),
        ],
        count // block,
        2 * count * wide * (deep + wide),
    )


def hidden_out(activated, base, spread, head, gain, shift, scales, targets, block):
    count, deep = activated.shape
    wide = base.shape[1]
    lanes = head.shape[0]
    if not spread.aligned or count % block:
        whole = spread.matrix()
        after = base + matmul(activated, whole)
        final, d_logits, loss, d_after = heads_and_back(after, head, gain, shift, scales, targets)
        return after, final, d_logits, d_after, d_after.astype(jnp.bfloat16), loss[None], whole

    def body(inputs, matrices, results):
        after = inputs[1][...] + matmul(inputs[0][...], matrices[0][...])
        results[0][...] = after
        final, d_logits, loss, d_after = heads_and_back(
            after,
            inputs[2][...],
            inputs[3][...],
            inputs[4][...],
            inputs[5][...],
            inputs[6][...],
        )
        results[1][...] = final
        results[2][...] = d_logits
        results[3][...] = d_after
        results[4][...] = d_after.astype(jnp.bfloat16)
        results[5][...] = jnp.full(results[5].shape, loss)

    rows = (block, wide)
    return with_matrices(
        spread.plan,
        body,
        [spread],
        [
            (activated, (block, deep), by_rows),
            (base, rows, by_rows),
            (head, head.shape, fixed),
            (gain, gain.shape, fixed),
            (shift, shift.shape, fixed),
            (scales, (block, 3), by_rows),
            (targets, (block, 3), by_rows),
        ],
        [
            ((count, wide), jnp.float32, rows, by_rows),
            ((count, wide), jnp.bfloat16, rows, by_rows),
            ((count, lanes), jnp.bfloat16, (block, lanes), by_rows),
            ((count, wide), jnp.float32, rows, by_rows),
            ((count, wide), jnp.bfloat16, rows, by_rows),
            ((8 * (count // block), 128), jnp.float32, (8, 128), by_rows),
        ],
        count // block,
        2 * count * deep * wide,
    )


def weight_grad(plan, left, right, rows, parts, split_columns, block):
    tokens, high = left.shape
    wide = right.shape[1]
    groups = plan.mp if split_columns else 1
    stride = wide // groups
    along = wide if split_columns else high
    unit = stride if split_columns else rows
    widths = [width for width, _, _ in parts]
    offsets = [sum(widths[:k]) for k in range(len(parts))]
    fits = along % block == 0 and (block % unit == 0 or unit % block == 0)
    if rows % 16 or any(width % 128 for width in widths) or not fits:
        whole = contract(left, right).astype(jnp.bfloat16).reshape(high, groups, stride)
        found = []
        for (width, counts, slots), offset in zip(parts, offsets):
            part = whole[:, :, offset : offset + width].reshape(high, groups * width)
            found.append(disassemble(plan, part, (rows, width), counts, slots, split_columns))
        return found
    tile = 256 if split_columns else block
    outs_of = [(width, count) for width, counts, _ in parts for count in counts]
    places = [
        (width, offset, slot)
        for (width, counts, _), offset in zip(parts, offsets)
        for count in counts
        for slot in range(count)
    ]

    def kernel(slots_ref, left_ref, right_ref, *refs):
        outs, gradient, sems = refs[: len(outs_of)], refs[len(outs_of)], refs[len(outs_of) + 1]
        step = pl.program_id(0)
        for start in range(0, high if split_columns else block, tile):
            lefts = left_ref[:, start : start + tile]
            product = rows_of_both(lefts, right_ref[...]).astype(jnp.bfloat16)
            if split_columns:
                gradient[start : start + tile, step_slice(block)] = product
            else:
                gradient[step_slice(block), :] = product
        targets = [out.at[slot] for out, (_, count) in zip(outs, outs_of) for slot in range(count)]
        copies = []
        for i, (width, offset, _) in enumerate(places):
            spot = spot_slice(
                gradient, plan, slots_ref[i], rows, width, split_columns, offset, stride
            )
            copies.append(pltpu.make_async_copy(spot, targets[i], sems.at[i]))
        for i, (width, offset, _) in enumerate(places):
            row_block, group = spot_of(slots_ref[i], plan, split_columns)
            if split_columns:
                done_in = (group * stride + offset + width - 1) // block
            else:
                done_in = (row_block * rows) // block

            @pl.when(done_in == step)
            def _(copy=copies[i]):
                copy.start()

        @pl.when(step == pl.num_programs(0) - 1)
        def _():
            for copy in copies:
                copy.wait()

    if split_columns:
        left_spec = pl.BlockSpec((tokens, high), fixed)
        right_spec = pl.BlockSpec((tokens, block), by_columns)
    else:
        left_spec = pl.BlockSpec((tokens, block), by_columns)
        right_spec = pl.BlockSpec((tokens, wide), fixed)
    flat = pl.pallas_call(
        kernel,
        out_shape=[
            jax.ShapeDtypeStruct((count, rows, width), jnp.bfloat16) for width, count in outs_of
        ],
        grid_spec=pltpu.PrefetchScalarGridSpec(
            num_scalar_prefetch=1,
            grid=(along // block,),
            in_specs=[left_spec, right_spec],
            out_specs=[ANY] * len(outs_of),
            scratch_shapes=[
                pltpu.VMEM((high, wide), jnp.bfloat16),
                pltpu.SemaphoreType.DMA((len(places),)),
            ],
        ),
        compiler_params=pltpu.CompilerParams(vmem_limit_bytes=VMEM_LIMIT),
        cost_estimate=pl.CostEstimate(
            flops=2 * tokens * high * wide,
            bytes_accessed=2 * (tokens * (high + wide) + high * wide),
            transcendentals=0,
        ),
    )(jnp.concatenate([slots for _, _, slots in parts]), left, right)
    found = []
    for _, counts, _ in parts:
        found.append(flat[: len(counts)])
        flat = flat[len(counts) :]
    return found


def adam_step(first, root, clipped, corr_first, corr_second):
    first = beta_first * first + (1.0 - beta_first) * clipped
    second = beta_second * root * root + (1.0 - beta_second) * clipped * clipped
    direction = first / corr_first / (jnp.sqrt(second / corr_second) + adam_eps)
    return first, jnp.sqrt(second), direction


def views(matrix, columns):
    width = matrix.shape[-1]
    if len(matrix.shape) == 3:
        return [((k,), 0, width) for k in range(matrix.shape[0])]
    starts = [sum(columns[:k]) for k in range(len(columns))]
    return [((), start, size) for start, size in zip(starts, columns)]


LOSS, SQUARE, WEIGHTS, GRAD_NORM = 0, 1, 2, 5


def number_at(row, place):
    lane = lax.broadcasted_iota(jnp.int32, row.shape, 1)
    return jnp.sum(jnp.where(lane == place, row, 0.0), keepdims=True)


def row_of(numbers):
    lane = lax.broadcasted_iota(jnp.int32, (1, 128), 1)
    row = jnp.zeros((1, 128), jnp.float32)
    for place, number in numbers.items():
        row = jnp.where(lane == place, number, row)
    return row


def moments_and_directions(corrections, small, gradients, states, masters, norms):
    count = len(masters)
    flat = [part for parts in gradients for part in parts]
    smem = pl.BlockSpec(memory_space=pltpu.SMEM)
    vmem = pl.BlockSpec(memory_space=pltpu.VMEM)

    def kernel(corrections_ref, small_ref, *refs):
        parts, refs = list(refs[: len(flat)]), refs[len(flat) :]
        old, weights, refs = refs[:count], refs[count : 2 * count], refs[2 * count :]
        (norm_old, norm_weight), refs = refs[:2], refs[2:]
        fresh, ways, refs = refs[:count], refs[count : 2 * count], refs[2 * count :]
        norm_fresh, norm_out, row_ref = refs
        corr_first, corr_second = corrections_ref[0], corrections_ref[1]
        head_grad, norm_grad = parts[-1][...], small_ref[:6]
        square = number_at(small_ref[6:7], SQUARE)
        square = square + jnp.sum(head_grad * head_grad, keepdims=True)
        grad_norm = jnp.sqrt(square + jnp.sum(norm_grad * norm_grad, keepdims=True))
        clip = jnp.minimum(1.0, clip_limit / grad_norm)
        numbers = {GRAD_NORM: grad_norm}
        for k in range(count):
            mine = [parts.pop(0) for _ in gradients[k]]
            total = jnp.zeros((1, 1), jnp.float32)
            for which, (lead, start, width) in enumerate(
                views(masters[k], [part.shape[1] for part in gradients[k]])
            ):
                columns = slice(start, start + width)
                if lead:
                    gradient = mine[0][:, which * width : (which + 1) * width]
                else:
                    gradient = mine[which][...]
                spot = lead + (slice(None), columns)
                first, root, direction = adam_step(
                    old[k][(0,) + spot],
                    old[k][(1,) + spot],
                    clip * gradient,
                    corr_first,
                    corr_second,
                )
                if k < count - 1:
                    fresh[k][(0,) + spot] = first
                    fresh[k][(1,) + spot] = root
                else:
                    fresh[k][:, 0, :] = first
                    fresh[k][:, 1, :] = root
                direction = direction + weight_decay * weights[k][spot]
                ways[k][spot] = direction
                total = total + jnp.sum(direction * direction, keepdims=True)
            numbers[k] = total
        first, root, direction = adam_step(
            norm_old[0], norm_old[1], clip * norm_grad, corr_first, corr_second
        )
        norm_fresh[0] = first
        norm_fresh[1] = root
        norm_out[...] = norm_weight[...] - learn_rate * direction
        row_ref[...] = row_of(numbers)

    like = lambda value: jax.ShapeDtypeStruct(value.shape, jnp.float32)
    head_rows, wide = masters[-1].shape
    found = pl.pallas_call(
        kernel,
        out_shape=[like(state) for state in states[:-1]]
        + [jax.ShapeDtypeStruct((head_rows, 2, wide), jnp.float32)]
        + [like(master) for master in masters]
        + [like(norms[0]), like(norms[1]), jax.ShapeDtypeStruct((1, 128), jnp.float32)],
        in_specs=[smem] + [vmem] * (len(flat) + 2 * count + 3),
        out_specs=[vmem] * (2 * count + 3),
        compiler_params=pltpu.CompilerParams(vmem_limit_bytes=VMEM_LIMIT),
    )(corrections, small, *flat, *states, *masters, *norms)
    fresh = list(found[: count - 1]) + [found[count - 1].transpose(1, 0, 2)]
    return fresh, found[count : 2 * count], *found[2 * count :]


def new_weights(head_square, small, row, summed, masters, directions):
    count = len(masters)
    smem = pl.BlockSpec(memory_space=pltpu.SMEM)
    vmem = pl.BlockSpec(memory_space=pltpu.VMEM)

    def kernel(head_ref, small_ref, row_ref, summed_ref, *refs):
        weights, ways, refs = refs[:count], refs[count : 2 * count], refs[2 * count :]
        weight_norms, update_norms = {}, {}
        for k in range(count):
            if k < count - 1:
                weight_norms[k] = jnp.sqrt(number_at(small_ref[6:7], WEIGHTS + k))
                update_norms[k] = jnp.sqrt(number_at(summed_ref[...], k))
            else:
                weight_norms[k] = jnp.sqrt(jnp.full((1, 1), head_ref[0]))
                update_norms[k] = jnp.sqrt(number_at(row_ref[...], k))
            step = learn_rate * (weight_norms[k] / update_norms[k])
            value = weights[k][...] - step * ways[k][...]
            refs[k][...] = value
            if k < count - 1:
                refs[count + k][...] = value.astype(jnp.bfloat16)
        refs[-1][0:1] = row_of(weight_norms)
        refs[-1][1:2] = row_of(update_norms)

    found = pl.pallas_call(
        kernel,
        out_shape=[jax.ShapeDtypeStruct(master.shape, jnp.float32) for master in masters]
        + [jax.ShapeDtypeStruct(master.shape, jnp.bfloat16) for master in masters[:-1]]
        + [jax.ShapeDtypeStruct((2, 128), jnp.float32)],
        in_specs=[smem] + [vmem] * (3 + 2 * count),
        out_specs=[vmem] * (2 * count),
        compiler_params=pltpu.CompilerParams(vmem_limit_bytes=VMEM_LIMIT),
    )(head_square, small, row, summed, *masters, *directions)
    return found[:count], found[count:-1], found[-1]


BY_COLUMNS = ("entry", "up")
SPLITS = {"up": ((0, 1), (2,)), "down": ((0, 1), (2,))}


def per_device(
    plan,
    tokens,
    segment_ids,
    game_ids,
    return_bins,
    action_bins,
    reward_bins,
    valid_flags,
    step_count,
    entry_weight,
    entry_state,
    exit_weight,
    exit_state,
    up_weight,
    up_state,
    down_weight,
    down_state,
    head_weight,
    head_state,
    norm_params,
    norm_state,
):
    own_rows = tokens.shape[0]
    here = lax.axis_index("dp") * plan.mp + lax.axis_index("mp")
    row_start = lax.axis_index("mp") * own_rows
    own_seqs = own_rows // LEN
    segments = lax.dynamic_slice_in_dim(segment_ids, lax.axis_index("mp") * own_seqs, own_seqs)
    row_games = lax.dynamic_slice_in_dim(jnp.repeat(game_ids, LEN), row_start, own_rows)

    clock = Clock(step_count.astype(jnp.float32))
    masters = {"entry": entry_weight, "exit": exit_weight, "up": up_weight, "down": down_weight}
    rows_here, half_wide = entry_weight.shape[1:]
    halves = {name: value.astype(jnp.bfloat16) for name, value in masters.items()}
    entry_shard = halves["entry"].transpose(1, 0, 2).reshape(rows_here, 3 * half_wide)
    paths = {
        name: Travel("gather_" + name, gather_shards(plan, shard, split))
        for name, shard, split in (
            ("entry", entry_shard, ()),
            ("up", halves["up"], ((0, 1), (2,))),
            ("down", halves["down"], ((0, 1), (2,))),
        )
    }
    game_match = (row_games[:, None] == jnp.arange(GAMES)[None, :]).astype(jnp.float32)
    flag_float = valid_flags.astype(jnp.float32)
    local_counts = jnp.sum(game_match * jnp.sum(flag_float, -1, keepdims=True), 0)
    exit_rows, wide = exit_weight.shape
    tens = jnp.floor(local_counts / 64.0)
    pair = jnp.concatenate([tens, local_counts - 64.0 * tens]).astype(jnp.bfloat16)
    below = jnp.zeros((16 - exit_rows % 16, wide), jnp.bfloat16).at[0, : 2 * GAMES].set(pair)
    exit_shard = jnp.concatenate([halves["exit"], below])
    slots = jnp.asarray(path_table(plan), jnp.int32)[here]

    def chosen(names):
        return [paths[name] for name in names.split() if paths[name].wanted]

    def start(names, *more):
        return clock.start(chosen(names), more)

    def wait(names, *more):
        return clock.wait([path for path in chosen(names) if path.going], more)

    def finish(name):
        while paths[name].wanted:
            start(name)
            wait(name)
        return paths[name].result

    def whole(name):
        return Spread(plan, [(finish(name), slots)], name in BY_COLUMNS)


    resid, gains = start("entry", tokens.astype(jnp.float32), norm_params)
    normed_one = layer_norm(resid, gains[0], gains[3]).astype(jnp.bfloat16)
    (normed_one,) = wait("entry", normed_one)
    (exit_shard,) = start("entry up", exit_shard)
    gathered = lax.all_gather(exit_shard, ("mp", "dp"), axis=0)
    exit_all = gathered[:, :exit_rows].reshape(-1, wide)
    pairs_all = jnp.sum(gathered[:, exit_rows, : 2 * GAMES].astype(jnp.float32), 0)
    counts_all = 64.0 * pairs_all[:GAMES] + pairs_all[GAMES:]
    inverse = 1.0 / (GAMES * jnp.maximum(counts_all, 1.0))
    token_scale = jnp.sum(game_match * inverse[None, :], -1)
    wait("entry up")
    start("entry up")
    wait("entry up")
    start("entry up")
    wait("entry")
    (normed_one,) = start("down", normed_one)
    projected, entry_all = project(normed_one, whole("entry"), 768)
    (projected,) = wait("up down", projected)
    (projected,) = start("up down", projected)
    context = attend_call(
        attend_kernel, segments, projected, [], tokens.shape[1], plan.mp, 2
    )
    after_attn = resid + matmul(context, exit_all)
    normed_two = layer_norm(after_attn, norm_params[1], norm_params[4]).astype(jnp.bfloat16)
    after_attn, normed_two = wait("up down", after_attn, normed_two)
    (normed_two,) = start("up down", normed_two)
    wait("up")
    (normed_two,) = start("", normed_two)
    activated, slope, up_all = hidden_forward(normed_two, whole("up"), 512)
    activated, slope = wait("down", activated, slope)
    head_rows = head_weight.shape[0]
    head_half = jnp.pad(head_weight.astype(jnp.bfloat16), ((0, -head_rows % 128), (0, 0)))
    targets = jnp.stack([return_bins, action_bins + RB, reward_bins + (RB + AB)], 1)
    scales = flag_float * token_scale[:, None]
    late = start("down", *masters.values())
    weight_local = jnp.stack([jnp.sum(master * master) for master in late])
    weight_local, head_half, targets, scales = wait(
        "down", weight_local, head_half, targets, scales
    )
    start("down")
    wait("down")
    after_mlp, final_norm, d_logits, d_mlp_in, d_mlp_out, losses, down_all = hidden_out(
        activated,
        after_attn,
        whole("down"),
        head_half,
        norm_params[2:3],
        norm_params[5:6],
        scales,
        targets,
        160,
    )
    loss_local = jnp.sum(losses.reshape(-1, 8, 128)[:, 0, 0]) if losses.ndim > 1 else losses[0]

    def leave(names, left, right, rows, widths, block):
        by_columns = names.split()[0] in ("entry_a", "up")
        parts = [(width, scatter_counts(plan), slots) for width in widths]
        found = weight_grad(plan, left, right, rows, parts, by_columns, block)
        for name, pieces in zip(names.split(), found):
            steps = scatter_shards(plan, pieces, SPLITS.get(name, ()), name == "up")
            paths[name] = Travel("scatter_" + name, steps)

    down_rows = down_weight.shape[0]
    entry_widths = (3 * half_wide * 8 // 15, 3 * half_wide - 3 * half_wide * 8 // 15)
    leave("down", activated, d_mlp_out, down_rows, [wide], 1280)
    d_head = contract(d_logits, final_norm)[: head_rows + head_rows % 2]
    paths["head"] = Travel("sum_head", total_steps(plan, d_head, halves=True))
    (d_mlp_out,) = start("down head", d_mlp_out)
    d_up_pre = hidden_back(d_mlp_out, slope, down_all, 1024)
    (d_up_pre,) = wait("down head", d_up_pre)
    (d_up_pre,) = start("down head", d_up_pre)
    leave("up", normed_two, d_up_pre, rows_here, [up_weight.shape[1]], 2560)
    (d_up_pre,) = wait("down head", d_up_pre)
    (d_up_pre,) = start("down up head", d_up_pre)
    d_normed_two, d_attn_out, d_context = context_back(
        d_up_pre, up_all, after_attn, norm_params[1:2], d_mlp_in, exit_all, 320
    )
    leave("exit", context, d_attn_out, exit_rows, [wide], 1280)
    (d_context,) = wait("down up head", d_context)
    (d_context,) = start("down up exit", d_context)
    d_projected = attend_call(
        attend_back_kernel, segments, projected, [d_context], projected.shape[1], plan.mp, 5
    )
    (d_projected,) = wait("down up exit", d_projected)
    (d_projected,) = start("up down exit", d_projected)
    leave("entry_a entry_b", normed_one, d_projected, rows_here, entry_widths, 1920)
    (d_projected,) = wait("up down exit", d_projected)
    (d_projected,) = start("up entry_a entry_b", d_projected)
    d_normed_one = project_back(d_projected, entry_all, 256)
    reds = {"down": finish("down")}
    (d_normed_one,) = wait("up entry_a entry_b", d_normed_one)
    d_normed_one, reds = start("entry_a entry_b up head", d_normed_one, reds)
    down_square = jnp.sum(reds["down"] * reds["down"])
    _, d_gain_one, d_shift_one = norm_back(resid, norm_params[0], norm_params[3], d_normed_one)
    d_gain_one, d_shift_one, reds, down_square = wait(
        "entry_a entry_b up head", d_gain_one, d_shift_one, reds, down_square
    )
    late = start("entry_a up exit", after_mlp, d_logits, after_attn, d_normed_two)
    d_final = matmul(late[1], head_half)
    _, d_gain_three, d_shift_three = norm_back(late[0], norm_params[2], norm_params[5], d_final)
    _, d_gain_two, d_shift_two = norm_back(late[2], norm_params[1], norm_params[4], late[3])
    late = wait("entry_a up exit", d_gain_two, d_shift_two, d_gain_three, d_shift_three)
    d_gain_two, d_shift_two, d_gain_three, d_shift_three = late
    start("entry_b entry_a head")
    reds["up"] = finish("up")
    up_square = jnp.sum(reds["up"] * reds["up"])
    reds, up_square = wait("entry_b entry_a head", reds, up_square)
    start("entry_b exit head")
    reds["entry_a"] = finish("entry_a")
    entry_square = jnp.sum(reds["entry_a"] * reds["entry_a"])
    reds, entry_square = wait("entry_b exit head", reds, entry_square)
    reds["exit"] = finish("exit")
    exit_square = jnp.sum(reds["exit"] * reds["exit"])
    red_head = finish("head")[:head_rows]
    reds["entry_b"] = finish("entry_b")
    local_square = down_square + up_square + exit_square + entry_square
    local_square = local_square + jnp.sum(reds["entry_b"] * reds["entry_b"])
    masters = [entry_weight, exit_weight, up_weight, down_weight, head_weight]
    states = [entry_state, exit_state, up_state, down_state, head_state]
    wide = norm_params.shape[1]
    scalars = jnp.concatenate(
        [jnp.stack([loss_local, local_square]), weight_local, clock.token]
    )
    small, _ = total_over_devices(
        plan,
        jnp.stack(
            [
                d_gain_one,
                d_gain_two,
                d_gain_three,
                d_shift_one,
                d_shift_two,
                d_shift_three,
                jnp.pad(scalars, (0, wide - scalars.shape[0])),
            ]
        ),
    )
    step_float = step_count.astype(jnp.float32)
    corrections = jnp.concatenate(
        [1.0 - jnp.power(beta_first, step_float), 1.0 - jnp.power(beta_second, step_float)]
    )
    gradients = [
        [jnp.concatenate([reds["entry_a"], reds["entry_b"]], 1)],
        [reds["exit"]],
        [reds["up"]],
        [reds["down"]],
        [red_head],
    ]
    moments, directions, norm_moments, norm_new, row = moments_and_directions(
        corrections, small, gradients, states, masters, (norm_state, norm_params)
    )
    summed, late = total_over_devices(plan, row, (moments[4], norm_moments))
    moments[4], norm_moments = late
    new, rounded, norms = new_weights(
        jnp.sum(head_weight * head_weight)[None], small, row, summed, masters, directions
    )
    loss_sum, grad_norm, matrix_norms = small[6, LOSS], row[0, GRAD_NORM], norms[:, :5]
    return (
        new[0],
        moments[0],
        rounded[0],
        new[1],
        moments[1],
        rounded[1],
        new[2],
        moments[2],
        rounded[2],
        new[3],
        moments[3],
        rounded[3],
        new[4],
        moments[4],
        norm_new,
        norm_moments,
        loss_sum,
        grad_norm,
        matrix_norms,
    )


def solution(mesh):
    in_specs = (
        P(("dp", "mp"), None),
        P("dp", None),
        P("dp"),
        P(("dp", "mp")),
        P(("dp", "mp")),
        P(("dp", "mp")),
        P(("dp", "mp"), None),
        P(),
        P(None, "dp", "mp"),
        P(None, None, "dp", "mp"),
        P(("mp", "dp"), None),
        P(None, ("mp", "dp"), None),
        P("dp", "mp"),
        P(None, "dp", "mp"),
        P(("mp", "dp"), None),
        P(None, ("mp", "dp"), None),
        P(),
        P(),
        P(),
        P(),
    )
    out_specs = (
        P(None, "dp", "mp"),
        P(None, None, "dp", "mp"),
        P(None, "dp", "mp"),
        P(("mp", "dp"), None),
        P(None, ("mp", "dp"), None),
        P(("mp", "dp"), None),
        P("dp", "mp"),
        P(None, "dp", "mp"),
        P("dp", "mp"),
        P(("mp", "dp"), None),
        P(None, ("mp", "dp"), None),
        P(("mp", "dp"), None),
        P(),
        P(),
        P(),
        P(),
        P(),
        P(),
        P(),
    )
    plan = Plan(mesh.shape["dp"], mesh.shape["mp"])
    return jax.shard_map(
        functools.partial(per_device, plan), mesh=mesh, in_specs=in_specs, out_specs=out_specs, check_vma=False
    )
```
